32 devices in a mesh: ch: 4 (over y, core), seq: 8 (over z, x).
Axes of the slice: x: 2, y: 2, z: 4, core: 2. Of those that a mesh axis runs over, the one named last changes fastest.
Arguments:
- tokens: bfloat16 [2, 4, 1024, 768], P(None, 'ch', 'seq'), may hold values from -6 to 6
- cotangent: bfloat16 [2, 4, 1024, 768], P(None, 'ch', 'seq'), may hold values from -6 to 6
- first_gain: bfloat16 [768], P(('ch', 'seq')), may hold values from 0.5 to 1.5
- first_shift: bfloat16 [768], P(('ch', 'seq')), may hold values from -1.1953125 to 1.1953125
- mixer_weight: bfloat16 [768, 2304], P(('ch', 'seq')), may hold values from -0.21875 to 0.21875
- mixer_bias: bfloat16 [2304], P(('ch', 'seq')), may hold values from -1.1953125 to 1.1953125
- short_weight: bfloat16 [3, 2304], P(None, ('ch', 'seq')), may hold values from -0.59765625 to 0.59765625
- short_bias: bfloat16 [2304], P(('ch', 'seq')), may hold values from -1.1953125 to 1.1953125
- embed_weight: float32 [33, 64], replicated, may hold values from -12 to 12
- embed_bias: float32 [64], replicated, may hold values from -3 to 3
- first_sine: float32 [64], replicated, may hold values from 0.5 to 1.5
- inner_weight: float32 [64, 64], replicated, may hold values from -12 to 12
- inner_bias: float32 [64], replicated, may hold values from -3 to 3
- second_sine: float32 [64], replicated, may hold values from 0.5 to 1.5
- filter_weight: float32 [64, 768], replicated, may hold values from -0.09375 to 0.09375
- decay_rate: float32 [768], replicated, may hold values from 0.00048828125 to 0.03
- long_bias: float32 [768], replicated, may hold values from -4 to 4
- output_weight: bfloat16 [768, 768], P(('ch', 'seq')), may hold values from -0.21875 to 0.21875
- output_bias: bfloat16 [768], P(('ch', 'seq')), may hold values from -1.1953125 to 1.1953125
- second_gain: bfloat16 [768], P(('ch', 'seq')), may hold values from 0.5 to 1.5
- second_shift: bfloat16 [768], P(('ch', 'seq')), may hold values from -1.1953125 to 1.1953125
- expand_weight: bfloat16 [768, 3072], P(('ch', 'seq')), may hold values from -0.21875 to 0.21875
- expand_bias: bfloat16 [3072], P(('ch', 'seq')), may hold values from -1.1953125 to 1.1953125
- shrink_weight: bfloat16 [3072, 768], P(('ch', 'seq')), may hold values from -0.15625 to 0.15625
- shrink_bias: bfloat16 [768], P(('ch', 'seq')), may hold values from -1.1953125 to 1.1953125
Outputs:
- block_out: bfloat16 [2, 4, 1024, 768], P(None, 'ch', 'seq')
- tokens_gradient: bfloat16 [2, 4, 1024, 768], P(None, 'ch', 'seq')
- first_gain_gradient: float32 [768], P(('ch', 'seq'))
- first_shift_gradient: float32 [768], P(('ch', 'seq'))
- mixer_weight_gradient: float32 [768, 2304], P(('ch', 'seq'))
- mixer_bias_gradient: float32 [2304], P(('ch', 'seq'))
- short_weight_gradient: float32 [3, 2304], P(None, ('ch', 'seq'))
- short_bias_gradient: float32 [2304], P(('ch', 'seq'))
- embed_weight_gradient: float32 [33, 64], replicated
- embed_bias_gradient: float32 [64], replicated
- first_sine_gradient: float32 [64], replicated
- inner_weight_gradient: float32 [64, 64], replicated
- inner_bias_gradient: float32 [64], replicated
- second_sine_gradient: float32 [64], replicated
- filter_weight_gradient: float32 [64, 768], replicated
- long_bias_gradient: float32 [768], replicated
- output_weight_gradient: float32 [768, 768], P(('ch', 'seq'))
- output_bias_gradient: float32 [768], P(('ch', 'seq'))
- second_gain_gradient: float32 [768], P(('ch', 'seq'))
- second_shift_gradient: float32 [768], P(('ch', 'seq'))
- expand_weight_gradient: float32 [768, 3072], P(('ch', 'seq'))
- expand_bias_gradient: float32 [3072], P(('ch', 'seq'))
- shrink_weight_gradient: float32 [3072, 768], P(('ch', 'seq'))
- shrink_bias_gradient: float32 [768], P(('ch', 'seq'))
The draws below stay inside these ranges and needn't reach their ends.
All inputs are finite; a program needn't handle non-finite values.
Results may differ from the reference program's by a relative error of at most 0.013.
Values may be sent and summed in bfloat16 or wider, within the bound.
A program may use at most 320 MiB of HBM per device.

```python
import math
import jax
import jax.numpy as jnp
from jax import lax

D = 768
FF = 3072
FORDER = 64
EMB = 33
BLK = 128
MICRO = 2
SEQ_LEN = 1024
N_CH = 4
N_SEQ = 8


def levels(key, extent, split, low, high):
    level = 1.0
    for axis_at, blocks in split:
        steps = jax.random.uniform(jax.random.fold_in(jax.random.fold_in(key, 6), axis_at), (blocks,), jnp.float32, low / len(split), high / len(split))
        level = level * jnp.repeat(jnp.exp(steps), extent[axis_at] // blocks).reshape((-1,) + (1,) * (len(extent) - 1 - axis_at))
    return level


def centred(rng, shape, scale, reach, split=(), kind=jnp.bfloat16):
    values = scale * jax.random.normal(rng, shape, jnp.float32)
    if split:
        values = values * levels(rng, shape, split, -0.22, 0.18)
    return jnp.clip(values, -reach, reach).astype(kind)


def setup_inputs(seed: int = 0) -> dict:
    key_of = jax.random.split(jax.random.key(seed), 26)
    tokens = centred(key_of[0], (MICRO, N_CH, SEQ_LEN, D), 1.0, 6.0, ((1, 4), (2, 8)))
    cotangent = centred(key_of[1], (MICRO, N_CH, SEQ_LEN, D), 1.0, 6.0, ((1, 4), (2, 8)))
    first_gain = jnp.clip(1.0 + 0.1 * jax.random.normal(key_of[2], (D,), jnp.float32), 0.5, 1.5).astype(jnp.bfloat16)
    first_shift = centred(key_of[3], (D,), 0.2, 1.1953125, ((0, 32),))
    mixer_weight = centred(key_of[4], (D, 3 * D), D ** -0.5, 0.21875, ((0, 32),))
    mixer_bias = centred(key_of[5], (3 * D,), 0.2, 1.1953125, ((0, 32),))
    short_weight = jnp.clip(jax.random.uniform(key_of[6], (3, 3 * D), jnp.float32, -0.59765625, 0.59765625) * levels(key_of[6], (3, 3 * D), ((1, 32),), -0.4, 0.0), -0.59765625, 0.59765625).astype(jnp.bfloat16)
    short_bias = centred(key_of[7], (3 * D,), 0.2, 1.1953125, ((0, 32),))
    embed_weight = centred(key_of[8], (EMB, FORDER), 3.0, 12.0, (), jnp.float32)
    embed_bias = centred(key_of[9], (FORDER,), 1.0, 3.0, (), jnp.float32)
    first_sine = jnp.clip(jax.random.uniform(key_of[10], (FORDER,), jnp.float32, 0.5, 1.5), 0.5, 1.5)
    inner_weight = centred(key_of[11], (FORDER, FORDER), 3.0, 12.0, (), jnp.float32)
    inner_bias = centred(key_of[12], (FORDER,), 1.0, 3.0, (), jnp.float32)
    second_sine = jnp.clip(jax.random.uniform(key_of[13], (FORDER,), jnp.float32, 0.5, 1.5), 0.5, 1.5)
    filter_weight = centred(key_of[14], (FORDER, D), (64 * FORDER) ** -0.5, 0.09375, (), jnp.float32)
    decay_rate = jnp.clip(jnp.exp(jax.random.uniform(key_of[15], (D,), jnp.float32, math.log(0.00048828125), math.log(0.03))), 0.00048828125, 0.03)
    long_bias = centred(key_of[16], (D,), 1.0, 4.0, (), jnp.float32)
    output_weight = centred(key_of[17], (D, D), D ** -0.5, 0.21875, ((0, 32),))
    output_bias = centred(key_of[18], (D,), 0.2, 1.1953125, ((0, 32),))
    second_gain = jnp.clip(1.0 + 0.1 * jax.random.normal(key_of[19], (D,), jnp.float32), 0.5, 1.5).astype(jnp.bfloat16)
    second_shift = centred(key_of[20], (D,), 0.2, 1.1953125, ((0, 32),))
    expand_weight = centred(key_of[21], (D, FF), D ** -0.5, 0.21875, ((0, 32),))
    expand_bias = centred(key_of[22], (FF,), 0.2, 1.1953125, ((0, 32),))
    shrink_weight = centred(key_of[23], (FF, D), (FF // 2) ** -0.5, 0.15625, ((0, 32),))
    shrink_bias = centred(key_of[24], (D,), 0.2, 1.1953125, ((0, 32),))
    return dict(tokens=tokens, cotangent=cotangent, first_gain=first_gain, first_shift=first_shift, mixer_weight=mixer_weight, mixer_bias=mixer_bias, short_weight=short_weight, short_bias=short_bias, embed_weight=embed_weight, embed_bias=embed_bias, first_sine=first_sine, inner_weight=inner_weight, inner_bias=inner_bias, second_sine=second_sine, filter_weight=filter_weight, decay_rate=decay_rate, long_bias=long_bias, output_weight=output_weight, output_bias=output_bias, second_gain=second_gain, second_shift=second_shift, expand_weight=expand_weight, expand_bias=expand_bias, shrink_weight=shrink_weight, shrink_bias=shrink_bias)


@jax.custom_vjp
def low(v):
    return lax.optimization_barrier(v.astype(jnp.bfloat16)).astype(jnp.float32)

@jax.custom_vjp
def low_back(v):
    return v

def low_keep(v):
    return (low(v), None)

def low_pass(kept, grad):
    return (grad,)

def back_keep(v):
    return (v, None)

def back_low(kept, grad):
    return (low(grad),)
low.defvjp(low_keep, low_pass)
low_back.defvjp(back_keep, back_low)
highest = lax.Precision.HIGHEST

def matmul(left, right):
    return jnp.dot(left, right, precision=highest, preferred_element_type=jnp.float32)

def layer_norm(values, gain, shift):
    centre = values - lax.optimization_barrier(jnp.mean(values, axis=-1, keepdims=True))
    spread = lax.optimization_barrier(jnp.mean(centre * centre, axis=-1, keepdims=True))
    return centre * lax.rsqrt(spread + 1e-05) * gain + shift

def filter_values(seq_length, embed_matrix, embed_offset, sine_first, inner_matrix, inner_offset, sine_second, head_matrix, rates):
    positions = jnp.arange(seq_length).astype(jnp.float32)
    band_count = (embed_matrix.shape[0] - 1) // 2
    frequency = jnp.linspace(0.0001, band_count - 1, band_count).astype(jnp.float32)
    angles = 2.0 * jnp.pi / seq_length * positions[:, None] * frequency[None, :]
    encoded = jnp.concatenate([positions[:, None] / (seq_length - 1), jnp.cos(angles), -jnp.sin(angles)], axis=1)
    layer_first = jnp.sin(sine_first * (matmul(encoded, embed_matrix) + embed_offset))
    layer_second = jnp.sin(sine_second * (matmul(layer_first, inner_matrix) + inner_offset))
    return matmul(layer_second, head_matrix) * jnp.exp(-rates[None, :] * positions[:, None])

def causal_conv(gated_input, impulse):
    seq_length = gated_input.shape[0]
    product = jnp.fft.rfft(gated_input, n=2 * seq_length, axis=0) * jnp.fft.rfft(impulse, n=2 * seq_length, axis=0)
    return jnp.fft.irfft(product, n=2 * seq_length, axis=0)[:seq_length]

def hyena_block(params, impulse, inputs):
    gain_one, shift_one, mix_matrix, mix_offset, short_taps, short_offset, skip_gain, out_matrix, out_offset, gain_two, shift_two, expand_matrix, expand_offset, shrink_matrix, shrink_offset = params
    width = inputs.shape[1]
    normed_one = low(layer_norm(inputs, gain_one, shift_one))
    mixed = low(low_back(matmul(normed_one, mix_matrix) + mix_offset))
    padded = jnp.pad(mixed, ((2, 0), (0, 0)))
    short_out = short_taps[0] * padded[:-2] + short_taps[1] * padded[1:-1] + short_taps[2] * padded[2:] + short_offset
    gate_out = short_out[:, :width]
    gate_in = short_out[:, width:2 * width]
    values = short_out[:, 2 * width:]
    gated_input = low(low_back(gate_in * values))
    long_out = causal_conv(gated_input, impulse) + skip_gain * gated_input
    long_low = low(low_back(long_out))
    gated_out = low(gate_out * long_low)
    middle = inputs + low_back(matmul(gated_out, out_matrix) + out_offset)
    normed_two = low(layer_norm(middle, gain_two, shift_two))
    hidden_pre = low_back(matmul(normed_two, expand_matrix) + expand_offset)
    hidden = low(jax.nn.gelu(hidden_pre, approximate=False))
    return middle + matmul(hidden, shrink_matrix) + shrink_offset

def reference(tokens, cotangent, first_gain, first_shift, mixer_weight, mixer_bias, short_weight, short_bias, embed_weight, embed_bias, first_sine, inner_weight, inner_bias, second_sine, filter_weight, decay_rate, long_bias, output_weight, output_bias, second_gain, second_shift, expand_weight, expand_bias, shrink_weight, shrink_bias):
    seq_length = BLK * N_SEQ
    params = tuple((item.astype(jnp.float32) for item in (first_gain, first_shift, mixer_weight, mixer_bias, short_weight, short_bias, long_bias, output_weight, output_bias, second_gain, second_shift, expand_weight, expand_bias, shrink_weight, shrink_bias)))

    def make_filter(embed_matrix, embed_offset, sine_first, inner_matrix, inner_offset, sine_second, head_matrix):
        return filter_values(seq_length, embed_matrix, embed_offset, sine_first, inner_matrix, inner_offset, sine_second, head_matrix, decay_rate)
    impulse, filter_back = jax.vjp(make_filter, embed_weight, embed_bias, first_sine, inner_weight, inner_bias, second_sine, filter_weight)
    seq_inputs = tokens.astype(jnp.float32).reshape(MICRO * N_CH, seq_length, D)
    seq_cots = cotangent.astype(jnp.float32).reshape(MICRO * N_CH, seq_length, D)

    def one_sequence(carry, item):
        grads, impulse_grad = carry
        inputs, cots = item
        result, back = jax.vjp(hyena_block, params, impulse, inputs)
        param_grads, filter_part, input_grad = back(cots)
        grads = jax.tree.map(lambda left, right: left + right, grads, param_grads)
        return ((grads, impulse_grad + filter_part), (result.astype(jnp.bfloat16), input_grad.astype(jnp.bfloat16)))
    zeros = jax.tree.map(jnp.zeros_like, params)
    (grads, impulse_grad), (outputs, input_grads) = lax.scan(one_sequence, (zeros, jnp.zeros_like(impulse)), (seq_inputs, seq_cots))
    filter_grads = filter_back(impulse_grad)
    shape = (MICRO, N_CH, seq_length, D)
    return (outputs.reshape(shape), input_grads.reshape(shape), grads[0], grads[1], grads[2], grads[3], grads[4], grads[5], filter_grads[0], filter_grads[1], filter_grads[2], filter_grads[3], filter_grads[4], filter_grads[5], filter_grads[6], grads[6], grads[7], grads[8], grads[9], grads[10], grads[11], grads[12], grads[13], grads[14])
```

```python
import functools
import types

import jax
import jax.numpy as jnp
import numpy as np
from jax import lax
from jax.experimental import pallas as pl
from jax.experimental.pallas import tpu as pltpu
from jax.sharding import PartitionSpec as P


MESH = pl.DeviceIdType.MESH
f32 = jnp.float32
bf16 = jnp.bfloat16
LANES = 128
PIECES = ("mix", "out", "exp", "shr")


def dot_nn(left, right, precision=None):
    return lax.dot_general(
        left, right, (((1,), (0,)), ((), ())), precision=precision, preferred_element_type=f32
    )


def dot_nt(left, right, precision=None):
    return lax.dot_general(
        left, right, (((1,), (1,)), ((), ())), precision=precision, preferred_element_type=f32
    )


def dot_tn(left, right, precision=None):
    return lax.dot_general(
        left, right, (((0,), (0,)), ((), ())), precision=precision, preferred_element_type=f32
    )


def normalise(values):
    centre = values - jnp.mean(values, axis=-1, keepdims=True)
    scale = lax.rsqrt(jnp.mean(centre * centre, axis=-1, keepdims=True) + 1e-05)
    return centre * scale, scale


def norm_back(unit, scale, grad):
    inner = grad - jnp.mean(grad, axis=-1, keepdims=True)
    return scale * (inner - unit * jnp.mean(grad * unit, axis=-1, keepdims=True))


def sin_cos(angle):
    turns = jnp.floor(angle * (1.0 / np.pi) + 0.5)
    rest = angle - turns * 3.140625
    rest = rest - turns * 9.670257568359375e-4
    rest = rest - turns * 6.2771141529083251953e-7
    rest = rest - turns * 1.21644916362129151821e-10
    sign = 1.0 - 2.0 * (turns - 2.0 * jnp.floor(turns * 0.5))
    sq = rest * rest
    low = sq * (1.0 / 362880.0 - sq * (1.0 / 39916800.0 - sq * (1.0 / 6227020800.0)))
    sine = rest * (1.0 - sq * (1.0 / 6.0 - sq * (1.0 / 120.0 - sq * (1.0 / 5040.0 - low))))
    high = sq * (1.0 / 3628800.0 - sq * (1.0 / 479001600.0 - sq * (1.0 / 87178291200.0)))
    cosine = 1.0 - sq * (0.5 - sq * (1.0 / 24.0 - sq * (1.0 / 720.0 - sq * (1.0 / 40320.0 - high))))
    return sign * sine, sign * cosine


def split_three(value):
    top = value.astype(bf16)
    rest = value - top.astype(f32)
    mid = rest.astype(bf16)
    low = (rest - mid.astype(f32)).astype(bf16)
    return top, mid, low


class Sizes:
    def __init__(self, chans, seqs, block, width, hidden):
        self.chans, self.seqs, self.block = chans, seqs, block
        self.width, self.hidden = width, hidden
        self.devices = chans * seqs
        self.y_n, self.z_n, self.x_n = chans // 2, seqs // 2, 2
        self.chips = self.devices // 2
        self.own = width // self.devices
        self.pair = 2 * self.own
        self.unit = hidden // self.devices
        self.cw = width // 2
        self.mw = 3 * self.cw
        self.hw = hidden // 2
        self.slab = 4 * self.own
        self.length = block * seqs
        self.tap = 3 * self.own
        self.blocks = {
            "mix": (self.pair, self.mw),
            "out": (self.pair, self.cw),
            "exp": (self.pair, self.hw),
            "shr": (self.unit, self.width),
        }
        third = self.cw // 3
        self.gathers = {
            "m": ("mix", 0, 5 * third, 4 * third),
            "o": ("out", 0, third, 2 * third),
            "e": ("exp", 0, self.hw // 2, self.hw // 2),
            "s": ("shr", 0, 2 * third, 3 * third),
            "t": ("shr", 5 * third, third),
        }
        self.sums = {
            "s": ("shr", 0, 2 * third, 3 * third),
            "t": ("shr", 5 * third, third),
            "e": ("exp", 0, self.hw // 2, self.hw // 2),
            "o": ("out", 0, third, 2 * third),
            "m0": ("mix", 0, 2 * third, third),
            "m1": ("mix", self.cw, 2 * third, third),
            "m2": ("mix", 2 * self.cw, third, 2 * third),
        }


def tables(n):
    out = np.full((16, n.hw), -1, np.int32)
    p = np.arange(n.width)
    out[0, : n.width], out[1, : n.width] = p % n.own, p // n.own
    col = np.arange(n.mw)
    group, k = col // n.cw, col % n.cw
    chip, r = k // n.own, k % n.own
    for core in range(2):
        dev = (2 * (chip // n.seqs) + core) * n.seqs + chip % n.seqs
        e = group * n.width + n.own * dev + r
        out[2 + 2 * core, : n.mw], out[3 + 2 * core, : n.mw] = e % n.tap, e // n.tap
    col = np.arange(n.hw)
    chip, r = col // n.unit, col % n.unit
    out[6], out[7] = r, 2 * (chip // n.seqs) * n.seqs + chip % n.seqs
    chip, rest = p // n.pair, p % n.pair
    dev = (2 * (chip // n.seqs) + rest // n.own) * n.seqs + chip % n.seqs
    out[8, : n.width] = n.own * dev + rest % n.own
    return out


def encoding_table(length, bands, rows):
    positions = np.arange(length).astype(np.float32)
    frequency = np.linspace(0.0001, bands - 1, bands).astype(np.float32)
    angles = np.float32(2.0 * np.pi / length) * positions[:, None] * frequency[None, :]
    out = np.zeros((rows, length), np.float32)
    out[0] = positions / np.float32(length - 1)
    out[1 : 1 + bands] = np.cos(angles.astype(np.float64)).T
    out[1 + bands : 1 + 2 * bands] = -np.sin(angles.astype(np.float64)).T
    return out


INPUTS = (
    "tok", "cot", "i_gain1", "i_shift1", "i_mix", "i_mixb", "i_sw", "i_sb", "embw", "i_be", "i_fs", "inw", "i_bi",
    "i_ss", "i_filt", "i_rate", "i_skip", "i_out", "i_outb", "i_gain2", "i_shift2", "i_exp", "i_expb", "wshr",
    "i_shrb", "tabs", "enc",
)
OUTPUTS = ("bo", "tg", "gmix", "gexp", "gout", "gshr", "gsm", "fg", "gnet")
VECTORS = (
    "i_gain1", "i_shift1", "i_outb", "i_gain2", "i_shift2", "i_shrb", "i_mixb", None, None, None, "i_sb", "i_expb",
)


def scratch_list(n):
    v = pltpu.VMEM
    sem = pltpu.SemaphoreType.DMA
    rows = 4 * n.block
    half = 2 * n.block
    halo = 64
    slabs = (n.chips, n.slab, LANES)
    flat = (n.chips * n.slab, LANES)
    items = [
        ("xs", v((2, n.block, n.width), bf16)),
        ("gs", v((2, n.block, n.width), bf16)),
        ("ho", v((2, 16, n.width), bf16)),
        ("hs", v((2, 16, n.width), bf16)),
        ("pall", v((n.devices, 16, LANES), bf16)),
        ("pallf", v((n.devices * 16, LANES), f32)),
        ("wpre", v((n.pair, n.mw + n.hw), f32)),
        ("wrecv", v((n.own, n.mw + n.hw), f32)),
        ("pvf", v((16, LANES), f32)),
        ("pvec", v((16, LANES), bf16)),
        ("fvr", v((8, LANES), f32)),
        ("fvec", v((LANES, 8), f32)),
        ("fsel", v((n.own, LANES), f32)),
        ("pv", v((16, n.hw), f32)),
        ("r24", v((LANES, n.width), bf16)),
        ("r72", v((LANES, n.mw), bf16)),
        ("r96", v((LANES, n.hw), bf16)),
        ("d24", v((n.devices, n.width), f32)),
        ("d72", v((n.devices, n.mw), f32)),
        ("d96", v((n.devices, n.hw), f32)),
        ("perm", v((n.width, n.width), bf16)),
        ("n1p", v((rows + halo, n.width), bf16)),
        ("mixed", v((rows + halo, n.mw), bf16)),
        ("so", v((rows, n.mw), f32)),
        ("of", v(flat, f32)),
        ("gm", v(flat, f32)),
        ("uf", v(flat, f32)),
        ("gf", v(flat, f32)),
        ("toep", v((n.own, n.block, n.length), bf16)),
        ("u1", v((64, n.length), f32)),
        ("u2", v((64, n.length), f32)),
        ("l1", v((64, n.length), f32)),
        ("l2", v((LANES, n.length), f32)),
        ("c1", v((64, n.length), f32)),
        ("c2", v((64, n.length), f32)),
        ("imp", v((n.own, n.length), f32)),
        ("ig", v((n.own, n.length), f32)),
        ("w2o", v((n.cw, n.width), bf16)),
        ("low", v((rows, n.cw), bf16)),
        ("gated", v((rows, n.cw), bf16)),
        ("middle", v((rows, n.width), f32)),
        ("n2p", v((rows, n.width), bf16)),
        ("hid", v((rows, n.hw), bf16)),
        ("pre", v((rows, n.hw), bf16)),
        ("peo_s", v((rows, n.width), bf16)),
        ("peo_r", v((rows, n.width), bf16)),
        ("peb_s", v((half, n.width), bf16)),
        ("peb_r", v((half, n.width), bf16)),
        ("ped_r", v((rows, n.width), bf16)),
        ("pef_r", v((half, n.width), bf16)),
        ("acc", v((rows, n.width), f32)),
        ("branch", v((rows, n.width), bf16)),
        ("sg", v((rows, n.mw), f32)),
        ("nb_s", v((8, n.mw), f32)),
        ("nb_r", v((8, n.mw), f32)),
        ("mg", v((rows, n.mw), bf16)),
        ("msgs", v((n.devices * 16, LANES), f32)),
        ("rall", v((n.devices * 16, LANES), f32)),
        ("smf", v((16, LANES), f32)),
        ("fall", v((n.devices * 8, LANES), f32)),
        ("gv", v((16, n.hw), f32)),
    ]
    for k in range(4):
        items.append((f"sb{k}", v(slabs, bf16)))
        items.append((f"rb{k}", v(slabs, bf16)))
    for p in PIECES:
        r, c = n.blocks[p]
        items.append((f"w_{p}", v((n.chips, r, c), bf16)))
        if p != "exp":
            items.append((f"g_{p}", v((n.chips, r, c), bf16)))
        items.append((f"b_{p}", v((n.chips // 2, r, c), bf16)))
        items.append((f"a_{p}", v((n.chips // 4, r, c), bf16)))
        items.append((f"z_{p}", v((n.z_n - 1, r, c), bf16)))
    items += [
        ("ag_s", sem((2 * len(n.gathers),))),
        ("ag_r", sem((2 * len(n.gathers) * n.chips,))),
        ("rs_s", sem((6 * len(n.sums),))),
        ("rs_r", sem((6 * len(n.sums),))),
        ("ex_s", sem((28,))),
        ("ex_r", sem((28,))),
    ]
    return items


def fused_kernel(n, names, *refs):
    S = types.SimpleNamespace(**dict(zip(names, refs)))
    rows, half, blk = 4 * n.block, 2 * n.block, n.block
    S.tok_, S.cot_ = S.tok.at[:, 0], S.cot.at[:, 0]
    ch, seq = lax.axis_index("ch"), lax.axis_index("seq")
    y, core = lax.div(ch, 2), lax.rem(ch, 2)
    z, x = lax.div(seq, n.x_n), lax.rem(seq, n.x_n)
    me_dev = ch * n.seqs + seq
    other_ch = ch + 1 - 2 * core

    def chip(yy, zz, xx):
        return yy * n.seqs + zz * n.x_n + xx

    def slot(yy, zz, xx):
        return (zz * n.x_n + xx) * n.y_n + yy

    def at(yy, zz, xx):
        return (yy * 2 + core, zz * n.x_n + xx)

    me_chip, me_slot = chip(y, z, x), slot(y, z, x)
    sib = (other_ch, seq)

    def z_peer(j):
        peer = z
        bit = 1
        while bit <= j:
            if j & bit:
                peer = peer + bit * (1 - 2 * lax.rem(lax.div(z, bit), 2))
            bit *= 2
        return peer

    ends = []

    def send(src, dst, send_sem, recv_sem, target):
        pltpu.make_async_remote_copy(
            src_ref=src, dst_ref=dst, send_sem=send_sem, recv_sem=recv_sem,
            device_id=target, device_id_type=MESH,
        ).start()

    def wait(ref, sem):
        pltpu.make_async_copy(ref, ref, sem).wait()

    def later(ref, sem):
        ends.append((ref, sem))

    exchange_count = [0]

    def exchange(src, dst, target, free=False):
        k = exchange_count[0]
        exchange_count[0] += 1
        send(src, dst, S.ex_s.at[k], S.ex_r.at[k], target)
        if free:
            return lambda: wait(dst, S.ex_r.at[k]), lambda: wait(src, S.ex_s.at[k])
        later(src, S.ex_s.at[k])
        return lambda: wait(dst, S.ex_r.at[k])

    def to_others(src, dst, total):
        k = exchange_count[0]
        exchange_count[0] += 1
        for dc in range(n.chans):
            for ds in range(n.seqs):
                if dc or ds:
                    cc, ss = lax.rem(ch + dc, n.chans), lax.rem(seq + ds, n.seqs)
                    send(src(cc * n.seqs + ss), dst, S.ex_s.at[k], S.ex_r.at[k], (cc, ss))
        later(total, S.ex_s.at[k])
        return lambda: wait(total, S.ex_r.at[k])

    def to_chips(src, dst, total):
        k = exchange_count[0]
        exchange_count[0] += 1
        for dy in range(n.y_n):
            for dz in range(n.z_n):
                for dx in range(n.x_n):
                    if dy or dz or dx:
                        yy, zz, xx = lax.rem(y + dy, n.y_n), lax.rem(z + dz, n.z_n), lax.rem(x + dx, n.x_n)
                        send(src(yy, zz, xx), dst, S.ex_s.at[k], S.ex_r.at[k], at(yy, zz, xx))
        later(total, S.ex_s.at[k])
        return lambda: wait(total, S.ex_r.at[k])

    barrier = pltpu.get_barrier_semaphore()
    for dc in range(n.chans):
        for ds in range(n.seqs):
            if dc or ds:
                pl.semaphore_signal(
                    barrier, inc=1,
                    device_id=(lax.rem(ch + dc, n.chans), lax.rem(seq + ds, n.seqs)),
                    device_id_type=MESH,
                )
    theirs = pl.ds(pl.multiple_of((1 - core) * n.own, 8), n.own)
    ours = pl.ds(pl.multiple_of(core * n.own, 8), n.own)
    rows_mix, rows_exp = S.i_mix[...].astype(f32), S.i_exp[...].astype(f32)
    span, wide_span = n.cw // 2, n.hw // 2
    for k in range(2):
        to = slice(k * n.own, (k + 1) * n.own)
        for g in range(3):
            for yy in range(2):
                lo, src = g * n.cw + yy * span, g * n.width + (2 * yy + k) * span
                S.wpre[to, lo : lo + span] = rows_mix[:, src : src + span]
        for yy in range(2):
            lo, src = n.mw + yy * wide_span, (2 * yy + k) * wide_span
            S.wpre[to, lo : lo + wide_span] = rows_exp[:, src : src + wide_span]
    S.pvf[...] = jnp.zeros_like(S.pvf)
    for i, name in enumerate(VECTORS):
        if name:
            ref = getattr(S, name)
            size = ref.shape[0]
            S.pvf[i : i + 1, :size] = ref[...].astype(f32).reshape(1, size)
    S.pvf[7:10, : n.tap] = S.i_sw[...].astype(f32)
    S.pvec[...] = S.pvf[...].astype(bf16)
    S.w_shr[me_chip] = S.wshr[...]
    out_rows = S.i_out[...].astype(f32)
    S.w_out[me_chip] = jnp.concatenate([out_rows[:, : n.cw], out_rows[:, n.cw :]], axis=0).astype(bf16)

    def chosen(row, width):
        return S.tabs[row : row + 1, :width]

    def pick(row0, row1, width):
        return jnp.where(core == 0, chosen(row0, width), chosen(row1, width))

    def one_hot(height, index):
        return lax.broadcasted_iota(jnp.int32, (height, index.shape[1]), 0) == index

    S.r24[...] = one_hot(LANES, chosen(0, n.width)).astype(f32).astype(bf16)
    S.d24[...] = one_hot(n.devices, chosen(1, n.width)).astype(f32)
    S.r72[...] = one_hot(LANES, pick(2, 4, n.mw)).astype(f32).astype(bf16)
    S.d72[...] = one_hot(n.devices, pick(3, 5, n.mw)).astype(f32)

    pl.semaphore_wait(barrier, n.devices - 1)


    wait_pre, sent_pre = exchange(S.wpre.at[theirs], S.wrecv, sib, free=True)
    wait_xs = exchange(S.tok_, S.xs, sib)
    after = lax.rem(seq + 1, n.seqs)
    wait_ho = exchange(S.tok_.at[:, blk - 16 : blk, :], S.ho, (ch, after))
    wait_hs = exchange(S.tok_.at[:, blk - 16 : blk, :], S.hs, (other_ch, after))
    wait_params = to_others(
        lambda d: S.pvec, S.pall.at[me_dev], S.pall.at[pl.ds(0, n.devices - 1)]
    )
    wait_gs = exchange(S.cot_, S.gs, sib)
    S.pall[me_dev] = S.pvec[...]

    def flip(axis):
        return (1 - y, z, x) if axis == "y" else (y, z, 1 - x)

    far = (1 - y, z, 1 - x)

    class Line:
        def __init__(self, p, h):
            weight, start, *widths = n.gathers[p]
            self.buf = getattr(S, f"w_{weight}")
            self.cols = pl.ds(start + h * widths[0], widths[h])
            self.base = list(n.gathers).index(p) * 2 + h
            first, second = ("x", "y") if h == 0 else ("y", "x")
            self.first_dev, self.second_dev = at(*flip(first)), at(*flip(second))
            self.lead, self.side = flip(first), flip(second)

        def part(self, index):
            return self.buf.at[index, :, self.cols]

        def recv(self, k):
            return S.ag_r.at[self.base * n.chips + k]

        def push(self, index, k, target):
            send(self.part(index), self.part(index), S.ag_s.at[self.base], self.recv(k), target)

        def start_z(self):
            for j in range(1, n.z_n):
                self.push(me_chip, j, at(y, z_peer(j), x))

        def start_xy(self):
            self.push(me_chip, n.z_n, self.first_dev)
            self.push(me_chip, 2 * n.z_n, self.second_dev)

        def along(self, j):
            index = chip(y, z_peer(j), x)
            wait(self.part(index), self.recv(j))
            self.push(index, n.z_n + j, self.first_dev)
            self.push(index, 2 * n.z_n + j, self.second_dev)

        def across(self, j):
            index = chip(self.lead[0], z_peer(j), self.lead[2])
            wait(self.part(index), self.recv(n.z_n + j))
            self.push(index, 3 * n.z_n + j, self.second_dev)

        def finish(self):
            for j in range(n.z_n):
                wait(self.part(chip(self.side[0], z_peer(j), self.side[2])), self.recv(2 * n.z_n + j))
            for j in range(n.z_n):
                wait(self.part(chip(far[0], z_peer(j), far[2])), self.recv(3 * n.z_n + j))

        def sent(self):
            wait(self.buf.at[pl.ds(0, n.chips - 1), :, self.cols], S.ag_s.at[self.base])

    class Plane:
        def __init__(self, p):
            weight, start, width = n.gathers[p]
            self.buf = getattr(S, f"w_{weight}")
            self.cols = pl.ds(start, width)
            self.base = list(n.gathers).index(p) * 2
            self.x_dev, self.y_dev = at(*flip("x")), at(*flip("y"))
            self.x_chip, self.y_chip, self.far_chip = chip(*flip("x")), chip(*flip("y")), chip(*far)

        def part(self, index):
            return self.buf.at[index, :, self.cols]

        def recv(self, k):
            return S.ag_r.at[self.base * n.chips + k]

        def push(self, index, k, target):
            send(self.part(index), self.part(index), S.ag_s.at[self.base], self.recv(k), target)

        def start_xy(self):
            self.push(me_chip, 0, self.x_dev)
            self.push(me_chip, 1, self.y_dev)

        def corner(self):
            wait(self.part(self.x_chip), self.recv(0))
            self.push(self.x_chip, 2, self.y_dev)
            wait(self.part(self.y_chip), self.recv(1))

        def start_z(self):
            for j in range(1, n.z_n):
                self.push(me_chip, 3 + j, at(y, z_peer(j), x))
                self.push(self.x_chip, 2 + n.z_n + j, at(y, z_peer(j), x))
                self.push(self.y_chip, 1 + 2 * n.z_n + j, at(y, z_peer(j), x))

        def corner_z(self):
            wait(self.part(self.far_chip), self.recv(2))
            for j in range(1, n.z_n):
                self.push(self.far_chip, 3 * n.z_n + j, at(y, z_peer(j), x))

        def finish(self):
            for q, (yy, xx) in enumerate(((y, x), (y, 1 - x), (1 - y, x), (1 - y, 1 - x))):
                for j in range(1, n.z_n):
                    wait(self.part(chip(yy, z_peer(j), xx)), self.recv(3 - q + q * n.z_n + j))

        def sent(self):
            wait(self.part(pl.ds(0, n.chips - 1)), S.ag_s.at[self.base])

    gathers = {p: [Plane(p)] if p == "t" else [Line(p, 0), Line(p, 1)] for p in n.gathers}

    def gather(p, step, *args):
        for g in gathers[p]:
            getattr(g, step)(*args)

    gather("t", "start_xy")

    wait_pre()
    own_half, sib_half = S.wpre[ours, :], S.wrecv[...]
    slab = jnp.concatenate(
        [jnp.where(core == 0, own_half, sib_half), jnp.where(core == 0, sib_half, own_half)], axis=0
    ).astype(bf16)
    S.w_mix[me_chip] = slab[:, : n.mw]
    gather("m", "start_z")
    gather("m", "start_xy")
    S.w_exp[me_chip] = slab[:, n.mw :]

    todo = []

    def plan(p, step, *args):
        todo.extend(functools.partial(getattr(g, step), *args) for g in gathers[p])

    for p, then in (("m", "o"), ("o", "e"), ("e", "s"), ("s", None)):
        for j in range(1, n.z_n):
            plan(p, "along", j)
        if then:
            plan(then, "start_z")
        if p == "m":
            plan("t", "corner")
        if p == "e":
            plan("t", "start_z")
            plan("t", "corner_z")
        for j in range(n.z_n):
            plan(p, "across", j)
        if then:
            plan(then, "start_xy")
        if p == "m":
            mixer_steps = len(todo)
    plan_length = len(todo)

    def pump(count):
        for _ in range(min(count, len(todo))):
            todo.pop(0)()

    pump(2)
    S.perm[...] = one_hot(n.width, chosen(8, n.width)).astype(f32).astype(bf16)
    pump(2)
    wait_params()
    S.pallf[...] = S.pall[...].astype(f32).reshape(n.devices * 16, LANES)
    groups = [(range(0, 6), S.r24, S.d24), (range(6, 11), S.r72, S.d72), (range(11, 12), S.r96, S.d96)]

    def vectors_from_shards(members, right, mask):
        width = right.shape[1]
        for i in members:
            left = S.pallf[pl.ds(i, n.devices, stride=16), :].astype(bf16)
            S.pv[i : i + 1, :width] = jnp.sum(dot_nn(left, right[...]) * mask[...], axis=0, keepdims=True)

    vectors_from_shards(*groups[0])
    pump(2)

    def vector(i, lo=0, size=None):
        return S.pv[i : i + 1, lo : lo + (n.width if size is None else size)]

    hi = lax.Precision.HIGHEST

    def filter_setup():
        for i, ref in enumerate((S.i_be, S.i_fs, S.i_bi, S.i_ss)):
            S.fvr[i : i + 1, 0:64] = ref[...].reshape(1, 64)
        S.fvec[...] = jnp.transpose(S.fvr[...])
        last = [ref[...].reshape(1, n.width) for ref in (S.i_rate, S.i_skip)]
        last = jnp.concatenate(last + [jnp.zeros((6, n.width), f32)], axis=0)
        table = jnp.concatenate([S.i_filt[...], last], axis=0)
        first = lax.broadcasted_iota(jnp.int32, (n.own, n.width), 0) + me_dev * n.own
        mine = lax.broadcasted_iota(jnp.int32, (n.own, n.width), 1) == first
        S.fsel[:, : 72] = dot_nt(jnp.where(mine, 1.0, 0.0), table, hi)

    def filter_first():
        u = dot_tn(S.embw[...], S.enc[0 : S.embw.shape[0]], hi) + S.fvec[0:64, 0:1]
        S.u1[...] = u
        s, c = sin_cos(u * S.fvec[0:64, 1:2])
        S.l1[...] = s
        S.c1[...] = c

    def filter_second():
        u = dot_tn(S.inw[...], S.l1[...], hi) + S.fvec[0:64, 2:3]
        S.u2[...] = u
        s, c = sin_cos(u * S.fvec[0:64, 3:4])
        S.l2[0:64] = s
        row = lax.broadcasted_iota(jnp.int32, (LANES - 64, n.length), 0)
        col = lax.broadcasted_iota(jnp.int32, (LANES - 64, n.length), 1)
        S.l2[64:LANES] = jnp.where((row == 0) & (col == 0), 1.0, 0.0)
        S.c2[...] = c

    def decay():
        time = lax.broadcasted_iota(jnp.int32, (n.own, n.length), 1).astype(f32)
        return jnp.exp(-S.fsel[:, 64:65] * time)

    def filter_third():
        S.imp[...] = dot_nn(S.fsel[:, 0:64], S.l2[0:64], hi) * decay()

    def toeplitz(r):
        line = S.imp[pl.ds(r, 1), :]
        line = jnp.concatenate([jnp.zeros((1, LANES), f32), line], axis=1)
        wide = jnp.broadcast_to(line, (blk, LANES + n.length))
        S.toep[r] = pltpu.roll(wide, 0, 1, stride=1, stride_axis=0)[:, LANES:].astype(bf16)

    def norm_rows(values, gain, shift):
        unit, _ = normalise(values.astype(f32))
        low = (unit * vector(gain) + vector(shift)).astype(bf16)
        return dot_nn(low, S.perm[...]).astype(bf16)

    S.n1p[0:half] = norm_rows(S.tok_[...].reshape(half, n.width), 0, 1)
    pump(2)
    wait_xs()
    S.n1p[half:rows] = norm_rows(S.xs[...].reshape(half, n.width), 0, 1)
    pump(2)
    wait_ho()
    wait_hs()
    S.n1p[rows : rows + 32] = norm_rows(S.ho[...].reshape(32, n.width), 0, 1)
    S.n1p[rows + 32 : rows + 64] = norm_rows(S.hs[...].reshape(32, n.width), 0, 1)
    pump(4)

    pump(mixer_steps - (plan_length - len(todo)))
    vectors_from_shards(*groups[1])
    gather("m", "finish")
    pump(10)

    for g in range(3):
        lo = g * n.cw
        weight = S.w_mix[:, :, lo : lo + n.cw].reshape(n.width, n.cw)
        for r0, r1 in ((0, half), (half, rows + 64)):
            S.mixed[r0:r1, lo : lo + n.cw] = (
                dot_nn(S.n1p[r0:r1], weight) + vector(6, lo, n.cw)
            ).astype(bf16)
    first_block = seq == 0
    last_block = seq == n.seqs - 1

    def shifted(s, lo):
        own = S.mixed[s * blk : (s + 1) * blk, lo : lo + n.cw].astype(f32)
        before = S.mixed[rows + 16 * s : rows + 16 * (s + 1), lo : lo + n.cw].astype(f32)
        before = jnp.where(first_block, jnp.zeros_like(before), before)
        both = jnp.concatenate([before, own], axis=0)
        return own, pltpu.roll(both, 1, 0)[16:], pltpu.roll(both, 2, 0)[16:]

    for s in range(4):
        for g in range(3):
            lo = g * n.cw
            now, one, two = shifted(s, lo)
            S.so[s * blk : (s + 1) * blk, lo : lo + n.cw] = (
                vector(7, lo, n.cw) * two + vector(8, lo, n.cw) * one
                + vector(9, lo, n.cw) * now + vector(10, lo, n.cw)
            )

    def token_rows(s):
        return slice(s * blk, (s + 1) * blk)

    def gate(s, g):
        return S.so[token_rows(s), g * n.cw : (g + 1) * n.cw]

    def to_channels(k, make):
        out, into = getattr(S, f"sb{k}"), getattr(S, f"rb{k}")
        for s in range(4):
            turned = jnp.transpose(make(s))
            for m in range(n.chips):
                row = m * n.slab + s * n.own
                S.of[row : row + n.own, :] = turned[m * n.own : (m + 1) * n.own]
        out[...] = S.of[...].astype(bf16).reshape(n.chips, n.slab, LANES)
        arrived = to_chips(
            lambda yy, zz, xx: out.at[chip(yy, zz, xx)], into.at[me_slot], into.at[pl.ds(0, n.chips - 1)]
        )
        into[me_slot] = out[me_chip]
        return arrived

    def to_tokens(k):
        out, into = getattr(S, f"sb{k}"), getattr(S, f"rb{k}")
        out[...] = S.of[...].astype(bf16).reshape(n.chips, n.slab, LANES)
        arrived = to_chips(
            lambda yy, zz, xx: out.at[slot(yy, zz, xx)], into.at[me_chip], into.at[pl.ds(0, n.chips - 1)]
        )
        into[me_chip] = out[me_slot]
        return arrived

    def token_view(k, s):
        got = getattr(S, f"rb{k}")[...].astype(f32)
        return jnp.transpose(got[:, s * n.own : (s + 1) * n.own, :].reshape(n.cw, LANES))

    wait_u = to_channels(0, lambda s: gate(s, 1) * gate(s, 2))
    third = n.own // 3
    pump(10)
    filter_setup()
    filter_first()
    filter_second()
    filter_third()
    S.r96[...] = one_hot(LANES, chosen(6, n.hw)).astype(f32).astype(bf16)
    S.d96[...] = one_hot(n.devices, chosen(7, n.hw) + core * n.seqs).astype(f32)
    vectors_from_shards(*groups[2])
    for q in range(3):
        lax.fori_loop(q * third, (q + 1) * third, lambda r, carry: (toeplitz(r), carry)[1], 0)
    pump(10)
    wait_u()

    group = n.y_n * 4
    lines = n.seqs * group
    S.uf[...] = S.rb0[...].astype(f32).reshape(n.chips * n.slab, LANES)

    def channel_rows(ref, r):
        return ref[pl.ds(r, lines, stride=n.own), :]

    def conv_forward(r, carry):
        own = channel_rows(S.uf, r)
        wide = dot_nn(own.astype(bf16), S.toep[r])
        blocks = []
        for i in range(n.seqs):
            total = wide[group * i : group * (i + 1), 0:LANES]
            for k in range(1, i + 1):
                total = total + wide[group * (i - k) : group * (i - k + 1), LANES * k : LANES * (k + 1)]
            blocks.append(total)
        result = jnp.concatenate(blocks, axis=0) + S.fsel[pl.ds(r, 1), 65:66] * own
        S.of[pl.ds(r, lines, stride=n.own), :] = result
        return carry

    for q in range(3):
        lax.fori_loop(q * third, (q + 1) * third, conv_forward, 0)
        pump(3)
    wait_low = to_tokens(1)
    pump(100)
    gather("o", "finish")
    slabs = S.w_out[...].astype(f32)
    S.w2o[:, : n.cw] = slabs[:, : n.own, :].reshape(n.cw, n.cw).astype(bf16)
    S.w2o[:, n.cw :] = slabs[:, n.own :, :].reshape(n.cw, n.cw).astype(bf16)
    wait_low()

    for s in range(4):
        low = token_view(1, s)
        S.low[token_rows(s)] = low.astype(bf16)
        S.gated[token_rows(s)] = (gate(s, 0) * low).astype(bf16)
    waits = []
    for part in (1, 0):
        r = slice(part * half, (part + 1) * half)
        o = slice((1 - part) * half, (2 - part) * half)
        S.acc[r] = dot_nn(S.gated[r], S.w2o[...])
        S.peo_s[r] = S.acc[r].astype(bf16)
        waits.append(exchange(S.peo_s.at[r], S.peo_r.at[o], sib, free=True))
    wait_gs()

    def tokens_of(part):
        return (S.tok_ if part == 0 else S.xs)[...].reshape(half, n.width).astype(f32)

    def cot_of(part):
        return (S.cot_ if part == 0 else S.gs)[...].reshape(half, n.width)

    for arrived, sent in waits:
        arrived()
        sent()
    for part in range(2):
        r = slice(part * half, (part + 1) * half)
        S.middle[r] = tokens_of(part) + (S.acc[r] + S.peo_r[r].astype(f32)) + vector(2)
        S.n2p[r] = norm_rows(S.middle[r], 3, 4)

    for p in "est":
        gather(p, "finish")
    chunk = n.hw // 4
    units = chunk // n.unit
    for q in range(4):
        lo = q * chunk
        weight = S.w_exp[:, :, lo : lo + chunk].reshape(n.width, chunk)
        shrink = S.w_shr[q * units : (q + 1) * units].reshape(chunk, n.width)
        total = jnp.zeros((1, chunk), f32)
        for part in range(2):
            r = slice(part * half, (part + 1) * half)
            v = dot_nn(S.n2p[r], weight) + vector(11, lo, chunk)
            back = dot_nt(cot_of(part), shrink)
            phi = 0.5 + 0.5 * lax.erf(v * np.float32(1.0 / np.sqrt(2.0)))
            slope = phi + v * (np.float32(1.0 / np.sqrt(2.0 * np.pi)) * jnp.exp(-0.5 * v * v))
            S.hid[r, lo : lo + chunk] = (v * phi).astype(bf16)
            pre = (back * slope).astype(bf16)
            S.pre[r, lo : lo + chunk] = pre
            total = total + jnp.sum(pre.astype(f32), axis=0, keepdims=True)
        S.gv[11:12, lo : lo + chunk] = total
    waits = []
    for part in (1, 0):
        r = slice(part * half, (part + 1) * half)
        o = slice((1 - part) * half, (2 - part) * half)
        S.acc[r] = dot_nt(S.pre[r], S.w_exp[...].reshape(n.width, n.hw))
        S.peo_s[r] = S.acc[r].astype(bf16)
        waits.append(exchange(S.peo_s.at[r], S.ped_r.at[o], sib))

    def gradient(weight):
        return S.w_exp if weight == "exp" else getattr(S, f"g_{weight}")

    def add_into(ref, index, cols, *terms):
        total = ref[index, :, cols].astype(f32)
        for term in terms:
            total = total + term.astype(f32)
        ref[index, :, cols] = total.astype(bf16)

    def scatter_line(p, h):
        weight, start, *widths = n.sums[p]
        grads, cols = gradient(weight), pl.ds(start + h * widths[0], widths[h])
        from_b, from_a, from_z = (getattr(S, f"{k}_{weight}") for k in "baz")
        base = list(n.sums).index(p) * 6 + h * 3
        second, first = ("y", "x") if h == 0 else ("x", "y")
        second_dev, first_dev = at(*flip(second)), at(*flip(first))

        def side(i, other):
            if second == "y":
                return (1 - y if other else y) * n.seqs + i
            return chip(lax.div(i, n.z_n), lax.rem(i, n.z_n), 1 - x if other else x)

        def near(zz, other):
            if first == "x":
                return chip(y, zz, 1 - x if other else x)
            return chip(1 - y if other else y, zz, x)

        def start_b():
            for i in range(n.chips // 2):
                send(grads.at[side(i, True), :, cols], from_b.at[i, :, cols], S.rs_s.at[base], S.rs_r.at[base], second_dev)
            later(from_b.at[:, :, cols], S.rs_s.at[base])

        def end_b():
            wait(from_b.at[:, :, cols], S.rs_r.at[base])

            def add(i, carry):
                add_into(grads, side(i, False), cols, from_b[i, :, cols])
                return carry

            lax.fori_loop(0, n.chips // 2, add, 0)
            for zz in range(n.z_n):
                send(grads.at[near(zz, True), :, cols], from_a.at[zz, :, cols], S.rs_s.at[base + 1], S.rs_r.at[base + 1], first_dev)
            later(from_a.at[:, :, cols], S.rs_s.at[base + 1])

        def end_a():
            wait(from_a.at[:, :, cols], S.rs_r.at[base + 1])

            def add(zz, carry):
                add_into(grads, near(zz, False), cols, from_a[zz, :, cols])
                return carry

            lax.fori_loop(0, n.z_n, add, 0)
            for j in range(1, n.z_n):
                send(
                    grads.at[chip(y, z_peer(j), x), :, cols], from_z.at[j - 1, :, cols],
                    S.rs_s.at[base + 2], S.rs_r.at[base + 2], at(y, z_peer(j), x),
                )
            later(from_z.at[:, :, cols], S.rs_s.at[base + 2])

        def end_z():
            wait(from_z.at[:, :, cols], S.rs_r.at[base + 2])
            total = grads[me_chip, :, cols].astype(f32)
            for j in range(n.z_n - 1):
                total = total + from_z[j, :, cols].astype(f32)
            return total

        return start_b, end_b, end_a, end_z

    def scatter_plane(p):
        weight, start, width = n.sums[p]
        grads, full = gradient(weight), pl.ds(start, width)
        eight, four, three = (getattr(S, f"{k}_{weight}") for k in "baz")
        base = list(n.sums).index(p) * 6
        plane = ((y, x), (y, 1 - x), (1 - y, x), (1 - y, 1 - x))
        x_dev, y_dev = at(*flip("x")), at(*flip("y"))
        x_chip, y_chip, far_chip = chip(*flip("x")), chip(*flip("y")), chip(*far)

        def landing(q, j):
            k = q * (n.z_n - 1) + j - 1
            many = n.chips // 2
            return (eight, k, 0) if k < many else (four, k - many, 1)

        def start_z():
            for q, (yy, xx) in enumerate(plane):
                for j in range(1, n.z_n):
                    ref, k, which = landing(q, j)
                    send(
                        grads.at[chip(yy, z_peer(j), xx), :, full], ref.at[k, :, full],
                        S.rs_s.at[base + which], S.rs_r.at[base + which], at(y, z_peer(j), x),
                    )
            later(eight.at[:, :, full], S.rs_s.at[base])
            later(four.at[:, :, full], S.rs_s.at[base + 1])

        def end_z():
            wait(eight.at[:, :, full], S.rs_r.at[base])
            wait(four.at[:, :, full], S.rs_r.at[base + 1])
            for q, (yy, xx) in enumerate(plane):
                terms = []
                for j in range(1, n.z_n):
                    ref, k, _ = landing(q, j)
                    terms.append(ref[k, :, full])
                add_into(grads, chip(yy, z, xx), full, *terms)
            send(grads.at[far_chip, :, full], three.at[0, :, full], S.rs_s.at[base + 2], S.rs_r.at[base + 2], x_dev)
            later(three.at[0, :, full], S.rs_s.at[base + 2])

        def end_corner():
            wait(three.at[0, :, full], S.rs_r.at[base + 2])
            add_into(grads, y_chip, full, three[0, :, full])
            for k, index, target in ((1, y_chip, y_dev), (2, x_chip, x_dev)):
                send(grads.at[index, :, full], three.at[k, :, full], S.rs_s.at[base + 3 + k], S.rs_r.at[base + 3 + k], target)
                later(three.at[k, :, full], S.rs_s.at[base + 3 + k])

        def end_xy():
            total = grads[me_chip, :, full].astype(f32)
            for k in (1, 2):
                wait(three.at[k, :, full], S.rs_r.at[base + 3 + k])
                total = total + three[k, :, full].astype(f32)
            return total

        return start_z, end_z, end_corner, end_xy

    scatters = {p: [scatter_plane(p)] if p == "t" else [scatter_line(p, h) for h in range(2)] for p in n.sums}

    def scatter(p, stage):
        return [s[stage]() for s in scatters[p]]

    all_cot = jnp.concatenate([cot_of(0), cot_of(1)], axis=0)
    for q in range(4):
        lo = q * chunk
        S.g_shr[q * units : (q + 1) * units] = (
            dot_tn(S.hid[:, lo : lo + chunk], all_cot).astype(bf16).reshape(units, n.unit, n.width)
        )
    scatter("s", 0)
    S.gv[5:6, : n.width] = jnp.sum(cot_of(0).astype(f32), axis=0, keepdims=True)
    for w in waits:
        w()

    for part in range(2):
        r = slice(part * half, (part + 1) * half)
        grad = dot_nt((S.acc[r] + S.ped_r[r].astype(f32)).astype(bf16), S.perm[...])
        unit, scale = normalise(S.middle[r])
        if part == 0:
            S.gv[3:4, : n.width] = jnp.sum(grad * unit, axis=0, keepdims=True)
            S.gv[4:5, : n.width] = jnp.sum(grad, axis=0, keepdims=True)
        total = cot_of(part).astype(f32) + norm_back(unit, scale, grad * vector(3))
        S.acc[r] = total
        S.branch[r] = total.astype(bf16)

    for s in range(4):
        S.sg[token_rows(s), : n.cw] = dot_nt(S.branch[token_rows(s)], S.w2o[...])
    wait_g = to_channels(2, lambda s: S.sg[token_rows(s), : n.cw] * gate(s, 0))
    for s in range(4):
        S.sg[token_rows(s), : n.cw] = S.sg[token_rows(s), : n.cw] * S.low[token_rows(s)].astype(f32)

    def send_heads(lo, width):
        head_row = lax.broadcasted_iota(jnp.int32, (8, width), 0)
        heads = jnp.zeros((8, width), f32)
        for s in range(4):
            top = S.sg[s * blk : s * blk + 8, lo : lo + width]
            heads = heads + jnp.where(lax.div(head_row, 2) == s, pltpu.roll(top, 2 * s, 0) if s else top, 0.0)
        cols = pl.ds(lo, width)
        S.nb_s[:, cols] = heads
        return exchange(S.nb_s.at[:, cols], S.nb_r.at[:, cols], (ch, lax.rem(seq + n.seqs - 1, n.seqs)))

    def tap_sums(g):
        lo = g * n.cw
        sums = [jnp.zeros((1, n.cw), f32) for _ in range(4)]
        for s in range(4):
            grad = S.sg[token_rows(s), lo : lo + n.cw]
            now, one, two = shifted(s, lo)
            for i, term in enumerate((grad * two, grad * one, grad * now, grad)):
                sums[i] = sums[i] + jnp.sum(term, axis=0, keepdims=True)
        for i in range(4):
            S.gv[7 + i : 8 + i, lo : lo + n.cw] = sums[i]

    def mixed_back(g):
        lo = g * n.cw
        total = jnp.zeros((1, n.cw), f32)
        nexts = S.nb_r[:, lo : lo + n.cw]
        nexts = jnp.where(last_block, jnp.zeros_like(nexts), nexts)
        for s in range(4):
            grad = S.sg[token_rows(s), lo : lo + n.cw]
            tail = pltpu.roll(nexts, 8 - 2 * s, 0) if s else nexts
            both = jnp.concatenate([grad, tail], axis=0)
            low = (
                vector(9, lo, n.cw) * grad
                + vector(8, lo, n.cw) * pltpu.roll(both, blk + 7, 0)[:blk]
                + vector(7, lo, n.cw) * pltpu.roll(both, blk + 6, 0)[:blk]
            ).astype(bf16)
            S.mg[token_rows(s), lo : lo + n.cw] = low
            total = total + jnp.sum(low.astype(f32), axis=0, keepdims=True)
        S.gv[6:7, lo : lo + n.cw] = total
        S.g_mix[:, :, lo : lo + n.cw] = (
            dot_tn(S.n1p[0:rows], S.mg[:, lo : lo + n.cw]).astype(bf16).reshape(n.chips, n.pair, n.cw)
        )

    wait_nb = send_heads(0, n.cw)
    S.gv[2:3, : n.width] = jnp.sum(S.branch[0:half].astype(f32), axis=0, keepdims=True)
    gather("e", "sent")
    for q in range(4):
        lo = q * chunk
        S.w_exp[:, :, lo : lo + chunk] = (
            dot_tn(S.n2p[...], S.pre[:, lo : lo + chunk]).astype(bf16).reshape(n.chips, n.pair, chunk)
        )
    scatter("s", 1)
    scatter("e", 0)

    for part in (1, 0):
        r = slice(part * half, (part + 1) * half)
        value = dot_nn(S.hid[r], S.w_shr[...].reshape(n.hw, n.width))
        if part:
            S.peb_s[...] = value.astype(bf16)
            wait_bo, sent_bo = exchange(S.peb_s, S.peb_r, sib, free=True)
        else:
            S.middle[r] = S.middle[r] + value + vector(5)
    outs = dot_tn(S.gated[...], S.branch[...]).reshape(n.chips, n.own, n.width)
    S.g_out[...] = jnp.concatenate([outs[:, :, : n.cw], outs[:, :, n.cw :]], axis=1).astype(bf16)
    tap_sums(0)
    wait_nb()
    mixed_back(0)
    wait_bo()
    sent_bo()
    S.bo[...] = (S.middle[0:half] + S.peb_r[...].astype(f32)).astype(bf16).reshape(2, blk, n.width)
    wait_g()
    scatter("t", 0)

    flat = lax.broadcasted_iota(jnp.int32, (blk, blk), 0) + lax.broadcasted_iota(jnp.int32, (blk, blk), 1)
    mirror = jnp.where(flat == blk - 1, 1.0, 0.0).astype(bf16)
    S.gf[...] = S.rb2[...].astype(f32).reshape(n.chips * n.slab, LANES)
    S.gm[...] = dot_nn(S.rb2[...].reshape(n.chips * n.slab, LANES), mirror)
    S.uf[...] = dot_nn(S.rb0[...].reshape(n.chips * n.slab, LANES), mirror)

    def conv_back(r, carry):
        turned = channel_rows(S.gm, r)
        wide = dot_nn(turned.astype(bf16), S.toep[r])
        blocks = []
        for i in range(n.seqs):
            total = wide[group * i : group * (i + 1), 0:LANES]
            for k in range(1, n.seqs - i):
                total = total + wide[group * (i + k) : group * (i + k + 1), LANES * k : LANES * (k + 1)]
            blocks.append(total)
        back = jnp.concatenate(blocks, axis=0) + S.fsel[pl.ds(r, 1), 65:66] * turned
        S.of[pl.ds(r, lines, stride=n.own), :] = dot_nn(back.astype(bf16), mirror)
        grad = channel_rows(S.gf, r)
        steps = [grad]
        for k in range(1, n.seqs):
            steps.append(
                jnp.concatenate([grad[group * k :], jnp.zeros((group * k, LANES), f32)], axis=0)
            )
        ahead = jnp.concatenate(steps, axis=1).astype(bf16)
        outer = dot_tn(channel_rows(S.uf, r).astype(bf16), ahead)
        outer = jnp.concatenate([jnp.zeros((blk, LANES), f32), outer], axis=1)
        outer = pltpu.roll(outer, n.length + 1, 1, stride=1, stride_axis=0)
        S.ig[pl.ds(r, 1), :] = jnp.sum(outer, axis=0, keepdims=True)[:, LANES:]
        return carry

    for q, steps in enumerate(((("s", 2),), (("e", 1), ("o", 0), ("m0", 0)), ())):
        lax.fori_loop(q * third, (q + 1) * third, conv_back, 0)
        if q == 2:
            wait_in = to_tokens(3)
        for p, stage in steps:
            scatter(p, stage)

    d_line = S.ig[...] * decay()
    fg_rows = pl.ds(pl.multiple_of(me_dev * n.own, 8), n.own)
    S.fg[fg_rows, :] = dot_nt(d_line, S.l2[...], hi)
    wait_fg = to_chips(lambda yy, zz, xx: S.fg.at[fg_rows], S.fg.at[fg_rows], S.fg.at[pl.ds(0, (n.chips - 1) * n.own)])
    d_l2 = dot_tn(S.fsel[:, 0:64], d_line, hi) * S.c2[...]
    d_u2 = d_l2 * S.fvec[0:64, 3:4]
    none = jnp.zeros((64, n.length), f32)
    unit_row = lax.broadcasted_iota(jnp.int32, (64, n.length), 0)

    def on_row(r):
        return jnp.where(unit_row == r, 1.0, 0.0)

    net = dot_nt(S.l1[...], jnp.concatenate([d_u2, none], axis=0), hi)
    net = net + dot_nt(on_row(42), jnp.concatenate([none, d_u2], axis=0), hi)
    net = net + dot_nt(on_row(43), jnp.concatenate([none, d_l2 * S.u2[...]], axis=0), hi)
    d_l1 = dot_nn(S.inw[...], d_u2, hi) * S.c1[...]
    d_u1 = d_l1 * S.fvec[0:64, 1:2]
    net = net + dot_nt(on_row(41), jnp.concatenate([none, d_l1 * S.u1[...]], axis=0), hi)
    net = net + dot_nt(S.enc[...] + on_row(40), jnp.concatenate([none, d_u1], axis=0), hi)
    S.msgs[pl.ds(12, n.devices, stride=16), :] = net[0 : n.devices]
    S.msgs[pl.ds(13, n.devices, stride=16), :] = net[n.devices :]
    scatter("e", 2)
    scatter("o", 1)
    scatter("m0", 1)
    wait_in()

    for s in range(4):
        grad = token_view(3, s)
        S.sg[token_rows(s), n.cw : 2 * n.cw] = grad * gate(s, 2)
        S.sg[token_rows(s), 2 * n.cw :] = grad * gate(s, 1)
    wait_nb = send_heads(n.cw, 2 * n.cw)
    tap_sums(1)
    tap_sums(2)
    wait_nb()
    mixed_back(1)
    scatter("m1", 0)
    mixed_back(2)
    scatter("m2", 0)
    scatter("o", 2)
    scatter("m0", 2)
    scatter("t", 1)
    weight = S.w_mix[...].reshape(n.width, n.mw)
    S.peb_s[...] = dot_nt(S.mg[half:rows], weight).astype(bf16)
    wait_f = exchange(S.peb_s, S.pef_r, sib)
    mine = dot_nt(S.mg[0:half], weight)
    scatter("m1", 1)
    wait_f()
    grad = dot_nt((mine + S.pef_r[...].astype(f32)).astype(bf16), S.perm[...])
    unit, scale = normalise(tokens_of(0))
    S.gv[0:1, : n.width] = jnp.sum(grad * unit, axis=0, keepdims=True)
    S.gv[1:2, : n.width] = jnp.sum(grad, axis=0, keepdims=True)
    S.tg[...] = (S.acc[0:half] + norm_back(unit, scale, grad * vector(0))).astype(bf16).reshape(2, blk, n.width)
    scatter("m2", 1)

    for members, right, mask in groups:
        width = right.shape[1]
        for i in members:
            value = S.gv[i : i + 1, :width] * mask[...]
            S.msgs[pl.ds(i, n.devices, stride=16), :] = sum(
                dot_nt(term, right[...]) for term in split_three(value)
            )
    S.msgs[pl.ds(14, n.devices, stride=16), :] = jnp.zeros((n.devices, LANES), f32)
    S.msgs[pl.ds(15, n.devices, stride=16), :] = jnp.zeros((n.devices, LANES), f32)

    def message(d):
        return pl.ds(pl.multiple_of(d * 16, 16), 16)

    wait_msgs = to_others(
        lambda d: S.msgs.at[message(d)], S.rall.at[message(me_dev)], S.rall.at[pl.ds(0, (n.devices - 1) * 16)]
    )
    S.rall[message(me_dev), :] = S.msgs[message(me_dev), :]
    scatter("t", 2)
    scatter("m1", 2)
    scatter("m2", 2)

    wait_fg()
    sib_waits = []
    for yy in range(n.y_n):
        span = pl.ds(pl.multiple_of((yy * 2 + core) * n.seqs * n.own, 8), n.seqs * n.own)
        sib_span = pl.ds(pl.multiple_of((yy * 2 + 1 - core) * n.seqs * n.own, 8), n.seqs * n.own)
        k = exchange_count[0]
        exchange_count[0] += 1
        send(S.fg.at[span], S.fg.at[span], S.ex_s.at[k], S.ex_r.at[k], sib)
        later(S.fg.at[span], S.ex_s.at[k])
        sib_waits.append((sib_span, k))
    wait_msgs()
    total = jnp.sum(S.rall[...].reshape(n.devices, 16, LANES), axis=0)
    S.smf[...] = total
    S.gsm[...] = total
    fall_rows = pl.ds(pl.multiple_of(me_dev * 8, 8), 8)
    wait_net = to_others(
        lambda d: S.smf.at[pl.ds(8, 8)], S.fall.at[fall_rows], S.fall.at[pl.ds(0, (n.devices - 1) * 8)]
    )
    S.fall[fall_rows, :] = total[8:16]
    sent_pre()

    def finish(p, ref, at_col):
        lo = at_col
        for value in scatter(p, 3):
            ref[:, lo : lo + value.shape[1]] = value
            lo += value.shape[1]

    finish("s", S.gshr, 0)
    finish("t", S.gshr, n.sums["t"][1])
    both = jnp.concatenate(scatter("o", 3), axis=1)
    S.gout[:, : n.cw], S.gout[:, n.cw :] = both[: n.own], both[n.own :]
    finish("e", S.wpre, n.mw)
    finish("m0", S.wpre, 0)
    for span, k in sib_waits:
        wait(S.fg.at[span], S.ex_r.at[k])
    finish("m1", S.wpre, n.cw)
    finish("m2", S.wpre, 2 * n.cw)
    wait_fin = exchange(S.wpre.at[theirs], S.wrecv, sib)
    S.gmix[core] = S.wpre[ours, : n.mw]
    S.gexp[core] = S.wpre[ours, n.mw :]
    wait_net()
    S.gnet[0 : n.devices] = S.fall[pl.ds(4, n.devices, stride=8), :]
    S.gnet[n.devices :] = S.fall[pl.ds(5, n.devices, stride=8), :]
    wait_fin()
    S.gmix[1 - core] = S.wrecv[:, : n.mw]
    S.gexp[1 - core] = S.wrecv[:, n.mw :]
    for p in "most":
        gather(p, "sent")
    for ref, sem in ends:
        wait(ref, sem)


def emit_kernel(n, emb, bo, tg, gmix, gexp, gout, gshr, gsm, fg, gnet, *outs):
    (o_bo, o_tg, o_g1, o_s1, o_mix, o_mixb, o_sw, o_sb, o_embw, o_be, o_fs, o_inw, o_bi, o_ss, o_fw, o_lb, o_out,
     o_outb, o_g2, o_s2, o_exp, o_expb, o_shr, o_shrb) = outs
    o_bo[:, 0], o_tg[:, 0] = bo[...], tg[...]
    span, wide_span = n.cw // 2, n.hw // 2
    for k in range(2):
        for yy in range(2):
            for g in range(3):
                lo, dst = g * n.cw + yy * span, g * n.width + (2 * yy + k) * span
                o_mix[:, dst : dst + span] = gmix[k, :, lo : lo + span]
            lo, dst = yy * wide_span, (2 * yy + k) * wide_span
            o_exp[:, dst : dst + wide_span] = gexp[k, :, lo : lo + wide_span]
    o_out[...], o_shr[...] = gout[...], gshr[...]
    for i, ref in ((0, o_g1), (1, o_s1), (2, o_outb), (3, o_g2), (4, o_s2), (5, o_shrb), (6, o_mixb), (10, o_sb), (11, o_expb)):
        size = ref.shape[0]
        ref[...] = gsm[i : i + 1, :size].reshape(size)
    o_sw[...] = gsm[7:10, : n.tap]
    o_inw[...] = gnet[:, :64]
    o_embw[...] = gnet[:emb, 64:]
    for i, ref in ((40, o_be), (41, o_fs), (42, o_bi), (43, o_ss)):
        ref[...] = gnet[i : i + 1, 64:].reshape(64)
    filt = jnp.transpose(fg[...])
    o_fw[...] = filt[0:64]
    o_lb[...] = filt[64:65].reshape(n.width)


def fused(n, *args):
    emb = args[8].shape[0]
    tables_in = (jnp.asarray(tables(n)), jnp.asarray(encoding_table(n.length, (emb - 1) // 2, 64)))
    shape = jax.ShapeDtypeStruct
    outs = (
        shape((2, n.block, n.width), bf16), shape((2, n.block, n.width), bf16),
        shape((2, n.own, n.mw), f32), shape((2, n.own, n.hw), f32), shape((n.own, n.width), f32),
        shape((n.unit, n.width), f32), shape((16, LANES), f32), shape((n.width, LANES), f32),
        shape((64, LANES), f32),
    )
    scratch = scratch_list(n)
    names = INPUTS + OUTPUTS + tuple(name for name, _ in scratch)
    vmem = pl.BlockSpec(memory_space=pltpu.VMEM)
    results = pl.pallas_call(
        functools.partial(fused_kernel, n, names),
        out_shape=outs,
        in_specs=[vmem] * len(INPUTS),
        out_specs=[vmem] * len(outs),
        scratch_shapes=[s for _, s in scratch],
        compiler_params=pltpu.CompilerParams(
            collective_id=0, has_side_effects=True, vmem_limit_bytes=63 << 20
        ),
    )(*args, *tables_in)
    like = args[:1] * 2 + args[2:15] + args[16:]
    final = tuple(shape(a.shape, f32 if i > 1 else bf16) for i, a in enumerate(like))
    return pl.pallas_call(
        functools.partial(emit_kernel, n, emb),
        out_shape=final,
        in_specs=[vmem] * len(outs),
        out_specs=[vmem] * len(final),
        compiler_params=pltpu.CompilerParams(vmem_limit_bytes=63 << 20),
    )(*results)


highest = lax.Precision.HIGHEST


def from_behind(block, axis, distance):
    devices = range(lax.axis_size(axis))
    route = [(i - distance, i) for i in devices if i - distance in devices]
    return lax.ppermute(block, axis, route)


def matmul(left, right):
    return jnp.dot(left, right, precision=highest, preferred_element_type=jnp.float32)


def layer_norm(values, gain, shift):
    centre = values - jnp.mean(values, axis=-1, keepdims=True)
    spread = jnp.mean(centre * centre, axis=-1, keepdims=True)
    return centre * lax.rsqrt(spread + 1e-05) * gain + shift


def exact_gelu(values):
    return jax.nn.gelu(values, approximate=False)


def filter_values(
    seq_length,
    embed_matrix,
    embed_offset,
    sine_first,
    inner_matrix,
    inner_offset,
    sine_second,
    head_matrix,
    rates,
):
    positions = jnp.arange(seq_length).astype(jnp.float32)
    band_count = (embed_matrix.shape[0] - 1) // 2
    frequency = jnp.linspace(0.0001, band_count - 1, band_count).astype(jnp.float32)
    angles = 2.0 * jnp.pi / seq_length * positions[:, None] * frequency[None, :]
    encoded = jnp.concatenate(
        [positions[:, None] / (seq_length - 1), jnp.cos(angles), -jnp.sin(angles)], axis=1
    )
    layer_first = jnp.sin(sine_first * (matmul(encoded, embed_matrix) + embed_offset))
    layer_second = jnp.sin(sine_second * (matmul(layer_first, inner_matrix) + inner_offset))
    return matmul(layer_second, head_matrix) * jnp.exp(-rates[None, :] * positions[:, None])


def spectral_tables(block_rows):
    period = 2 * block_rows
    freq_rows = jnp.arange(block_rows + 1)
    sample_cols = jnp.arange(period)
    phase = (freq_rows[:, None] * sample_cols[None, :] % period).astype(jnp.float32) * (
        2.0 * jnp.pi / period
    )
    forward_full = jnp.concatenate([jnp.cos(phase), -jnp.sin(phase)], axis=0)
    out_times = jnp.arange(block_rows) + block_rows
    out_phase = (out_times[:, None] * freq_rows[None, :] % period).astype(jnp.float32) * (
        2.0 * jnp.pi / period
    )
    edge = (freq_rows == 0) | (freq_rows == block_rows)
    factor = jnp.where(edge, 1.0, 2.0).astype(jnp.float32) / period
    inverse_table = jnp.concatenate(
        [factor[None, :] * jnp.cos(out_phase), -factor[None, :] * jnp.sin(out_phase)], axis=1
    )
    return (forward_full, inverse_table)


def spec_product(filt, spectrum):
    return jnp.stack(
        [
            filt[0] * spectrum[0] - filt[1] * spectrum[1],
            filt[0] * spectrum[1] + filt[1] * spectrum[0],
        ]
    )


def spec_adjoint(filt, grad_spec):
    return jnp.stack(
        [
            filt[0] * grad_spec[0] + filt[1] * grad_spec[1],
            filt[0] * grad_spec[1] - filt[1] * grad_spec[0],
        ]
    )


def contract_rows(left, right):
    return lax.dot_general(
        left, right, (((0,), (0,)), ((), ())), preferred_element_type=jnp.float32
    )


def contract_cols(left, right):
    return lax.dot_general(
        left, right, (((1,), (1,)), ((), ())), preferred_element_type=jnp.float32
    )


def on_device(
    tokens,
    cotangent,
    first_gain,
    first_shift,
    mixer_weight,
    mixer_bias,
    short_weight,
    short_bias,
    embed_weight,
    embed_bias,
    first_sine,
    inner_weight,
    inner_bias,
    second_sine,
    filter_weight,
    decay_rate,
    long_bias,
    output_weight,
    output_bias,
    second_gain,
    second_shift,
    expand_weight,
    expand_bias,
    shrink_weight,
    shrink_bias,
):
    chan_count = lax.axis_size("ch")
    seq_count = lax.axis_size("seq")
    chan_index = lax.axis_index("ch")
    seq_index = lax.axis_index("seq")
    block_rows = tokens.shape[2]
    width = tokens.shape[3]
    span_width = width // chan_count
    seq_length = block_rows * seq_count
    freq_count = block_rows + 1
    gathered = (
        lax.all_gather(first_gain, ("ch", "seq"), axis=0, tiled=True),
        lax.all_gather(first_shift, ("ch", "seq"), axis=0, tiled=True),
        lax.all_gather(mixer_weight, ("ch", "seq"), axis=0, tiled=True),
        lax.all_gather(mixer_bias, ("ch", "seq"), axis=0, tiled=True),
        lax.all_gather(short_weight, ("ch", "seq"), axis=1, tiled=True),
        lax.all_gather(short_bias, ("ch", "seq"), axis=0, tiled=True),
        lax.all_gather(output_weight, ("ch", "seq"), axis=0, tiled=True),
        lax.all_gather(output_bias, ("ch", "seq"), axis=0, tiled=True),
        lax.all_gather(second_gain, ("ch", "seq"), axis=0, tiled=True),
        lax.all_gather(second_shift, ("ch", "seq"), axis=0, tiled=True),
        lax.all_gather(expand_weight, ("ch", "seq"), axis=0, tiled=True),
        lax.all_gather(expand_bias, ("ch", "seq"), axis=0, tiled=True),
        lax.all_gather(shrink_weight, ("ch", "seq"), axis=0, tiled=True),
        lax.all_gather(shrink_bias, ("ch", "seq"), axis=0, tiled=True),
    )
    (
        gain_one,
        shift_one,
        mix_matrix,
        mix_offset,
        short_taps,
        short_offset,
        out_matrix,
        out_offset,
        gain_two,
        shift_two,
        expand_matrix,
        expand_offset,
        shrink_matrix,
        shrink_offset,
    ) = gathered
    gain_one_f = gain_one.astype(jnp.float32)
    shift_one_f = shift_one.astype(jnp.float32)
    mix_offset_f = mix_offset.astype(jnp.float32)
    taps_f = short_taps.astype(jnp.float32)
    short_offset_f = short_offset.astype(jnp.float32)
    out_offset_f = out_offset.astype(jnp.float32)
    gain_two_f = gain_two.astype(jnp.float32)
    shift_two_f = shift_two.astype(jnp.float32)
    expand_offset_f = expand_offset.astype(jnp.float32)
    shrink_offset_f = shrink_offset.astype(jnp.float32)

    def local_filter(params):
        (
            embed_matrix,
            embed_offset,
            sine_a,
            inner_matrix,
            inner_offset,
            sine_b,
            head_matrix,
            skip_gain,
        ) = params
        head_slice = lax.dynamic_slice_in_dim(head_matrix, chan_index * span_width, span_width, 1)
        rate_slice = lax.dynamic_slice_in_dim(decay_rate, chan_index * span_width, span_width, 0)
        skip_slice = lax.dynamic_slice_in_dim(skip_gain, chan_index * span_width, span_width, 0)
        impulse_part = filter_values(
            seq_length,
            embed_matrix,
            embed_offset,
            sine_a,
            inner_matrix,
            inner_offset,
            sine_b,
            head_slice,
            rate_slice,
        )
        return (impulse_part, skip_slice)

    filter_params = (
        embed_weight,
        embed_bias,
        first_sine,
        inner_weight,
        inner_bias,
        second_sine,
        filter_weight,
        long_bias,
    )
    (impulse, skip_part), filter_back = jax.vjp(local_filter, filter_params)
    skip_tiled = jnp.tile(skip_part, chan_count)
    forward_full, inverse_table = spectral_tables(block_rows)
    forward_half = forward_full[:, :block_rows]
    inverse_adjoint = inverse_table.T
    impulse_blocks = impulse.reshape(seq_count, block_rows, span_width)
    earlier = jnp.concatenate([jnp.zeros_like(impulse_blocks[:1]), impulse_blocks[:-1]], axis=0)
    segments = jnp.concatenate([earlier, impulse_blocks], axis=1)
    filt_spec = jnp.einsum("fm,nmc->nfc", forward_full, segments, precision=highest)
    filt_spec = filt_spec.reshape(seq_count, 2, freq_count, 1, span_width)
    zero_spec = jnp.zeros((2 * freq_count, width), jnp.float32)

    def contribution(spectrum, source):
        distance = seq_index - source
        causal = (distance >= 0).astype(jnp.float32)
        slot_index = jnp.clip(distance, 0, seq_count - 1)
        filt = lax.dynamic_index_in_dim(filt_spec, slot_index, 0, keepdims=False)
        shaped = spectrum.reshape(2, freq_count, chan_count, span_width)
        return causal * spec_product(filt, shaped).reshape(2 * freq_count, width)

    def micro_step(carry, inputs):
        grads, filt_grad, skip_grad = carry
        block_in, block_cot = inputs
        resid = block_in.astype(jnp.float32)
        normed_one, norm_back_one = jax.vjp(layer_norm, resid, gain_one_f, shift_one_f)
        normed_low = normed_one.astype(jnp.bfloat16)
        mixed = (
            jnp.dot(normed_low, mix_matrix, preferred_element_type=jnp.float32) + mix_offset_f
        ).astype(jnp.bfloat16)
        before = from_behind(mixed[block_rows - 2 :], "seq", 1)
        padded = jnp.concatenate([before, mixed], axis=0).astype(jnp.float32)
        short_out = (
            taps_f[0] * padded[:-2]
            + taps_f[1] * padded[1:-1]
            + taps_f[2] * padded[2:]
            + short_offset_f
        )
        gate_out = short_out[:, :width]
        gate_in = short_out[:, width : 2 * width]
        values = short_out[:, 2 * width :]
        product = (gate_in * values).astype(jnp.bfloat16)
        channel_view = lax.all_to_all(
            product.reshape(block_rows, chan_count, span_width),
            "ch",
            split_axis=1,
            concat_axis=1,
            tiled=True,
        ).reshape(block_rows, width)
        own_float = channel_view.astype(jnp.float32)
        own_spec = matmul(forward_half, own_float)
        shard_piece = lax.all_gather(channel_view[None], "seq", axis=0, tiled=True)

        def add_single(offset, partial_value):
            spectrum = matmul(forward_half, shard_piece[offset].astype(jnp.float32))
            return partial_value + contribution(spectrum, offset)

        summed = lax.fori_loop(0, shard_piece.shape[0], add_single, zero_spec)
        long_out = matmul(inverse_table, summed) + skip_tiled * own_float
        long_low = long_out.astype(jnp.bfloat16)
        token_view = lax.all_to_all(
            long_low.reshape(block_rows, chan_count, span_width),
            "ch",
            split_axis=1,
            concat_axis=1,
            tiled=True,
        ).reshape(block_rows, width)
        token_float = token_view.astype(jnp.float32)
        gated_out = (gate_out * token_float).astype(jnp.bfloat16)
        middle = (
            resid
            + jnp.dot(gated_out, out_matrix, preferred_element_type=jnp.float32)
            + out_offset_f
        )
        normed_two, norm_back_two = jax.vjp(layer_norm, middle, gain_two_f, shift_two_f)
        normed_two_low = normed_two.astype(jnp.bfloat16)
        hidden_pre = (
            jnp.dot(normed_two_low, expand_matrix, preferred_element_type=jnp.float32)
            + expand_offset_f
        )
        hidden_act, gelu_back = jax.vjp(exact_gelu, hidden_pre)
        hidden_low = hidden_act.astype(jnp.bfloat16)
        result = (
            middle
            + jnp.dot(hidden_low, shrink_matrix, preferred_element_type=jnp.float32)
            + shrink_offset_f
        )
        block_result = result.astype(jnp.bfloat16)
        grad_out = block_cot.astype(jnp.float32)
        shrink_grad = contract_rows(hidden_low, block_cot)
        shrink_off_grad = jnp.sum(grad_out, axis=0)
        hidden_grad = contract_cols(block_cot, shrink_matrix)
        pre_grad = gelu_back(hidden_grad)[0].astype(jnp.bfloat16)
        expand_grad = contract_rows(normed_two_low, pre_grad)
        expand_off_grad = jnp.sum(pre_grad.astype(jnp.float32), axis=0)
        normed_two_grad = contract_cols(pre_grad, expand_matrix)
        middle_ln_grad, gain_two_grad, shift_two_grad = norm_back_two(normed_two_grad)
        middle_grad = grad_out + middle_ln_grad
        branch_low = middle_grad.astype(jnp.bfloat16)
        out_grad = contract_rows(gated_out, branch_low)
        out_off_grad = jnp.sum(branch_low.astype(jnp.float32), axis=0)
        gated_grad = contract_cols(branch_low, out_matrix)
        gate_out_grad = gated_grad * token_float
        token_grad = (gated_grad * gate_out).astype(jnp.bfloat16)
        channel_grad = lax.all_to_all(
            token_grad.reshape(block_rows, chan_count, span_width),
            "ch",
            split_axis=1,
            concat_axis=1,
            tiled=True,
        ).reshape(block_rows, width)
        channel_grad_f = channel_grad.astype(jnp.float32)
        own_shaped = own_spec.reshape(2, freq_count, chan_count, span_width)

        def back_term(running, grad_spec, target):
            spec_acc, filt_acc = running
            distance = target - seq_index
            causal = (distance >= 0).astype(jnp.float32)
            slot_index = jnp.clip(distance, 0, seq_count - 1)
            filt = lax.dynamic_index_in_dim(filt_spec, slot_index, 0, keepdims=False)
            shaped = grad_spec.reshape(2, freq_count, chan_count, span_width)
            spec_acc = spec_acc + causal * spec_adjoint(filt, shaped).reshape(2 * freq_count, width)
            filt_term = causal * jnp.sum(spec_adjoint(own_shaped, shaped), axis=2, keepdims=True)
            current = lax.dynamic_index_in_dim(filt_acc, slot_index, 0, keepdims=True)
            filt_acc = lax.dynamic_update_index_in_dim(
                filt_acc, current + filt_term[None], slot_index, 0
            )
            return (spec_acc, filt_acc)

        back_shard_piece = lax.all_gather(channel_grad[None], "seq", axis=0, tiled=True)

        def back_single(offset, partial_value):
            grad_spec = matmul(inverse_adjoint, back_shard_piece[offset].astype(jnp.float32))
            return back_term(partial_value, grad_spec, offset)

        spec_grad, filt_grad = lax.fori_loop(
            0, back_shard_piece.shape[0], back_single, (zero_spec, filt_grad)
        )
        input_grad = (
            lax.dot_general(
                forward_half,
                spec_grad,
                (((0,), (0,)), ((), ())),
                precision=highest,
                preferred_element_type=jnp.float32,
            )
            + skip_tiled * channel_grad_f
        )
        skip_grad = skip_grad + jnp.sum(
            (channel_grad_f * own_float).reshape(block_rows, chan_count, span_width), axis=(0, 1)
        )
        input_low = input_grad.astype(jnp.bfloat16)
        token_input = (
            lax.all_to_all(
                input_low.reshape(block_rows, chan_count, span_width),
                "ch",
                split_axis=1,
                concat_axis=1,
                tiled=True,
            )
            .reshape(block_rows, width)
            .astype(jnp.float32)
        )
        short_grad = jnp.concatenate(
            [gate_out_grad, token_input * values, token_input * gate_in], axis=1
        )
        short_off_grad = jnp.sum(short_grad, axis=0)
        taps_grad = jnp.stack(
            [
                jnp.sum(short_grad * padded[:-2], axis=0),
                jnp.sum(short_grad * padded[1:-1], axis=0),
                jnp.sum(short_grad * padded[2:], axis=0),
            ]
        )
        padded_grad = (
            jnp.pad(taps_f[0] * short_grad, ((0, 2), (0, 0)))
            + jnp.pad(taps_f[1] * short_grad, ((1, 1), (0, 0)))
            + jnp.pad(taps_f[2] * short_grad, ((2, 0), (0, 0)))
        )
        after = from_behind(padded_grad[:2], "seq", -1)
        mixed_grad = padded_grad[2:] + jnp.concatenate(
            [jnp.zeros((block_rows - 2, 3 * width), jnp.float32), after], axis=0
        )
        mixed_low = mixed_grad.astype(jnp.bfloat16)
        mix_grad = contract_rows(normed_low, mixed_low)
        mix_off_grad = jnp.sum(mixed_low.astype(jnp.float32), axis=0)
        normed_one_grad = contract_cols(mixed_low, mix_matrix)
        resid_ln_grad, gain_one_grad, shift_one_grad = norm_back_one(normed_one_grad)
        tokens_grad = (middle_grad + resid_ln_grad).astype(jnp.bfloat16)
        step_grads = (
            gain_one_grad,
            shift_one_grad,
            mix_grad,
            mix_off_grad,
            taps_grad,
            short_off_grad,
            out_grad,
            out_off_grad,
            gain_two_grad,
            shift_two_grad,
            expand_grad,
            expand_off_grad,
            shrink_grad,
            shrink_off_grad,
        )
        grads = jax.tree.map(lambda left, right: left + right, grads, step_grads)
        return ((grads, filt_grad, skip_grad), (block_result, tokens_grad))

    zero_grads = tuple((jnp.zeros(item.shape, jnp.float32) for item in gathered))
    init = (zero_grads, jnp.zeros_like(filt_spec), jnp.zeros((span_width,), jnp.float32))
    (grads, filt_grad, skip_grad), (results, token_grads) = lax.scan(
        micro_step, init, (tokens[:, 0], cotangent[:, 0])
    )
    shards = (
        lax.psum_scatter(grads[0], ("ch", "seq"), scatter_dimension=0, tiled=True),
        lax.psum_scatter(grads[1], ("ch", "seq"), scatter_dimension=0, tiled=True),
        lax.psum_scatter(grads[2], ("ch", "seq"), scatter_dimension=0, tiled=True),
        lax.psum_scatter(grads[3], ("ch", "seq"), scatter_dimension=0, tiled=True),
        lax.psum_scatter(grads[4], ("ch", "seq"), scatter_dimension=1, tiled=True),
        lax.psum_scatter(grads[5], ("ch", "seq"), scatter_dimension=0, tiled=True),
        lax.psum_scatter(grads[6], ("ch", "seq"), scatter_dimension=0, tiled=True),
        lax.psum_scatter(grads[7], ("ch", "seq"), scatter_dimension=0, tiled=True),
        lax.psum_scatter(grads[8], ("ch", "seq"), scatter_dimension=0, tiled=True),
        lax.psum_scatter(grads[9], ("ch", "seq"), scatter_dimension=0, tiled=True),
        lax.psum_scatter(grads[10], ("ch", "seq"), scatter_dimension=0, tiled=True),
        lax.psum_scatter(grads[11], ("ch", "seq"), scatter_dimension=0, tiled=True),
        lax.psum_scatter(grads[12], ("ch", "seq"), scatter_dimension=0, tiled=True),
        lax.psum_scatter(grads[13], ("ch", "seq"), scatter_dimension=0, tiled=True),
    )
    segment_grad = jnp.einsum(
        "fm,nfc->nmc",
        forward_full,
        filt_grad.reshape(seq_count, 2 * freq_count, span_width),
        precision=highest,
    )
    impulse_grad = segment_grad[:, block_rows:] + jnp.concatenate(
        [segment_grad[1:, :block_rows], jnp.zeros((1, block_rows, span_width), jnp.float32)], axis=0
    )
    local_grads = filter_back((impulse_grad.reshape(seq_length, span_width), skip_grad))[0]
    summed_filter = lax.psum(local_grads, ("ch", "seq"))
    return (
        results[:, None],
        token_grads[:, None],
        shards[0],
        shards[1],
        shards[2],
        shards[3],
        shards[4],
        shards[5],
        summed_filter[0],
        summed_filter[1],
        summed_filter[2],
        summed_filter[3],
        summed_filter[4],
        summed_filter[5],
        summed_filter[6],
        summed_filter[7],
        shards[6],
        shards[7],
        shards[8],
        shards[9],
        shards[10],
        shards[11],
        shards[12],
        shards[13],
    )


def block(*args):
    tokens, expand_weight = args[0], args[21]
    n = Sizes(
        lax.axis_size("ch"), lax.axis_size("seq"), tokens.shape[2], tokens.shape[3], expand_weight.shape[1]
    )
    if n.own % 8 == 0 and n.pair % 16 == 0 and n.unit % 16 == 0 and n.block == LANES:
        return fused(n, *args)
    return on_device(*args)


def solution(mesh):
    return jax.shard_map(
        block,
        mesh=mesh,
        in_specs=(
            P(None, "ch", "seq", None),
            P(None, "ch", "seq", None),
            P(("ch", "seq")),
            P(("ch", "seq")),
            P(("ch", "seq"), None),
            P(("ch", "seq")),
            P(None, ("ch", "seq")),
            P(("ch", "seq")),
            P(),
            P(),
            P(),
            P(),
            P(),
            P(),
            P(),
            P(),
            P(),
            P(("ch", "seq"), None),
            P(("ch", "seq")),
            P(("ch", "seq")),
            P(("ch", "seq")),
            P(("ch", "seq"), None),
            P(("ch", "seq")),
            P(("ch", "seq"), None),
            P(("ch", "seq")),
        ),
        out_specs=(
            P(None, "ch", "seq", None),
            P(None, "ch", "seq", None),
            P(("ch", "seq")),
            P(("ch", "seq")),
            P(("ch", "seq"), None),
            P(("ch", "seq")),
            P(None, ("ch", "seq")),
            P(("ch", "seq")),
            P(),
            P(),
            P(),
            P(),
            P(),
            P(),
            P(),
            P(),
            P(("ch", "seq"), None),
            P(("ch", "seq")),
            P(("ch", "seq")),
            P(("ch", "seq")),
            P(("ch", "seq"), None),
            P(("ch", "seq")),
            P(("ch", "seq"), None),
            P(("ch", "seq")),
        ),
        check_vma=False,
    )
```

```python
import functools
import types

import jax
import jax.numpy as jnp
import numpy as np
from jax import lax
from jax.experimental import pallas as pl
from jax.experimental.pallas import tpu as pltpu
from jax.sharding import PartitionSpec as P


MESH = pl.DeviceIdType.MESH
f32 = jnp.float32
bf16 = jnp.bfloat16
LANES = 128
PIECES = ("mix", "out", "exp", "shr")


def dot_nn(left, right, precision=None):
    return lax.dot_general(
        left, right, (((1,), (0,)), ((), ())), precision=precision, preferred_element_type=f32
    )


def dot_nt(left, right, precision=None):
    return lax.dot_general(
        left, right, (((1,), (1,)), ((), ())), precision=precision, preferred_element_type=f32
    )


def dot_tn(left, right, precision=None):
    return lax.dot_general(
        left, right, (((0,), (0,)), ((), ())), precision=precision, preferred_element_type=f32
    )


def normalise(values):
    centre = values - jnp.mean(values, axis=-1, keepdims=True)
    scale = lax.rsqrt(jnp.mean(centre * centre, axis=-1, keepdims=True) + 1e-05)
    return centre * scale, scale


def norm_back(unit, scale, grad):
    inner = grad - jnp.mean(grad, axis=-1, keepdims=True)
    return scale * (inner - unit * jnp.mean(grad * unit, axis=-1, keepdims=True))


def sin_cos(angle):
    turns = jnp.floor(angle * (1.0 / np.pi) + 0.5)
    rest = angle - turns * 3.140625
    rest = rest - turns * 9.670257568359375e-4
    rest = rest - turns * 6.2771141529083251953e-7
    rest = rest - turns * 1.21644916362129151821e-10
    sign = 1.0 - 2.0 * (turns - 2.0 * jnp.floor(turns * 0.5))
    sq = rest * rest
    low = sq * (1.0 / 362880.0 - sq * (1.0 / 39916800.0 - sq * (1.0 / 6227020800.0)))
    sine = rest * (1.0 - sq * (1.0 / 6.0 - sq * (1.0 / 120.0 - sq * (1.0 / 5040.0 - low))))
    high = sq * (1.0 / 3628800.0 - sq * (1.0 / 479001600.0 - sq * (1.0 / 87178291200.0)))
    cosine = 1.0 - sq * (0.5 - sq * (1.0 / 24.0 - sq * (1.0 / 720.0 - sq * (1.0 / 40320.0 - high))))
    return sign * sine, sign * cosine


def split_two(value):
    top = value.astype(bf16)
    return top, (value - top.astype(f32)).astype(bf16)


def dot_two(dot, left, right):
    top, low = split_two(left)
    right = right.astype(bf16)
    return dot(top, right) + dot(low, right)


STEPS = {
    ("shrink",): (("s", 0),),
    ("expand",): (("s", 1), ("e", 0)),
    ("after", "grad"): (("t", 0),),
    ("conv_back", 0): (("s", 2),),
    ("conv_back", 1): (("o", 0), ("m0", 0)),
    ("conv_back", 2): (("e", 1),),
    ("before", "input"): (("e", 2), ("o", 1), ("m0", 1)),
    ("mixer", 1): (("m1", 0),),
    ("mixer", 2): (("m2", 0), ("o", 2), ("m0", 2), ("t", 1)),
    ("first", "norm"): (("m1", 1),),
    ("tokens",): (("m2", 1),),
    ("vectors",): (("t", 2), ("m1", 2), ("m2", 2)),
}


class Sizes:
    def __init__(self, chans, seqs, block, width, hidden):
        self.chans, self.seqs, self.block = chans, seqs, block
        self.width, self.hidden = width, hidden
        self.devices = chans * seqs
        self.y_n, self.z_n, self.x_n = chans // 2, seqs // 2, 2
        self.chips = self.devices // 2
        self.own = width // self.devices
        self.pair = 2 * self.own
        self.unit = hidden // self.devices
        self.cw = width // 2
        self.mw = 3 * self.cw
        self.hw = hidden // 2
        self.slab = 4 * self.own
        self.length = block * seqs
        self.tap = 3 * self.own
        self.blocks = {
            "mix": (self.pair, self.mw),
            "out": (self.pair, self.cw),
            "exp": (self.pair, self.hw),
            "shr": (self.unit, self.width),
        }
        third = self.cw // 3
        self.gathers = {
            "m": ("mix", self.cw, self.cw, self.cw),
            "g": ("mix", 0, 2 * third, third),
            "o": ("out", 0, third, 2 * third),
            "e": ("exp", 0, self.hw // 2, self.hw // 2),
            "s": ("shr", 0, 2 * third, 3 * third),
            "t": ("shr", 5 * third, third),
        }
        self.sums = {
            "s": ("shr", 0, 2 * third, 3 * third),
            "t": ("shr", 5 * third, third),
            "e": ("exp", 0, self.hw // 2, self.hw // 2),
            "o": ("out", 0, third, 2 * third),
            "m0": ("mix", 0, 2 * third, third),
            "m1": ("mix", self.cw, 2 * third, third),
            "m2": ("mix", 2 * self.cw, third, 2 * third),
        }


def tables(n):
    out = np.full((16, n.hw), -1, np.int32)
    p = np.arange(n.width)
    out[0, : n.width], out[1, : n.width] = p % n.own, p // n.own
    col = np.arange(n.mw)
    group, k = col // n.cw, col % n.cw
    chip, r = k // n.own, k % n.own
    for core in range(2):
        dev = (2 * (chip // n.seqs) + core) * n.seqs + chip % n.seqs
        e = group * n.width + n.own * dev + r
        out[2 + 2 * core, : n.mw], out[3 + 2 * core, : n.mw] = e % n.tap, e // n.tap
    col = np.arange(n.hw)
    chip, r = col // n.unit, col % n.unit
    out[6], out[7] = r, 2 * (chip // n.seqs) * n.seqs + chip % n.seqs
    chip, rest = p // n.pair, p % n.pair
    dev = (2 * (chip // n.seqs) + rest // n.own) * n.seqs + chip % n.seqs
    out[8, : n.width] = n.own * dev + rest % n.own
    return out


def encoding_table(length, bands, rows):
    positions = np.arange(length).astype(np.float32)
    frequency = np.linspace(0.0001, bands - 1, bands).astype(np.float32)
    angles = np.float32(2.0 * np.pi / length) * positions[:, None] * frequency[None, :]
    out = np.zeros((rows, length), np.float32)
    out[0] = positions / np.float32(length - 1)
    out[1 : 1 + bands] = np.cos(angles.astype(np.float64)).T
    out[1 + bands : 1 + 2 * bands] = -np.sin(angles.astype(np.float64)).T
    return out


INPUTS = (
    "tok", "cot", "i_gain1", "i_shift1", "i_mix", "i_mixb", "i_sw", "i_sb", "embw", "i_be", "i_fs", "inw", "i_bi",
    "i_ss", "i_filt", "i_rate", "i_skip", "i_out", "i_outb", "i_gain2", "i_shift2", "i_exp", "i_expb", "wshr",
    "i_shrb", "tabs", "enc",
)
OUTPUTS = ("bo", "tg", "gmix", "gexp", "gout", "gshr", "gsm", "fg", "gnet")
VECTORS = (
    "i_gain1", "i_shift1", "i_outb", "i_gain2", "i_shift2", "i_shrb", "i_mixb", None, None, None, "i_sb", "i_expb",
)


def scratch_list(n):
    v = pltpu.VMEM
    sem = pltpu.SemaphoreType.DMA
    rows = 4 * n.block
    half = 2 * n.block
    halo = 64
    slabs = (n.chips, n.slab, LANES)
    flat = (n.chips * n.slab, LANES)
    items = [
        ("xs", v((2, n.block, n.width), bf16)),
        ("gs", v((2, n.block, n.width), bf16)),
        ("ho", v((2, 16, n.width), bf16)),
        ("hs", v((2, 16, n.width), bf16)),
        ("pall", v((n.devices, 16, LANES), bf16)),
        ("pallf", v((n.devices * 16, LANES), f32)),
        ("wpre", v((n.pair, n.mw + n.hw), f32)),
        ("wrecv", v((n.own, n.mw + n.hw), f32)),
        ("pvf", v((16, LANES), f32)),
        ("pvec", v((16, LANES), bf16)),
        ("fvr", v((8, LANES), f32)),
        ("fvec", v((LANES, 8), f32)),
        ("fsel", v((n.own, LANES), f32)),
        ("pv", v((16, n.hw), f32)),
        ("r24", v((LANES, n.width), bf16)),
        ("r72", v((LANES, n.mw), bf16)),
        ("r96", v((LANES, n.hw), bf16)),
        ("d24", v((n.devices, n.width), f32)),
        ("d72", v((n.devices, n.mw), f32)),
        ("d96", v((n.devices, n.hw), f32)),
        ("perm", v((n.width, n.width), bf16)),
        ("n1p", v((rows + halo, n.width), bf16)),
        ("mixed", v((rows + halo, n.mw), bf16)),
        ("so", v((rows, n.mw), f32)),
        ("of", v(flat, f32)),
        ("gm", v(flat, f32)),
        ("uf", v(flat, f32)),
        ("gf", v(flat, f32)),
        ("toep", v((n.own, n.block, n.length), bf16)),
        ("u1", v((64, n.length), f32)),
        ("u2", v((64, n.length), f32)),
        ("l1", v((64, n.length), f32)),
        ("l2", v((LANES, n.length), f32)),
        ("c1", v((64, n.length), f32)),
        ("c2", v((64, n.length), f32)),
        ("imp", v((n.own, n.length), f32)),
        ("ig", v((n.own, n.length), f32)),
        ("w2o", v((n.cw, n.width), bf16)),
        ("low", v((rows, n.cw), bf16)),
        ("gated", v((rows, n.cw), bf16)),
        ("middle", v((rows, n.width), f32)),
        ("n2p", v((rows, n.width), bf16)),
        ("hid", v((rows, n.hw), bf16)),
        ("pre", v((rows, n.hw), bf16)),
        ("peo_s", v((rows, n.width), bf16)),
        ("peo_r", v((rows, n.width), bf16)),
        ("peb_s", v((half, n.width), bf16)),
        ("peb_r", v((half, n.width), bf16)),
        ("ped_r", v((rows, n.width), bf16)),
        ("pef_r", v((half, n.width), bf16)),
        ("acc", v((rows, n.width), f32)),
        ("branch", v((rows, n.width), bf16)),
        ("sg", v((rows, n.mw), f32)),
        ("nb_s", v((8, n.mw), f32)),
        ("nb_r", v((8, n.mw), f32)),
        ("mg", v((rows, n.mw), bf16)),
        ("msgs", v((n.devices * 16, LANES), f32)),
        ("rall", v((n.devices * 16, LANES), f32)),
        ("smf", v((8, LANES), f32)),
        ("msgf", v((n.devices * 8, LANES), f32)),
        ("rallf", v((n.devices * 8, LANES), f32)),
        ("fall", v((n.devices * 8, LANES), f32)),
        ("gv", v((16, n.hw), f32)),
    ]
    for k in range(4):
        items.append((f"sb{k}", v(slabs, bf16)))
        items.append((f"rb{k}", v(slabs, bf16)))
    for p in PIECES:
        r, c = n.blocks[p]
        items.append((f"w_{p}", v((n.chips, r, c), bf16)))
        if p != "exp":
            items.append((f"g_{p}", v((n.chips, r, c), bf16)))
        items.append((f"b_{p}", v((n.chips // 2, r, c), bf16)))
        items.append((f"a_{p}", v((n.chips // 4, r, c), bf16)))
        items.append((f"z_{p}", v((n.z_n - 1, r, c), bf16)))
    items += [
        ("ag_s", sem((2 * len(n.gathers),))),
        ("ag_r", sem((2 * len(n.gathers) * n.chips,))),
        ("rs_s", sem((6 * len(n.sums),))),
        ("rs_r", sem((6 * len(n.sums),))),
        ("ex_s", sem((28,))),
        ("ex_r", sem((28,))),
    ]
    return items


def fused_kernel(n, names, *refs):
    S = types.SimpleNamespace(**dict(zip(names, refs)))
    rows, half, blk = 4 * n.block, 2 * n.block, n.block
    S.tok_, S.cot_ = S.tok.at[:, 0], S.cot.at[:, 0]
    ch, seq = lax.axis_index("ch"), lax.axis_index("seq")
    y, core = lax.div(ch, 2), lax.rem(ch, 2)
    z, x = lax.div(seq, n.x_n), lax.rem(seq, n.x_n)
    me_dev = ch * n.seqs + seq
    other_ch = ch + 1 - 2 * core

    def chip(yy, zz, xx):
        return yy * n.seqs + zz * n.x_n + xx

    def slot(yy, zz, xx):
        return (zz * n.x_n + xx) * n.y_n + yy

    def at(yy, zz, xx):
        return (yy * 2 + core, zz * n.x_n + xx)

    me_chip, me_slot = chip(y, z, x), slot(y, z, x)
    sib = (other_ch, seq)

    def z_peer(j):
        peer = z
        bit = 1
        while bit <= j:
            if j & bit:
                peer = peer + bit * (1 - 2 * lax.rem(lax.div(z, bit), 2))
            bit *= 2
        return peer

    ends = []

    def send(src, dst, send_sem, recv_sem, target):
        pltpu.make_async_remote_copy(
            src_ref=src, dst_ref=dst, send_sem=send_sem, recv_sem=recv_sem,
            device_id=target, device_id_type=MESH,
        ).start()

    def wait(ref, sem):
        pltpu.make_async_copy(ref, ref, sem).wait()

    def later(ref, sem):
        ends.append((ref, sem))

    exchange_count = [0]

    def exchange(src, dst, target, free=False):
        k = exchange_count[0]
        exchange_count[0] += 1
        send(src, dst, S.ex_s.at[k], S.ex_r.at[k], target)
        if free:
            return lambda: wait(dst, S.ex_r.at[k]), lambda: wait(src, S.ex_s.at[k])
        later(src, S.ex_s.at[k])
        return lambda: wait(dst, S.ex_r.at[k])

    def to_others(src, dst, total):
        k = exchange_count[0]
        exchange_count[0] += 1
        for dc in range(n.chans):
            for ds in range(n.seqs):
                if dc or ds:
                    cc, ss = lax.rem(ch + dc, n.chans), lax.rem(seq + ds, n.seqs)
                    send(src(cc * n.seqs + ss), dst, S.ex_s.at[k], S.ex_r.at[k], (cc, ss))
        later(total, S.ex_s.at[k])
        return lambda: wait(total, S.ex_r.at[k])

    def to_chips(src, dst, total):
        k = exchange_count[0]
        exchange_count[0] += 1
        for dy in range(n.y_n):
            for dz in range(n.z_n):
                for dx in range(n.x_n):
                    if dy or dz or dx:
                        yy, zz, xx = lax.rem(y + dy, n.y_n), lax.rem(z + dz, n.z_n), lax.rem(x + dx, n.x_n)
                        send(src(yy, zz, xx), dst, S.ex_s.at[k], S.ex_r.at[k], at(yy, zz, xx))
        later(total, S.ex_s.at[k])
        return lambda: wait(total, S.ex_r.at[k])

    barrier = pltpu.get_barrier_semaphore()
    for dc in range(n.chans):
        for ds in range(n.seqs):
            if dc or ds:
                pl.semaphore_signal(
                    barrier, inc=1,
                    device_id=(lax.rem(ch + dc, n.chans), lax.rem(seq + ds, n.seqs)),
                    device_id_type=MESH,
                )
    theirs = pl.ds(pl.multiple_of((1 - core) * n.own, 8), n.own)
    ours = pl.ds(pl.multiple_of(core * n.own, 8), n.own)
    rows_mix, rows_exp = S.i_mix[...].astype(f32), S.i_exp[...].astype(f32)
    span, wide_span = n.cw // 2, n.hw // 2
    for k in range(2):
        to = slice(k * n.own, (k + 1) * n.own)
        for g in range(3):
            for yy in range(2):
                lo, src = g * n.cw + yy * span, g * n.width + (2 * yy + k) * span
                S.wpre[to, lo : lo + span] = rows_mix[:, src : src + span]
        for yy in range(2):
            lo, src = n.mw + yy * wide_span, (2 * yy + k) * wide_span
            S.wpre[to, lo : lo + wide_span] = rows_exp[:, src : src + wide_span]
    S.pvf[...] = jnp.zeros_like(S.pvf)
    for i, name in enumerate(VECTORS):
        if name:
            ref = getattr(S, name)
            size = ref.shape[0]
            S.pvf[i : i + 1, :size] = ref[...].astype(f32).reshape(1, size)
    S.pvf[7:10, : n.tap] = S.i_sw[...].astype(f32)
    S.pvec[...] = S.pvf[...].astype(bf16)
    S.w_shr[me_chip] = S.wshr[...]
    out_rows = S.i_out[...].astype(f32)
    S.w_out[me_chip] = jnp.concatenate([out_rows[:, : n.cw], out_rows[:, n.cw :]], axis=0).astype(bf16)

    def chosen(row, width):
        return S.tabs[row : row + 1, :width]

    def pick(row0, row1, width):
        return jnp.where(core == 0, chosen(row0, width), chosen(row1, width))

    def one_hot(height, index):
        return lax.broadcasted_iota(jnp.int32, (height, index.shape[1]), 0) == index

    S.r24[...] = one_hot(LANES, chosen(0, n.width)).astype(f32).astype(bf16)
    S.d24[...] = one_hot(n.devices, chosen(1, n.width)).astype(f32)
    S.r72[...] = one_hot(LANES, pick(2, 4, n.mw)).astype(f32).astype(bf16)
    S.d72[...] = one_hot(n.devices, pick(3, 5, n.mw)).astype(f32)

    pl.semaphore_wait(barrier, n.devices - 1)


    wait_pre, sent_pre = exchange(S.wpre.at[theirs], S.wrecv, sib, free=True)
    wait_xs = exchange(S.tok_, S.xs, sib)
    after = lax.rem(seq + 1, n.seqs)
    wait_ho = exchange(S.tok_.at[:, blk - 16 : blk, :], S.ho, (ch, after))
    wait_hs = exchange(S.tok_.at[:, blk - 16 : blk, :], S.hs, (other_ch, after))
    wait_params = to_others(
        lambda d: S.pvec, S.pall.at[me_dev], S.pall.at[pl.ds(0, n.devices - 1)]
    )
    wait_gs = exchange(S.cot_, S.gs, sib)
    S.pall[me_dev] = S.pvec[...]

    def flip(axis):
        return (1 - y, z, x) if axis == "y" else (y, z, 1 - x)

    far = (1 - y, z, 1 - x)

    class Line:
        def __init__(self, p, h):
            weight, start, *widths = n.gathers[p]
            self.buf = getattr(S, f"w_{weight}")
            self.cols = pl.ds(start + h * widths[0], widths[h])
            self.base = list(n.gathers).index(p) * 2 + h
            first, second = ("x", "y") if h == 0 else ("y", "x")
            self.first_dev, self.second_dev = at(*flip(first)), at(*flip(second))
            self.lead, self.side = flip(first), flip(second)

        def part(self, index):
            return self.buf.at[index, :, self.cols]

        def recv(self, k):
            return S.ag_r.at[self.base * n.chips + k]

        def push(self, index, k, target):
            send(self.part(index), self.part(index), S.ag_s.at[self.base], self.recv(k), target)

        def start_z(self):
            for j in range(1, n.z_n):
                self.push(me_chip, j, at(y, z_peer(j), x))

        def start_xy(self):
            self.push(me_chip, n.z_n, self.first_dev)
            self.push(me_chip, 2 * n.z_n, self.second_dev)

        def along(self, j):
            index = chip(y, z_peer(j), x)
            wait(self.part(index), self.recv(j))
            self.push(index, n.z_n + j, self.first_dev)
            self.push(index, 2 * n.z_n + j, self.second_dev)

        def across(self, j):
            index = chip(self.lead[0], z_peer(j), self.lead[2])
            wait(self.part(index), self.recv(n.z_n + j))
            self.push(index, 3 * n.z_n + j, self.second_dev)

        def finish(self):
            for j in range(n.z_n):
                wait(self.part(chip(self.side[0], z_peer(j), self.side[2])), self.recv(2 * n.z_n + j))
            for j in range(n.z_n):
                wait(self.part(chip(far[0], z_peer(j), far[2])), self.recv(3 * n.z_n + j))

        def sent(self):
            wait(self.buf.at[pl.ds(0, n.chips - 1), :, self.cols], S.ag_s.at[self.base])

    class Plane:
        def __init__(self, p):
            weight, start, width = n.gathers[p]
            self.buf = getattr(S, f"w_{weight}")
            self.cols = pl.ds(start, width)
            self.base = list(n.gathers).index(p) * 2
            self.x_dev, self.y_dev = at(*flip("x")), at(*flip("y"))
            self.x_chip, self.y_chip, self.far_chip = chip(*flip("x")), chip(*flip("y")), chip(*far)

        def part(self, index):
            return self.buf.at[index, :, self.cols]

        def recv(self, k):
            return S.ag_r.at[self.base * n.chips + k]

        def push(self, index, k, target):
            send(self.part(index), self.part(index), S.ag_s.at[self.base], self.recv(k), target)

        def start_xy(self):
            self.push(me_chip, 0, self.x_dev)
            self.push(me_chip, 1, self.y_dev)

        def corner(self):
            wait(self.part(self.x_chip), self.recv(0))
            self.push(self.x_chip, 2, self.y_dev)
            wait(self.part(self.y_chip), self.recv(1))

        def start_z(self):
            for j in range(1, n.z_n):
                self.push(me_chip, 3 + j, at(y, z_peer(j), x))
                self.push(self.x_chip, 2 + n.z_n + j, at(y, z_peer(j), x))
                self.push(self.y_chip, 1 + 2 * n.z_n + j, at(y, z_peer(j), x))

        def corner_z(self):
            wait(self.part(self.far_chip), self.recv(2))
            for j in range(1, n.z_n):
                self.push(self.far_chip, 3 * n.z_n + j, at(y, z_peer(j), x))

        def finish(self):
            for q, (yy, xx) in enumerate(((y, x), (y, 1 - x), (1 - y, x), (1 - y, 1 - x))):
                for j in range(1, n.z_n):
                    wait(self.part(chip(yy, z_peer(j), xx)), self.recv(3 - q + q * n.z_n + j))

        def sent(self):
            wait(self.part(pl.ds(0, n.chips - 1)), S.ag_s.at[self.base])

    gathers = {p: [Plane(p)] if p == "t" else [Line(p, 0), Line(p, 1)] for p in n.gathers}

    def gather(p, step, *args):
        for g in gathers[p]:
            getattr(g, step)(*args)

    gather("t", "start_xy")

    wait_pre()
    own_half, sib_half = S.wpre[ours, :], S.wrecv[...]
    slab = jnp.concatenate(
        [jnp.where(core == 0, own_half, sib_half), jnp.where(core == 0, sib_half, own_half)], axis=0
    ).astype(bf16)
    S.w_mix[me_chip] = slab[:, : n.mw]
    gather("m", "start_z")
    gather("m", "start_xy")
    S.w_exp[me_chip] = slab[:, n.mw :]

    todo = []

    def plan(p, step, *args):
        todo.extend(functools.partial(getattr(g, step), *args) for g in gathers[p])

    for p, then in (("m", "go"), ("go", "e"), ("e", "s"), ("s", "")):
        for j in range(1, n.z_n):
            for q in p:
                plan(q, "along", j)
        for q in then:
            plan(q, "start_z")
        if p == "m":
            plan("t", "corner")
        if p == "e":
            plan("t", "start_z")
            plan("t", "corner_z")
        for j in range(n.z_n):
            for q in p:
                plan(q, "across", j)
        for q in then:
            plan(q, "start_xy")
        if p == "m":
            mixer_steps = len(todo)
    plan_length = len(todo)

    def pump(count):
        for _ in range(min(count, len(todo))):
            todo.pop(0)()

    pump(2)
    S.perm[...] = one_hot(n.width, chosen(8, n.width)).astype(f32).astype(bf16)
    pump(2)
    wait_params()
    S.pallf[...] = S.pall[...].astype(f32).reshape(n.devices * 16, LANES)
    groups = [(range(0, 6), S.r24, S.d24), (range(6, 11), S.r72, S.d72), (range(11, 12), S.r96, S.d96)]

    def vectors_from_shards(members, right, mask):
        width = right.shape[1]
        for i in members:
            left = S.pallf[pl.ds(i, n.devices, stride=16), :].astype(bf16)
            S.pv[i : i + 1, :width] = jnp.sum(dot_nn(left, right[...]) * mask[...], axis=0, keepdims=True)

    vectors_from_shards(*groups[0])
    pump(2)

    def vector(i, lo=0, size=None):
        return S.pv[i : i + 1, lo : lo + (n.width if size is None else size)]

    hi = lax.Precision.HIGHEST

    def filter_setup():
        for i, ref in enumerate((S.i_be, S.i_fs, S.i_bi, S.i_ss)):
            S.fvr[i : i + 1, 0:64] = ref[...].reshape(1, 64)
        S.fvec[...] = jnp.transpose(S.fvr[...])
        last = [ref[...].reshape(1, n.width) for ref in (S.i_rate, S.i_skip)]
        last = jnp.concatenate(last + [jnp.zeros((6, n.width), f32)], axis=0)
        table = jnp.concatenate([S.i_filt[...], last], axis=0)
        first = lax.broadcasted_iota(jnp.int32, (n.own, n.width), 0) + me_dev * n.own
        mine = lax.broadcasted_iota(jnp.int32, (n.own, n.width), 1) == first
        S.fsel[:, : 72] = dot_nt(jnp.where(mine, 1.0, 0.0), table, hi)

    def filter_first():
        u = dot_tn(S.embw[...], S.enc[0 : S.embw.shape[0]], hi) + S.fvec[0:64, 0:1]
        S.u1[...] = u
        s, c = sin_cos(u * S.fvec[0:64, 1:2])
        S.l1[...] = s
        S.c1[...] = c

    def filter_second():
        u = dot_tn(S.inw[...], S.l1[...], hi) + S.fvec[0:64, 2:3]
        S.u2[...] = u
        s, c = sin_cos(u * S.fvec[0:64, 3:4])
        S.l2[0:64] = s
        row = lax.broadcasted_iota(jnp.int32, (LANES - 64, n.length), 0)
        col = lax.broadcasted_iota(jnp.int32, (LANES - 64, n.length), 1)
        S.l2[64:LANES] = jnp.where((row == 0) & (col == 0), 1.0, 0.0)
        S.c2[...] = c

    def decay():
        time = lax.broadcasted_iota(jnp.int32, (n.own, n.length), 1).astype(f32)
        return jnp.exp(-S.fsel[:, 64:65] * time)

    def filter_third():
        S.imp[...] = dot_nn(S.fsel[:, 0:64], S.l2[0:64], hi) * decay()

    def toeplitz(r):
        line = S.imp[pl.ds(r, 1), :]
        line = jnp.concatenate([jnp.zeros((1, LANES), f32), line], axis=1)
        wide = jnp.broadcast_to(line, (blk, LANES + n.length))
        S.toep[r] = pltpu.roll(wide, 0, 1, stride=1, stride_axis=0)[:, LANES:].astype(bf16)

    def norm_rows(values, gain, shift):
        unit, _ = normalise(values.astype(f32))
        low = (unit * vector(gain) + vector(shift)).astype(bf16)
        return dot_nn(low, S.perm[...]).astype(bf16)

    S.n1p[0:half] = norm_rows(S.tok_[...].reshape(half, n.width), 0, 1)
    pump(2)
    wait_xs()
    S.n1p[half:rows] = norm_rows(S.xs[...].reshape(half, n.width), 0, 1)
    pump(2)
    wait_ho()
    wait_hs()
    S.n1p[rows : rows + 32] = norm_rows(S.ho[...].reshape(32, n.width), 0, 1)
    S.n1p[rows + 32 : rows + 64] = norm_rows(S.hs[...].reshape(32, n.width), 0, 1)
    pump(4)

    pump(mixer_steps - (plan_length - len(todo)))
    vectors_from_shards(*groups[1])
    gather("m", "finish")
    pump(4)

    def project(g):
        lo = g * n.cw
        weight = S.w_mix[:, :, lo : lo + n.cw].reshape(n.width, n.cw)
        for r0, r1 in ((0, half), (half, rows + 64)):
            S.mixed[r0:r1, lo : lo + n.cw] = (
                dot_nn(S.n1p[r0:r1], weight) + vector(6, lo, n.cw)
            ).astype(bf16)
    first_block = seq == 0
    last_block = seq == n.seqs - 1

    def shifted(s, lo):
        own = S.mixed[s * blk : (s + 1) * blk, lo : lo + n.cw].astype(f32)
        before = S.mixed[rows + 16 * s : rows + 16 * (s + 1), lo : lo + n.cw].astype(f32)
        before = jnp.where(first_block, jnp.zeros_like(before), before)
        both = jnp.concatenate([before, own], axis=0)
        return own, pltpu.roll(both, 1, 0)[16:], pltpu.roll(both, 2, 0)[16:]

    def short_forward(g):
        lo = g * n.cw
        for s in range(4):
            now, one, two = shifted(s, lo)
            S.so[s * blk : (s + 1) * blk, lo : lo + n.cw] = (
                vector(7, lo, n.cw) * two + vector(8, lo, n.cw) * one
                + vector(9, lo, n.cw) * now + vector(10, lo, n.cw)
            )

    for g in (1, 2):
        project(g)
        short_forward(g)

    def token_rows(s):
        return slice(s * blk, (s + 1) * blk)

    def gate(s, g):
        return S.so[token_rows(s), g * n.cw : (g + 1) * n.cw]

    def to_channels(k, make):
        out, into = getattr(S, f"sb{k}"), getattr(S, f"rb{k}")
        for s in range(4):
            turned = jnp.transpose(make(s))
            for m in range(n.chips):
                row = m * n.slab + s * n.own
                S.of[row : row + n.own, :] = turned[m * n.own : (m + 1) * n.own]
        out[...] = S.of[...].astype(bf16).reshape(n.chips, n.slab, LANES)
        arrived = to_chips(
            lambda yy, zz, xx: out.at[chip(yy, zz, xx)], into.at[me_slot], into.at[pl.ds(0, n.chips - 1)]
        )
        into[me_slot] = out[me_chip]
        return arrived

    def to_tokens(k):
        out, into = getattr(S, f"sb{k}"), getattr(S, f"rb{k}")
        out[...] = S.of[...].astype(bf16).reshape(n.chips, n.slab, LANES)
        arrived = to_chips(
            lambda yy, zz, xx: out.at[slot(yy, zz, xx)], into.at[me_chip], into.at[pl.ds(0, n.chips - 1)]
        )
        into[me_chip] = out[me_slot]
        return arrived

    def token_view(k, s):
        got = getattr(S, f"rb{k}")[...].astype(f32)
        return jnp.transpose(got[:, s * n.own : (s + 1) * n.own, :].reshape(n.cw, LANES))

    wait_u = to_channels(0, lambda s: gate(s, 1) * gate(s, 2))
    third = n.own // 3
    pump(14)
    filter_setup()
    filter_first()
    filter_second()
    filter_third()
    S.r96[...] = one_hot(LANES, chosen(6, n.hw)).astype(f32).astype(bf16)
    S.d96[...] = one_hot(n.devices, chosen(7, n.hw) + core * n.seqs).astype(f32)
    vectors_from_shards(*groups[2])
    for q in range(3):
        lax.fori_loop(q * third, (q + 1) * third, lambda r, carry: (toeplitz(r), carry)[1], 0)
    pump(12)
    wait_u()

    group = n.y_n * 4
    lines = n.seqs * group
    S.uf[...] = S.rb0[...].astype(f32).reshape(n.chips * n.slab, LANES)

    def channel_rows(ref, r):
        return ref[pl.ds(r, lines, stride=n.own), :]

    def conv_forward(r, carry):
        own = channel_rows(S.uf, r)
        wide = dot_nn(own.astype(bf16), S.toep[r])
        blocks = []
        for i in range(n.seqs):
            total = wide[group * i : group * (i + 1), 0:LANES]
            for k in range(1, i + 1):
                total = total + wide[group * (i - k) : group * (i - k + 1), LANES * k : LANES * (k + 1)]
            blocks.append(total)
        result = jnp.concatenate(blocks, axis=0) + S.fsel[pl.ds(r, 1), 65:66] * own
        S.of[pl.ds(r, lines, stride=n.own), :] = result
        return carry

    for q in range(3):
        lax.fori_loop(q * third, (q + 1) * third, conv_forward, 0)
        pump(3)
    wait_low = to_tokens(1)
    pump(100)
    gather("g", "finish")
    project(0)
    short_forward(0)
    gather("o", "finish")
    slabs = S.w_out[...].astype(f32)
    S.w2o[:, : n.cw] = slabs[:, : n.own, :].reshape(n.cw, n.cw).astype(bf16)
    S.w2o[:, n.cw :] = slabs[:, n.own :, :].reshape(n.cw, n.cw).astype(bf16)
    wait_low()

    for s in range(4):
        low = token_view(1, s)
        S.low[token_rows(s)] = low.astype(bf16)
        S.gated[token_rows(s)] = (gate(s, 0) * low).astype(bf16)
    waits = []
    for part in (1, 0):
        r = slice(part * half, (part + 1) * half)
        o = slice((1 - part) * half, (2 - part) * half)
        S.acc[r] = dot_nn(S.gated[r], S.w2o[...])
        S.peo_s[r] = S.acc[r].astype(bf16)
        waits.append(exchange(S.peo_s.at[r], S.peo_r.at[o], sib, free=True))
    wait_gs()

    def tokens_of(part):
        return (S.tok_ if part == 0 else S.xs)[...].reshape(half, n.width).astype(f32)

    def cot_of(part):
        return (S.cot_ if part == 0 else S.gs)[...].reshape(half, n.width)

    for arrived, sent in waits:
        arrived()
        sent()
    for part in range(2):
        r = slice(part * half, (part + 1) * half)
        S.middle[r] = tokens_of(part) + (S.acc[r] + S.peo_r[r].astype(f32)) + vector(2)
        S.n2p[r] = norm_rows(S.middle[r], 3, 4)

    for p in "est":
        gather(p, "finish")
    chunk = n.hw // 4
    units = chunk // n.unit
    for q in range(4):
        lo = q * chunk
        weight = S.w_exp[:, :, lo : lo + chunk].reshape(n.width, chunk)
        shrink = S.w_shr[q * units : (q + 1) * units].reshape(chunk, n.width)
        total = jnp.zeros((1, chunk), f32)
        for part in range(2):
            r = slice(part * half, (part + 1) * half)
            v = dot_nn(S.n2p[r], weight) + vector(11, lo, chunk)
            back = dot_nt(cot_of(part), shrink)
            phi = 0.5 + 0.5 * lax.erf(v * np.float32(1.0 / np.sqrt(2.0)))
            slope = phi + v * (np.float32(1.0 / np.sqrt(2.0 * np.pi)) * jnp.exp(-0.5 * v * v))
            S.hid[r, lo : lo + chunk] = (v * phi).astype(bf16)
            pre = (back * slope).astype(bf16)
            S.pre[r, lo : lo + chunk] = pre
            total = total + jnp.sum(pre.astype(f32), axis=0, keepdims=True)
        S.gv[11:12, lo : lo + chunk] = total
    waits = []
    for part in (1, 0):
        r = slice(part * half, (part + 1) * half)
        o = slice((1 - part) * half, (2 - part) * half)
        S.acc[r] = dot_nt(S.pre[r], S.w_exp[...].reshape(n.width, n.hw))
        S.peo_s[r] = S.acc[r].astype(bf16)
        waits.append(exchange(S.peo_s.at[r], S.ped_r.at[o], sib))

    def gradient(weight):
        return S.w_exp if weight == "exp" else getattr(S, f"g_{weight}")

    def add_into(ref, index, cols, *terms):
        total = ref[index, :, cols].astype(f32)
        for term in terms:
            total = total + term.astype(f32)
        ref[index, :, cols] = total.astype(bf16)

    def scatter_line(p, h):
        weight, start, *widths = n.sums[p]
        grads, cols = gradient(weight), pl.ds(start + h * widths[0], widths[h])
        from_b, from_a, from_z = (getattr(S, f"{k}_{weight}") for k in "baz")
        base = list(n.sums).index(p) * 6 + h * 3
        second, first = ("y", "x") if h == 0 else ("x", "y")
        second_dev, first_dev = at(*flip(second)), at(*flip(first))

        def side(i):
            if second == "y":
                return y * n.seqs + i
            return chip(lax.div(i, n.z_n), lax.rem(i, n.z_n), x)

        def boxed(ref):
            return ref.reshape(n.y_n, n.z_n, n.x_n, *ref.shape[1:])

        def start_b():
            if second == "y":
                src, dst = grads.at[pl.ds((1 - y) * n.seqs, n.seqs), :, cols], from_b.at[:, :, cols]
            else:
                src = boxed(grads).at[:, :, 1 - x, :, cols]
                dst = from_b.reshape(n.y_n, n.z_n, *from_b.shape[1:]).at[:, :, :, cols]
            send(src, dst, S.rs_s.at[base], S.rs_r.at[base], second_dev)
            later(from_b.at[:, :, cols], S.rs_s.at[base])

        def end_b():
            wait(from_b.at[:, :, cols], S.rs_r.at[base])

            def add(i, carry):
                add_into(grads, side(i), cols, from_b[i, :, cols])
                return carry

            lax.fori_loop(0, n.chips // 2, add, 0)
            yy, xx = (y, 1 - x) if first == "x" else (1 - y, x)
            send(boxed(grads).at[yy, :, xx, :, cols], from_a.at[:, :, cols], S.rs_s.at[base + 1], S.rs_r.at[base + 1], first_dev)
            later(from_a.at[:, :, cols], S.rs_s.at[base + 1])

        def end_a():
            wait(from_a.at[:, :, cols], S.rs_r.at[base + 1])

            def add(zz, carry):
                add_into(grads, chip(y, zz, x), cols, from_a[zz, :, cols])
                return carry

            lax.fori_loop(0, n.z_n, add, 0)
            for j in range(1, n.z_n):
                send(
                    grads.at[chip(y, z_peer(j), x), :, cols], from_z.at[j - 1, :, cols],
                    S.rs_s.at[base + 2], S.rs_r.at[base + 2], at(y, z_peer(j), x),
                )
            later(from_z.at[:, :, cols], S.rs_s.at[base + 2])

        def end_z():
            wait(from_z.at[:, :, cols], S.rs_r.at[base + 2])
            total = grads[me_chip, :, cols].astype(f32)
            for j in range(n.z_n - 1):
                total = total + from_z[j, :, cols].astype(f32)
            return total

        return start_b, end_b, end_a, end_z

    def scatter_plane(p):
        weight, start, width = n.sums[p]
        grads, full = gradient(weight), pl.ds(start, width)
        eight, four, three = (getattr(S, f"{k}_{weight}") for k in "baz")
        base = list(n.sums).index(p) * 6
        plane = ((y, x), (y, 1 - x), (1 - y, x), (1 - y, 1 - x))
        x_dev, y_dev = at(*flip("x")), at(*flip("y"))
        x_chip, y_chip, far_chip = chip(*flip("x")), chip(*flip("y")), chip(*far)

        def landing(q, j):
            k = q * (n.z_n - 1) + j - 1
            many = n.chips // 2
            return (eight, k, 0) if k < many else (four, k - many, 1)

        def start_z():
            for q, (yy, xx) in enumerate(plane):
                for j in range(1, n.z_n):
                    ref, k, which = landing(q, j)
                    send(
                        grads.at[chip(yy, z_peer(j), xx), :, full], ref.at[k, :, full],
                        S.rs_s.at[base + which], S.rs_r.at[base + which], at(y, z_peer(j), x),
                    )
            later(eight.at[:, :, full], S.rs_s.at[base])
            later(four.at[:, :, full], S.rs_s.at[base + 1])

        def end_z():
            wait(eight.at[:, :, full], S.rs_r.at[base])
            wait(four.at[:, :, full], S.rs_r.at[base + 1])
            for q, (yy, xx) in enumerate(plane):
                terms = []
                for j in range(1, n.z_n):
                    ref, k, _ = landing(q, j)
                    terms.append(ref[k, :, full])
                add_into(grads, chip(yy, z, xx), full, *terms)
            send(grads.at[far_chip, :, full], three.at[0, :, full], S.rs_s.at[base + 2], S.rs_r.at[base + 2], x_dev)
            later(three.at[0, :, full], S.rs_s.at[base + 2])

        def end_corner():
            wait(three.at[0, :, full], S.rs_r.at[base + 2])
            add_into(grads, y_chip, full, three[0, :, full])
            for k, index, target in ((1, y_chip, y_dev), (2, x_chip, x_dev)):
                send(grads.at[index, :, full], three.at[k, :, full], S.rs_s.at[base + 3 + k], S.rs_r.at[base + 3 + k], target)
                later(three.at[k, :, full], S.rs_s.at[base + 3 + k])

        def end_xy():
            total = grads[me_chip, :, full].astype(f32)
            for k in (1, 2):
                wait(three.at[k, :, full], S.rs_r.at[base + 3 + k])
                total = total + three[k, :, full].astype(f32)
            return total

        return start_z, end_z, end_corner, end_xy

    scatters = {p: [scatter_plane(p)] if p == "t" else [scatter_line(p, h) for h in range(2)] for p in n.sums}

    def scatter(p, stage):
        return [s[stage]() for s in scatters[p]]

    def steps(*place):
        for p, stage in STEPS.get(place, ()):
            scatter(p, stage)

    all_cot = jnp.concatenate([cot_of(0), cot_of(1)], axis=0)
    for q in range(4):
        lo = q * chunk
        S.g_shr[q * units : (q + 1) * units] = (
            dot_tn(S.hid[:, lo : lo + chunk], all_cot).astype(bf16).reshape(units, n.unit, n.width)
        )
    steps("shrink")
    S.gv[5:6, : n.width] = jnp.sum(cot_of(0).astype(f32), axis=0, keepdims=True)
    for w in waits:
        w()

    for part in range(2):
        r = slice(part * half, (part + 1) * half)
        grad = dot_nt((S.acc[r] + S.ped_r[r].astype(f32)).astype(bf16), S.perm[...])
        unit, scale = normalise(S.middle[r])
        if part == 0:
            S.gv[3:4, : n.width] = jnp.sum(grad * unit, axis=0, keepdims=True)
            S.gv[4:5, : n.width] = jnp.sum(grad, axis=0, keepdims=True)
        total = cot_of(part).astype(f32) + norm_back(unit, scale, grad * vector(3))
        S.acc[r] = total
        S.branch[r] = total.astype(bf16)

    for s in range(4):
        S.sg[token_rows(s), : n.cw] = dot_nt(S.branch[token_rows(s)], S.w2o[...])
    wait_g = to_channels(2, lambda s: S.sg[token_rows(s), : n.cw] * gate(s, 0))
    for s in range(4):
        S.sg[token_rows(s), : n.cw] = S.sg[token_rows(s), : n.cw] * S.low[token_rows(s)].astype(f32)

    def send_heads(lo, width):
        head_row = lax.broadcasted_iota(jnp.int32, (8, width), 0)
        heads = jnp.zeros((8, width), f32)
        for s in range(4):
            top = S.sg[s * blk : s * blk + 8, lo : lo + width]
            heads = heads + jnp.where(lax.div(head_row, 2) == s, pltpu.roll(top, 2 * s, 0) if s else top, 0.0)
        cols = pl.ds(lo, width)
        S.nb_s[:, cols] = heads
        return exchange(S.nb_s.at[:, cols], S.nb_r.at[:, cols], (ch, lax.rem(seq + n.seqs - 1, n.seqs)))

    def tap_sums(g):
        lo = g * n.cw
        sums = [jnp.zeros((1, n.cw), f32) for _ in range(4)]
        for s in range(4):
            grad = S.sg[token_rows(s), lo : lo + n.cw]
            now, one, two = shifted(s, lo)
            for i, term in enumerate((grad * two, grad * one, grad * now, grad)):
                sums[i] = sums[i] + jnp.sum(term, axis=0, keepdims=True)
        for i in range(4):
            S.gv[7 + i : 8 + i, lo : lo + n.cw] = sums[i]

    def mixed_back(g):
        lo = g * n.cw
        total = jnp.zeros((1, n.cw), f32)
        nexts = S.nb_r[:, lo : lo + n.cw]
        nexts = jnp.where(last_block, jnp.zeros_like(nexts), nexts)
        for s in range(4):
            grad = S.sg[token_rows(s), lo : lo + n.cw]
            tail = pltpu.roll(nexts, 8 - 2 * s, 0) if s else nexts
            both = jnp.concatenate([grad, tail], axis=0)
            low = (
                vector(9, lo, n.cw) * grad
                + vector(8, lo, n.cw) * pltpu.roll(both, blk + 7, 0)[:blk]
                + vector(7, lo, n.cw) * pltpu.roll(both, blk + 6, 0)[:blk]
            ).astype(bf16)
            S.mg[token_rows(s), lo : lo + n.cw] = low
            total = total + jnp.sum(low.astype(f32), axis=0, keepdims=True)
        S.gv[6:7, lo : lo + n.cw] = total
        S.g_mix[:, :, lo : lo + n.cw] = (
            dot_tn(S.n1p[0:rows], S.mg[:, lo : lo + n.cw]).astype(bf16).reshape(n.chips, n.pair, n.cw)
        )

    S.msgs[...] = jnp.zeros_like(S.msgs)

    def pack(members, right, mask):
        width = right.shape[1]
        value = jnp.concatenate([S.gv[i : i + 1, :width] * mask[...] for i in members], axis=0)
        shards = dot_two(dot_nt, value, right[...])
        for k, i in enumerate(members):
            S.msgs[pl.ds(i, n.devices, stride=16), :] = shards[k * n.devices : (k + 1) * n.devices]

    wait_nb = send_heads(0, n.cw)
    steps("heads")
    S.gv[2:3, : n.width] = jnp.sum(S.branch[0:half].astype(f32), axis=0, keepdims=True)
    gather("e", "sent")
    for q in range(4):
        lo = q * chunk
        S.w_exp[:, :, lo : lo + chunk] = (
            dot_tn(S.n2p[...], S.pre[:, lo : lo + chunk]).astype(bf16).reshape(n.chips, n.pair, chunk)
        )

    steps("expand")

    for part in (1, 0):
        r = slice(part * half, (part + 1) * half)
        value = dot_nn(S.hid[r], S.w_shr[...].reshape(n.hw, n.width))
        if part:
            S.peb_s[...] = value.astype(bf16)
            wait_bo, sent_bo = exchange(S.peb_s, S.peb_r, sib, free=True)
        else:
            S.middle[r] = S.middle[r] + value + vector(5)
    outs = dot_tn(S.gated[...], S.branch[...]).reshape(n.chips, n.own, n.width)
    S.g_out[...] = jnp.concatenate([outs[:, :, : n.cw], outs[:, :, n.cw :]], axis=1).astype(bf16)
    steps("output")
    tap_sums(0)
    wait_nb()
    mixed_back(0)
    steps("mixer", 0)
    pack((2, 3, 4, 5), S.r24, S.d24)
    pack((11,), S.r96, S.d96)
    wait_bo()
    sent_bo()
    S.bo[...] = (S.middle[0:half] + S.peb_r[...].astype(f32)).astype(bf16).reshape(2, blk, n.width)
    steps("before", "grad")
    wait_g()
    steps("after", "grad")

    flat = lax.broadcasted_iota(jnp.int32, (blk, blk), 0) + lax.broadcasted_iota(jnp.int32, (blk, blk), 1)
    mirror = jnp.where(flat == blk - 1, 1.0, 0.0).astype(bf16)
    S.gf[...] = S.rb2[...].astype(f32).reshape(n.chips * n.slab, LANES)
    S.gm[...] = dot_nn(S.rb2[...].reshape(n.chips * n.slab, LANES), mirror)
    S.uf[...] = dot_nn(S.rb0[...].reshape(n.chips * n.slab, LANES), mirror)

    def conv_back(r, carry):
        turned = channel_rows(S.gm, r)
        wide = dot_nn(turned.astype(bf16), S.toep[r])
        blocks = []
        for i in range(n.seqs):
            total = wide[group * i : group * (i + 1), 0:LANES]
            for k in range(1, n.seqs - i):
                total = total + wide[group * (i + k) : group * (i + k + 1), LANES * k : LANES * (k + 1)]
            blocks.append(total)
        back = jnp.concatenate(blocks, axis=0) + S.fsel[pl.ds(r, 1), 65:66] * turned
        S.of[pl.ds(r, lines, stride=n.own), :] = dot_nn(back.astype(bf16), mirror)
        grad = channel_rows(S.gf, r)
        steps = [grad]
        for k in range(1, n.seqs):
            steps.append(
                jnp.concatenate([grad[group * k :], jnp.zeros((group * k, LANES), f32)], axis=0)
            )
        ahead = jnp.concatenate(steps, axis=1).astype(bf16)
        outer = dot_tn(channel_rows(S.uf, r).astype(bf16), ahead)
        outer = jnp.concatenate([jnp.zeros((blk, LANES), f32), outer], axis=1)
        outer = pltpu.roll(outer, n.length + 1, 1, stride=1, stride_axis=0)
        S.ig[pl.ds(r, 1), :] = jnp.sum(outer, axis=0, keepdims=True)[:, LANES:]
        return carry

    for q in range(3):
        lax.fori_loop(q * third, (q + 1) * third, conv_back, 0)
        if q == 2:
            wait_in = to_tokens(3)
        steps("conv_back", q)

    d_line = S.ig[...] * decay()
    fg_rows = pl.ds(pl.multiple_of(me_dev * n.own, 8), n.own)
    S.fg[fg_rows, :] = dot_two(dot_nt, d_line, S.l2[...])
    wait_fg = to_chips(lambda yy, zz, xx: S.fg.at[fg_rows], S.fg.at[fg_rows], S.fg.at[pl.ds(0, (n.chips - 1) * n.own)])
    steps("filter")
    top, low = split_two(d_line)
    wide_filter = S.fsel[:, 0:64].astype(bf16)
    d_l2 = (dot_tn(wide_filter, top) + dot_tn(wide_filter, low)) * S.c2[...]
    d_u2 = d_l2 * S.fvec[0:64, 3:4]
    top, low = split_two(d_u2)
    inner = S.inw[...].astype(bf16)
    d_l1 = (dot_nn(inner, top) + dot_nn(inner, low)) * S.c1[...]
    d_u1 = d_l1 * S.fvec[0:64, 1:2]
    l1, enc = S.l1[...].astype(bf16), S.enc[...].astype(bf16)
    net = jnp.concatenate([dot_nt(top, l1) + dot_nt(low, l1), dot_two(dot_nt, d_u1, enc)], axis=1)
    net_lane = lax.broadcasted_iota(jnp.int32, (64, LANES), 1)
    for i, term in enumerate((d_u1, d_l1 * S.u1[...], d_u2, d_l2 * S.u2[...])):
        net = jnp.where(net_lane == LANES - 8 + i, jnp.sum(term, axis=1, keepdims=True), net)
    S.msgf[...] = jnp.zeros_like(S.msgf)
    S.msgf[pl.ds(0, n.devices, stride=8), :] = net[0 : n.devices]
    S.msgf[pl.ds(1, n.devices, stride=8), :] = net[n.devices :]

    def eight(d):
        return pl.ds(pl.multiple_of(d * 8, 8), 8)

    wait_msgf = to_others(
        lambda d: S.msgf.at[eight(d)], S.rallf.at[eight(me_dev)], S.rallf.at[pl.ds(0, (n.devices - 1) * 8)]
    )
    S.rallf[eight(me_dev), :] = S.msgf[eight(me_dev), :]
    steps("before", "input")
    wait_in()

    for s in range(4):
        grad = token_view(3, s)
        S.sg[token_rows(s), n.cw : 2 * n.cw] = grad * gate(s, 2)
        S.sg[token_rows(s), 2 * n.cw :] = grad * gate(s, 1)
    wait_nb = send_heads(n.cw, 2 * n.cw)
    wait_msgf()
    S.smf[...] = jnp.sum(S.rallf[...].reshape(n.devices, 8, LANES), axis=0)
    wait_net = to_others(lambda d: S.smf, S.fall.at[eight(me_dev)], S.fall.at[pl.ds(0, (n.devices - 1) * 8)])
    S.fall[eight(me_dev), :] = S.smf[...]
    wait_fg()
    sib_waits = []
    for yy in range(n.y_n):
        span = pl.ds(pl.multiple_of((yy * 2 + core) * n.seqs * n.own, 8), n.seqs * n.own)
        sib_span = pl.ds(pl.multiple_of((yy * 2 + 1 - core) * n.seqs * n.own, 8), n.seqs * n.own)
        k = exchange_count[0]
        exchange_count[0] += 1
        send(S.fg.at[span], S.fg.at[span], S.ex_s.at[k], S.ex_r.at[k], sib)
        later(S.fg.at[span], S.ex_s.at[k])
        sib_waits.append((sib_span, k))
    steps("next", "heads")
    tap_sums(1)
    tap_sums(2)
    wait_nb()
    mixed_back(1)
    steps("mixer", 1)
    mixed_back(2)
    steps("mixer", 2)
    weight = S.w_mix[...].reshape(n.width, n.mw)
    S.peb_s[...] = dot_nt(S.mg[half:rows], weight).astype(bf16)
    wait_f = exchange(S.peb_s, S.pef_r, sib)
    pack(range(6, 11), S.r72, S.d72)
    mine = dot_nt(S.mg[0:half], weight)
    steps("first", "norm")
    wait_f()
    grad = dot_nt((mine + S.pef_r[...].astype(f32)).astype(bf16), S.perm[...])
    unit, scale = normalise(tokens_of(0))
    S.gv[0:1, : n.width] = jnp.sum(grad * unit, axis=0, keepdims=True)
    S.gv[1:2, : n.width] = jnp.sum(grad, axis=0, keepdims=True)
    S.tg[...] = (S.acc[0:half] + norm_back(unit, scale, grad * vector(0))).astype(bf16).reshape(2, blk, n.width)

    steps("tokens")

    pack((0, 1), S.r24, S.d24)

    def message(d):
        return pl.ds(pl.multiple_of(d * 16, 16), 16)

    wait_msgs = to_others(
        lambda d: S.msgs.at[message(d)], S.rall.at[message(me_dev)], S.rall.at[pl.ds(0, (n.devices - 1) * 16)]
    )
    S.rall[message(me_dev), :] = S.msgs[message(me_dev), :]
    steps("vectors")

    wait_msgs()
    S.gsm[...] = jnp.sum(S.rall[...].reshape(n.devices, 16, LANES), axis=0)
    sent_pre()

    def finish(p, ref, at_col):
        lo = at_col
        for value in scatter(p, 3):
            ref[:, lo : lo + value.shape[1]] = value
            lo += value.shape[1]

    finish("s", S.gshr, 0)
    finish("t", S.gshr, n.sums["t"][1])
    both = jnp.concatenate(scatter("o", 3), axis=1)
    S.gout[:, : n.cw], S.gout[:, n.cw :] = both[: n.own], both[n.own :]
    finish("e", S.wpre, n.mw)
    finish("m0", S.wpre, 0)
    for span, k in sib_waits:
        wait(S.fg.at[span], S.ex_r.at[k])
    finish("m1", S.wpre, n.cw)
    finish("m2", S.wpre, 2 * n.cw)
    wait_fin = exchange(S.wpre.at[theirs], S.wrecv, sib)
    S.gmix[core] = S.wpre[ours, : n.mw]
    S.gexp[core] = S.wpre[ours, n.mw :]
    wait_net()
    S.gnet[0 : n.devices] = S.fall[pl.ds(0, n.devices, stride=8), :]
    S.gnet[n.devices :] = S.fall[pl.ds(1, n.devices, stride=8), :]
    wait_fin()
    S.gmix[1 - core] = S.wrecv[:, : n.mw]
    S.gexp[1 - core] = S.wrecv[:, n.mw :]
    for p in "mgost":
        gather(p, "sent")
    for ref, sem in ends:
        wait(ref, sem)


def emit_kernel(n, emb, bo, tg, gmix, gexp, gout, gshr, gsm, fg, gnet, *outs):
    (o_bo, o_tg, o_g1, o_s1, o_mix, o_mixb, o_sw, o_sb, o_embw, o_be, o_fs, o_inw, o_bi, o_ss, o_fw, o_lb, o_out,
     o_outb, o_g2, o_s2, o_exp, o_expb, o_shr, o_shrb) = outs
    o_bo[:, 0], o_tg[:, 0] = bo[...], tg[...]
    span, wide_span = n.cw // 2, n.hw // 2
    for k in range(2):
        for yy in range(2):
            for g in range(3):
                lo, dst = g * n.cw + yy * span, g * n.width + (2 * yy + k) * span
                o_mix[:, dst : dst + span] = gmix[k, :, lo : lo + span]
            lo, dst = yy * wide_span, (2 * yy + k) * wide_span
            o_exp[:, dst : dst + wide_span] = gexp[k, :, lo : lo + wide_span]
    o_out[...], o_shr[...] = gout[...], gshr[...]
    for i, ref in ((0, o_g1), (1, o_s1), (2, o_outb), (3, o_g2), (4, o_s2), (5, o_shrb), (6, o_mixb), (10, o_sb), (11, o_expb)):
        size = ref.shape[0]
        ref[...] = gsm[i : i + 1, :size].reshape(size)
    o_sw[...] = gsm[7:10, : n.tap]
    net = jnp.transpose(gnet[...])
    o_inw[...] = net[0:64]
    o_embw[...] = net[64 : 64 + emb]
    for i, ref in enumerate((o_be, o_fs, o_bi, o_ss)):
        ref[...] = net[LANES - 8 + i : LANES - 7 + i].reshape(64)
    filt = jnp.transpose(fg[...])
    o_fw[...] = filt[0:64]
    o_lb[...] = filt[64:65].reshape(n.width)


def fused(n, *args):
    emb = args[8].shape[0]
    tables_in = (jnp.asarray(tables(n)), jnp.asarray(encoding_table(n.length, (emb - 1) // 2, 64)))
    shape = jax.ShapeDtypeStruct
    outs = (
        shape((2, n.block, n.width), bf16), shape((2, n.block, n.width), bf16),
        shape((2, n.own, n.mw), f32), shape((2, n.own, n.hw), f32), shape((n.own, n.width), f32),
        shape((n.unit, n.width), f32), shape((16, LANES), f32), shape((n.width, LANES), f32),
        shape((64, LANES), f32),
    )
    scratch = scratch_list(n)
    names = INPUTS + OUTPUTS + tuple(name for name, _ in scratch)
    vmem = pl.BlockSpec(memory_space=pltpu.VMEM)
    results = pl.pallas_call(
        functools.partial(fused_kernel, n, names),
        out_shape=outs,
        in_specs=[vmem] * len(INPUTS),
        out_specs=[vmem] * len(outs),
        scratch_shapes=[s for _, s in scratch],
        compiler_params=pltpu.CompilerParams(
            collective_id=0, has_side_effects=True, vmem_limit_bytes=63 << 20
        ),
    )(*args, *tables_in)
    like = args[:1] * 2 + args[2:15] + args[16:]
    final = tuple(shape(a.shape, f32 if i > 1 else bf16) for i, a in enumerate(like))
    return pl.pallas_call(
        functools.partial(emit_kernel, n, emb),
        out_shape=final,
        in_specs=[vmem] * len(outs),
        out_specs=[vmem] * len(final),
        compiler_params=pltpu.CompilerParams(vmem_limit_bytes=63 << 20),
    )(*results)


highest = lax.Precision.HIGHEST


def from_behind(block, axis, distance):
    devices = range(lax.axis_size(axis))
    route = [(i - distance, i) for i in devices if i - distance in devices]
    return lax.ppermute(block, axis, route)


def matmul(left, right):
    return jnp.dot(left, right, precision=highest, preferred_element_type=jnp.float32)


def layer_norm(values, gain, shift):
    centre = values - jnp.mean(values, axis=-1, keepdims=True)
    spread = jnp.mean(centre * centre, axis=-1, keepdims=True)
    return centre * lax.rsqrt(spread + 1e-05) * gain + shift


def exact_gelu(values):
    return jax.nn.gelu(values, approximate=False)


def filter_values(
    seq_length,
    embed_matrix,
    embed_offset,
    sine_first,
    inner_matrix,
    inner_offset,
    sine_second,
    head_matrix,
    rates,
):
    positions = jnp.arange(seq_length).astype(jnp.float32)
    band_count = (embed_matrix.shape[0] - 1) // 2
    frequency = jnp.linspace(0.0001, band_count - 1, band_count).astype(jnp.float32)
    angles = 2.0 * jnp.pi / seq_length * positions[:, None] * frequency[None, :]
    encoded = jnp.concatenate(
        [positions[:, None] / (seq_length - 1), jnp.cos(angles), -jnp.sin(angles)], axis=1
    )
    layer_first = jnp.sin(sine_first * (matmul(encoded, embed_matrix) + embed_offset))
    layer_second = jnp.sin(sine_second * (matmul(layer_first, inner_matrix) + inner_offset))
    return matmul(layer_second, head_matrix) * jnp.exp(-rates[None, :] * positions[:, None])


def spectral_tables(block_rows):
    period = 2 * block_rows
    freq_rows = jnp.arange(block_rows + 1)
    sample_cols = jnp.arange(period)
    phase = (freq_rows[:, None] * sample_cols[None, :] % period).astype(jnp.float32) * (
        2.0 * jnp.pi / period
    )
    forward_full = jnp.concatenate([jnp.cos(phase), -jnp.sin(phase)], axis=0)
    out_times = jnp.arange(block_rows) + block_rows
    out_phase = (out_times[:, None] * freq_rows[None, :] % period).astype(jnp.float32) * (
        2.0 * jnp.pi / period
    )
    edge = (freq_rows == 0) | (freq_rows == block_rows)
    factor = jnp.where(edge, 1.0, 2.0).astype(jnp.float32) / period
    inverse_table = jnp.concatenate(
        [factor[None, :] * jnp.cos(out_phase), -factor[None, :] * jnp.sin(out_phase)], axis=1
    )
    return (forward_full, inverse_table)


def spec_product(filt, spectrum):
    return jnp.stack(
        [
            filt[0] * spectrum[0] - filt[1] * spectrum[1],
            filt[0] * spectrum[1] + filt[1] * spectrum[0],
        ]
    )


def spec_adjoint(filt, grad_spec):
    return jnp.stack(
        [
            filt[0] * grad_spec[0] + filt[1] * grad_spec[1],
            filt[0] * grad_spec[1] - filt[1] * grad_spec[0],
        ]
    )


def contract_rows(left, right):
    return lax.dot_general(
        left, right, (((0,), (0,)), ((), ())), preferred_element_type=jnp.float32
    )


def contract_cols(left, right):
    return lax.dot_general(
        left, right, (((1,), (1,)), ((), ())), preferred_element_type=jnp.float32
    )


def on_device(
    tokens,
    cotangent,
    first_gain,
    first_shift,
    mixer_weight,
    mixer_bias,
    short_weight,
    short_bias,
    embed_weight,
    embed_bias,
    first_sine,
    inner_weight,
    inner_bias,
    second_sine,
    filter_weight,
    decay_rate,
    long_bias,
    output_weight,
    output_bias,
    second_gain,
    second_shift,
    expand_weight,
    expand_bias,
    shrink_weight,
    shrink_bias,
):
    chan_count = lax.axis_size("ch")
    seq_count = lax.axis_size("seq")
    chan_index = lax.axis_index("ch")
    seq_index = lax.axis_index("seq")
    block_rows = tokens.shape[2]
    width = tokens.shape[3]
    span_width = width // chan_count
    seq_length = block_rows * seq_count
    freq_count = block_rows + 1
    gathered = (
        lax.all_gather(first_gain, ("ch", "seq"), axis=0, tiled=True),
        lax.all_gather(first_shift, ("ch", "seq"), axis=0, tiled=True),
        lax.all_gather(mixer_weight, ("ch", "seq"), axis=0, tiled=True),
        lax.all_gather(mixer_bias, ("ch", "seq"), axis=0, tiled=True),
        lax.all_gather(short_weight, ("ch", "seq"), axis=1, tiled=True),
        lax.all_gather(short_bias, ("ch", "seq"), axis=0, tiled=True),
        lax.all_gather(output_weight, ("ch", "seq"), axis=0, tiled=True),
        lax.all_gather(output_bias, ("ch", "seq"), axis=0, tiled=True),
        lax.all_gather(second_gain, ("ch", "seq"), axis=0, tiled=True),
        lax.all_gather(second_shift, ("ch", "seq"), axis=0, tiled=True),
        lax.all_gather(expand_weight, ("ch", "seq"), axis=0, tiled=True),
        lax.all_gather(expand_bias, ("ch", "seq"), axis=0, tiled=True),
        lax.all_gather(shrink_weight, ("ch", "seq"), axis=0, tiled=True),
        lax.all_gather(shrink_bias, ("ch", "seq"), axis=0, tiled=True),
    )
    (
        gain_one,
        shift_one,
        mix_matrix,
        mix_offset,
        short_taps,
        short_offset,
        out_matrix,
        out_offset,
        gain_two,
        shift_two,
        expand_matrix,
        expand_offset,
        shrink_matrix,
        shrink_offset,
    ) = gathered
    gain_one_f = gain_one.astype(jnp.float32)
    shift_one_f = shift_one.astype(jnp.float32)
    mix_offset_f = mix_offset.astype(jnp.float32)
    taps_f = short_taps.astype(jnp.float32)
    short_offset_f = short_offset.astype(jnp.float32)
    out_offset_f = out_offset.astype(jnp.float32)
    gain_two_f = gain_two.astype(jnp.float32)
    shift_two_f = shift_two.astype(jnp.float32)
    expand_offset_f = expand_offset.astype(jnp.float32)
    shrink_offset_f = shrink_offset.astype(jnp.float32)

    def local_filter(params):
        (
            embed_matrix,
            embed_offset,
            sine_a,
            inner_matrix,
            inner_offset,
            sine_b,
            head_matrix,
            skip_gain,
        ) = params
        head_slice = lax.dynamic_slice_in_dim(head_matrix, chan_index * span_width, span_width, 1)
        rate_slice = lax.dynamic_slice_in_dim(decay_rate, chan_index * span_width, span_width, 0)
        skip_slice = lax.dynamic_slice_in_dim(skip_gain, chan_index * span_width, span_width, 0)
        impulse_part = filter_values(
            seq_length,
            embed_matrix,
            embed_offset,
            sine_a,
            inner_matrix,
            inner_offset,
            sine_b,
            head_slice,
            rate_slice,
        )
        return (impulse_part, skip_slice)

    filter_params = (
        embed_weight,
        embed_bias,
        first_sine,
        inner_weight,
        inner_bias,
        second_sine,
        filter_weight,
        long_bias,
    )
    (impulse, skip_part), filter_back = jax.vjp(local_filter, filter_params)
    skip_tiled = jnp.tile(skip_part, chan_count)
    forward_full, inverse_table = spectral_tables(block_rows)
    forward_half = forward_full[:, :block_rows]
    inverse_adjoint = inverse_table.T
    impulse_blocks = impulse.reshape(seq_count, block_rows, span_width)
    earlier = jnp.concatenate([jnp.zeros_like(impulse_blocks[:1]), impulse_blocks[:-1]], axis=0)
    segments = jnp.concatenate([earlier, impulse_blocks], axis=1)
    filt_spec = jnp.einsum("fm,nmc->nfc", forward_full, segments, precision=highest)
    filt_spec = filt_spec.reshape(seq_count, 2, freq_count, 1, span_width)
    zero_spec = jnp.zeros((2 * freq_count, width), jnp.float32)

    def contribution(spectrum, source):
        distance = seq_index - source
        causal = (distance >= 0).astype(jnp.float32)
        slot_index = jnp.clip(distance, 0, seq_count - 1)
        filt = lax.dynamic_index_in_dim(filt_spec, slot_index, 0, keepdims=False)
        shaped = spectrum.reshape(2, freq_count, chan_count, span_width)
        return causal * spec_product(filt, shaped).reshape(2 * freq_count, width)

    def micro_step(carry, inputs):
        grads, filt_grad, skip_grad = carry
        block_in, block_cot = inputs
        resid = block_in.astype(jnp.float32)
        normed_one, norm_back_one = jax.vjp(layer_norm, resid, gain_one_f, shift_one_f)
        normed_low = normed_one.astype(jnp.bfloat16)
        mixed = (
            jnp.dot(normed_low, mix_matrix, preferred_element_type=jnp.float32) + mix_offset_f
        ).astype(jnp.bfloat16)
        before = from_behind(mixed[block_rows - 2 :], "seq", 1)
        padded = jnp.concatenate([before, mixed], axis=0).astype(jnp.float32)
        short_out = (
            taps_f[0] * padded[:-2]
            + taps_f[1] * padded[1:-1]
            + taps_f[2] * padded[2:]
            + short_offset_f
        )
        gate_out = short_out[:, :width]
        gate_in = short_out[:, width : 2 * width]
        values = short_out[:, 2 * width :]
        product = (gate_in * values).astype(jnp.bfloat16)
        channel_view = lax.all_to_all(
            product.reshape(block_rows, chan_count, span_width),
            "ch",
            split_axis=1,
            concat_axis=1,
            tiled=True,
        ).reshape(block_rows, width)
        own_float = channel_view.astype(jnp.float32)
        own_spec = matmul(forward_half, own_float)
        shard_piece = lax.all_gather(channel_view[None], "seq", axis=0, tiled=True)

        def add_single(offset, partial_value):
            spectrum = matmul(forward_half, shard_piece[offset].astype(jnp.float32))
            return partial_value + contribution(spectrum, offset)

        summed = lax.fori_loop(0, shard_piece.shape[0], add_single, zero_spec)
        long_out = matmul(inverse_table, summed) + skip_tiled * own_float
        long_low = long_out.astype(jnp.bfloat16)
        token_view = lax.all_to_all(
            long_low.reshape(block_rows, chan_count, span_width),
            "ch",
            split_axis=1,
            concat_axis=1,
            tiled=True,
        ).reshape(block_rows, width)
        token_float = token_view.astype(jnp.float32)
        gated_out = (gate_out * token_float).astype(jnp.bfloat16)
        middle = (
            resid
            + jnp.dot(gated_out, out_matrix, preferred_element_type=jnp.float32)
            + out_offset_f
        )
        normed_two, norm_back_two = jax.vjp(layer_norm, middle, gain_two_f, shift_two_f)
        normed_two_low = normed_two.astype(jnp.bfloat16)
        hidden_pre = (
            jnp.dot(normed_two_low, expand_matrix, preferred_element_type=jnp.float32)
            + expand_offset_f
        )
        hidden_act, gelu_back = jax.vjp(exact_gelu, hidden_pre)
        hidden_low = hidden_act.astype(jnp.bfloat16)
        result = (
            middle
            + jnp.dot(hidden_low, shrink_matrix, preferred_element_type=jnp.float32)
            + shrink_offset_f
        )
        block_result = result.astype(jnp.bfloat16)
        grad_out = block_cot.astype(jnp.float32)
        shrink_grad = contract_rows(hidden_low, block_cot)
        shrink_off_grad = jnp.sum(grad_out, axis=0)
        hidden_grad = contract_cols(block_cot, shrink_matrix)
        pre_grad = gelu_back(hidden_grad)[0].astype(jnp.bfloat16)
        expand_grad = contract_rows(normed_two_low, pre_grad)
        expand_off_grad = jnp.sum(pre_grad.astype(jnp.float32), axis=0)
        normed_two_grad = contract_cols(pre_grad, expand_matrix)
        middle_ln_grad, gain_two_grad, shift_two_grad = norm_back_two(normed_two_grad)
        middle_grad = grad_out + middle_ln_grad
        branch_low = middle_grad.astype(jnp.bfloat16)
        out_grad = contract_rows(gated_out, branch_low)
        out_off_grad = jnp.sum(branch_low.astype(jnp.float32), axis=0)
        gated_grad = contract_cols(branch_low, out_matrix)
        gate_out_grad = gated_grad * token_float
        token_grad = (gated_grad * gate_out).astype(jnp.bfloat16)
        channel_grad = lax.all_to_all(
            token_grad.reshape(block_rows, chan_count, span_width),
            "ch",
            split_axis=1,
            concat_axis=1,
            tiled=True,
        ).reshape(block_rows, width)
        channel_grad_f = channel_grad.astype(jnp.float32)
        own_shaped = own_spec.reshape(2, freq_count, chan_count, span_width)

        def back_term(running, grad_spec, target):
            spec_acc, filt_acc = running
            distance = target - seq_index
            causal = (distance >= 0).astype(jnp.float32)
            slot_index = jnp.clip(distance, 0, seq_count - 1)
            filt = lax.dynamic_index_in_dim(filt_spec, slot_index, 0, keepdims=False)
            shaped = grad_spec.reshape(2, freq_count, chan_count, span_width)
            spec_acc = spec_acc + causal * spec_adjoint(filt, shaped).reshape(2 * freq_count, width)
            filt_term = causal * jnp.sum(spec_adjoint(own_shaped, shaped), axis=2, keepdims=True)
            current = lax.dynamic_index_in_dim(filt_acc, slot_index, 0, keepdims=True)
            filt_acc = lax.dynamic_update_index_in_dim(
                filt_acc, current + filt_term[None], slot_index, 0
            )
            return (spec_acc, filt_acc)

        back_shard_piece = lax.all_gather(channel_grad[None], "seq", axis=0, tiled=True)

        def back_single(offset, partial_value):
            grad_spec = matmul(inverse_adjoint, back_shard_piece[offset].astype(jnp.float32))
            return back_term(partial_value, grad_spec, offset)

        spec_grad, filt_grad = lax.fori_loop(
            0, back_shard_piece.shape[0], back_single, (zero_spec, filt_grad)
        )
        input_grad = (
            lax.dot_general(
                forward_half,
                spec_grad,
                (((0,), (0,)), ((), ())),
                precision=highest,
                preferred_element_type=jnp.float32,
            )
            + skip_tiled * channel_grad_f
        )
        skip_grad = skip_grad + jnp.sum(
            (channel_grad_f * own_float).reshape(block_rows, chan_count, span_width), axis=(0, 1)
        )
        input_low = input_grad.astype(jnp.bfloat16)
        token_input = (
            lax.all_to_all(
                input_low.reshape(block_rows, chan_count, span_width),
                "ch",
                split_axis=1,
                concat_axis=1,
                tiled=True,
            )
            .reshape(block_rows, width)
            .astype(jnp.float32)
        )
        short_grad = jnp.concatenate(
            [gate_out_grad, token_input * values, token_input * gate_in], axis=1
        )
        short_off_grad = jnp.sum(short_grad, axis=0)
        taps_grad = jnp.stack(
            [
                jnp.sum(short_grad * padded[:-2], axis=0),
                jnp.sum(short_grad * padded[1:-1], axis=0),
                jnp.sum(short_grad * padded[2:], axis=0),
            ]
        )
        padded_grad = (
            jnp.pad(taps_f[0] * short_grad, ((0, 2), (0, 0)))
            + jnp.pad(taps_f[1] * short_grad, ((1, 1), (0, 0)))
            + jnp.pad(taps_f[2] * short_grad, ((2, 0), (0, 0)))
        )
        after = from_behind(padded_grad[:2], "seq", -1)
        mixed_grad = padded_grad[2:] + jnp.concatenate(
            [jnp.zeros((block_rows - 2, 3 * width), jnp.float32), after], axis=0
        )
        mixed_low = mixed_grad.astype(jnp.bfloat16)
        mix_grad = contract_rows(normed_low, mixed_low)
        mix_off_grad = jnp.sum(mixed_low.astype(jnp.float32), axis=0)
        normed_one_grad = contract_cols(mixed_low, mix_matrix)
        resid_ln_grad, gain_one_grad, shift_one_grad = norm_back_one(normed_one_grad)
        tokens_grad = (middle_grad + resid_ln_grad).astype(jnp.bfloat16)
        step_grads = (
            gain_one_grad,
            shift_one_grad,
            mix_grad,
            mix_off_grad,
            taps_grad,
            short_off_grad,
            out_grad,
            out_off_grad,
            gain_two_grad,
            shift_two_grad,
            expand_grad,
            expand_off_grad,
            shrink_grad,
            shrink_off_grad,
        )
        grads = jax.tree.map(lambda left, right: left + right, grads, step_grads)
        return ((grads, filt_grad, skip_grad), (block_result, tokens_grad))

    zero_grads = tuple((jnp.zeros(item.shape, jnp.float32) for item in gathered))
    init = (zero_grads, jnp.zeros_like(filt_spec), jnp.zeros((span_width,), jnp.float32))
    (grads, filt_grad, skip_grad), (results, token_grads) = lax.scan(
        micro_step, init, (tokens[:, 0], cotangent[:, 0])
    )
    shards = (
        lax.psum_scatter(grads[0], ("ch", "seq"), scatter_dimension=0, tiled=True),
        lax.psum_scatter(grads[1], ("ch", "seq"), scatter_dimension=0, tiled=True),
        lax.psum_scatter(grads[2], ("ch", "seq"), scatter_dimension=0, tiled=True),
        lax.psum_scatter(grads[3], ("ch", "seq"), scatter_dimension=0, tiled=True),
        lax.psum_scatter(grads[4], ("ch", "seq"), scatter_dimension=1, tiled=True),
        lax.psum_scatter(grads[5], ("ch", "seq"), scatter_dimension=0, tiled=True),
        lax.psum_scatter(grads[6], ("ch", "seq"), scatter_dimension=0, tiled=True),
        lax.psum_scatter(grads[7], ("ch", "seq"), scatter_dimension=0, tiled=True),
        lax.psum_scatter(grads[8], ("ch", "seq"), scatter_dimension=0, tiled=True),
        lax.psum_scatter(grads[9], ("ch", "seq"), scatter_dimension=0, tiled=True),
        lax.psum_scatter(grads[10], ("ch", "seq"), scatter_dimension=0, tiled=True),
        lax.psum_scatter(grads[11], ("ch", "seq"), scatter_dimension=0, tiled=True),
        lax.psum_scatter(grads[12], ("ch", "seq"), scatter_dimension=0, tiled=True),
        lax.psum_scatter(grads[13], ("ch", "seq"), scatter_dimension=0, tiled=True),
    )
    segment_grad = jnp.einsum(
        "fm,nfc->nmc",
        forward_full,
        filt_grad.reshape(seq_count, 2 * freq_count, span_width),
        precision=highest,
    )
    impulse_grad = segment_grad[:, block_rows:] + jnp.concatenate(
        [segment_grad[1:, :block_rows], jnp.zeros((1, block_rows, span_width), jnp.float32)], axis=0
    )
    local_grads = filter_back((impulse_grad.reshape(seq_length, span_width), skip_grad))[0]
    summed_filter = lax.psum(local_grads, ("ch", "seq"))
    return (
        results[:, None],
        token_grads[:, None],
        shards[0],
        shards[1],
        shards[2],
        shards[3],
        shards[4],
        shards[5],
        summed_filter[0],
        summed_filter[1],
        summed_filter[2],
        summed_filter[3],
        summed_filter[4],
        summed_filter[5],
        summed_filter[6],
        summed_filter[7],
        shards[6],
        shards[7],
        shards[8],
        shards[9],
        shards[10],
        shards[11],
        shards[12],
        shards[13],
    )


def block(*args):
    tokens, expand_weight = args[0], args[21]
    n = Sizes(
        lax.axis_size("ch"), lax.axis_size("seq"), tokens.shape[2], tokens.shape[3], expand_weight.shape[1]
    )
    if n.own % 8 == 0 and n.pair % 16 == 0 and n.unit % 16 == 0 and n.block == LANES:
        return fused(n, *args)
    return on_device(*args)


def solution(mesh):
    return jax.shard_map(
        block,
        mesh=mesh,
        in_specs=(
            P(None, "ch", "seq", None),
            P(None, "ch", "seq", None),
            P(("ch", "seq")),
            P(("ch", "seq")),
            P(("ch", "seq"), None),
            P(("ch", "seq")),
            P(None, ("ch", "seq")),
            P(("ch", "seq")),
            P(),
            P(),
            P(),
            P(),
            P(),
            P(),
            P(),
            P(),
            P(),
            P(("ch", "seq"), None),
            P(("ch", "seq")),
            P(("ch", "seq")),
            P(("ch", "seq")),
            P(("ch", "seq"), None),
            P(("ch", "seq")),
            P(("ch", "seq"), None),
            P(("ch", "seq")),
        ),
        out_specs=(
            P(None, "ch", "seq", None),
            P(None, "ch", "seq", None),
            P(("ch", "seq")),
            P(("ch", "seq")),
            P(("ch", "seq"), None),
            P(("ch", "seq")),
            P(None, ("ch", "seq")),
            P(("ch", "seq")),
            P(),
            P(),
            P(),
            P(),
            P(),
            P(),
            P(),
            P(),
            P(("ch", "seq"), None),
            P(("ch", "seq")),
            P(("ch", "seq")),
            P(("ch", "seq")),
            P(("ch", "seq"), None),
            P(("ch", "seq")),
            P(("ch", "seq"), None),
            P(("ch", "seq")),
        ),
        check_vma=False,
    )
```

```python
import functools
import types

import jax
import jax.numpy as jnp
import numpy as np
from jax import lax
from jax.experimental import pallas as pl
from jax.experimental.pallas import tpu as pltpu
from jax.sharding import PartitionSpec as P


MESH = pl.DeviceIdType.MESH
f32 = jnp.float32
bf16 = jnp.bfloat16
LANES = 128
PIECES = ("mix", "out", "exp", "shr")


def dot_nn(left, right, precision=None):
    return lax.dot_general(
        left, right, (((1,), (0,)), ((), ())), precision=precision, preferred_element_type=f32
    )


def dot_nt(left, right, precision=None):
    return lax.dot_general(
        left, right, (((1,), (1,)), ((), ())), precision=precision, preferred_element_type=f32
    )


def dot_tn(left, right, precision=None):
    return lax.dot_general(
        left, right, (((0,), (0,)), ((), ())), precision=precision, preferred_element_type=f32
    )


def normalise(values):
    centre = values - jnp.mean(values, axis=-1, keepdims=True)
    scale = lax.rsqrt(jnp.mean(centre * centre, axis=-1, keepdims=True) + 1e-05)
    return centre * scale, scale


def norm_back(unit, scale, grad):
    inner = grad - jnp.mean(grad, axis=-1, keepdims=True)
    return scale * (inner - unit * jnp.mean(grad * unit, axis=-1, keepdims=True))


def sin_cos(angle):
    turns = jnp.floor(angle * (1.0 / np.pi) + 0.5)
    rest = angle - turns * 3.140625
    rest = rest - turns * 9.670257568359375e-4
    rest = rest - turns * 6.2771141529083251953e-7
    rest = rest - turns * 1.21644916362129151821e-10
    sign = 1.0 - 2.0 * (turns - 2.0 * jnp.floor(turns * 0.5))
    sq = rest * rest
    low = sq * (1.0 / 362880.0 - sq * (1.0 / 39916800.0 - sq * (1.0 / 6227020800.0)))
    sine = rest * (1.0 - sq * (1.0 / 6.0 - sq * (1.0 / 120.0 - sq * (1.0 / 5040.0 - low))))
    high = sq * (1.0 / 3628800.0 - sq * (1.0 / 479001600.0 - sq * (1.0 / 87178291200.0)))
    cosine = 1.0 - sq * (0.5 - sq * (1.0 / 24.0 - sq * (1.0 / 720.0 - sq * (1.0 / 40320.0 - high))))
    return sign * sine, sign * cosine


def split_two(value):
    top = value.astype(bf16)
    return top, (value - top.astype(f32)).astype(bf16)


def dot_two(dot, left, right):
    top, low = split_two(left)
    right = right.astype(bf16)
    return dot(top, right) + dot(low, right)


STEPS = {
    ("shrink",): (("s", 0),),
    ("expand",): (("s", 1), ("e", 0)),
    ("after", "grad"): (("t", 0),),
    ("conv_back", 0): (("s", 2),),
    ("conv_back", 1): (("o", 0), ("m0", 0)),
    ("conv_back", 2): (("e", 1),),
    ("before", "input"): (("e", 2), ("o", 1), ("m0", 1)),
    ("mixer", 1): (("m1", 0),),
    ("mixer", 2): (("m2", 0), ("o", 2), ("m0", 2), ("t", 1)),
    ("first", "norm"): (("m1", 1),),
    ("tokens",): (("m2", 1),),
    ("vectors",): (("t", 2), ("m1", 2), ("m2", 2)),
}


class Sizes:
    def __init__(self, chans, seqs, block, width, hidden):
        self.chans, self.seqs, self.block = chans, seqs, block
        self.width, self.hidden = width, hidden
        self.devices = chans * seqs
        self.y_n, self.z_n, self.x_n = chans // 2, seqs // 2, 2
        self.chips = self.devices // 2
        self.own = width // self.devices
        self.pair = 2 * self.own
        self.unit = hidden // self.devices
        self.cw = width // 2
        self.mw = 3 * self.cw
        self.hw = hidden // 2
        self.slab = 4 * self.own
        self.length = block * seqs
        self.tap = 3 * self.own
        self.blocks = {
            "mix": (self.pair, self.mw),
            "out": (self.pair, self.cw),
            "exp": (self.pair, self.hw),
            "shr": (self.unit, self.width),
        }
        third = self.cw // 3
        self.gathers = {
            "m": ("mix", self.cw, self.cw, self.cw),
            "g": ("mix", 0, 2 * third, third),
            "o": ("out", 0, third, 2 * third),
            "e": ("exp", 0, self.hw // 2, self.hw // 2),
            "s": ("shr", 0, 2 * third, 3 * third),
            "t": ("shr", 5 * third, third),
        }
        self.sums = {
            "s": ("shr", 0, 2 * third, 3 * third),
            "t": ("shr", 5 * third, third),
            "e": ("exp", 0, self.hw // 2, self.hw // 2),
            "o": ("out", 0, third, 2 * third),
            "m0": ("mix", 0, 2 * third, third),
            "m1": ("mix", self.cw, 2 * third, third),
            "m2": ("mix", 2 * self.cw, third, 2 * third),
        }


def tables(n):
    out = np.full((16, n.hw), -1, np.int32)
    p = np.arange(n.width)
    out[0, : n.width], out[1, : n.width] = p % n.own, p // n.own
    col = np.arange(n.mw)
    group, k = col // n.cw, col % n.cw
    chip, r = k // n.own, k % n.own
    for core in range(2):
        dev = (2 * (chip // n.seqs) + core) * n.seqs + chip % n.seqs
        e = group * n.width + n.own * dev + r
        out[2 + 2 * core, : n.mw], out[3 + 2 * core, : n.mw] = e % n.tap, e // n.tap
    col = np.arange(n.hw)
    chip, r = col // n.unit, col % n.unit
    out[6], out[7] = r, 2 * (chip // n.seqs) * n.seqs + chip % n.seqs
    chip, rest = p // n.pair, p % n.pair
    dev = (2 * (chip // n.seqs) + rest // n.own) * n.seqs + chip % n.seqs
    out[8, : n.width] = n.own * dev + rest % n.own
    return out


def encoding_table(length, bands, rows):
    positions = np.arange(length).astype(np.float32)
    frequency = np.linspace(0.0001, bands - 1, bands).astype(np.float32)
    angles = np.float32(2.0 * np.pi / length) * positions[:, None] * frequency[None, :]
    out = np.zeros((rows, length), np.float32)
    out[0] = positions / np.float32(length - 1)
    out[1 : 1 + bands] = np.cos(angles.astype(np.float64)).T
    out[1 + bands : 1 + 2 * bands] = -np.sin(angles.astype(np.float64)).T
    return out


INPUTS = (
    "tok", "cot", "i_gain1", "i_shift1", "i_mix", "i_mixb", "i_sw", "i_sb", "embw", "i_be", "i_fs", "inw", "i_bi",
    "i_ss", "i_filt", "i_rate", "i_skip", "i_out", "i_outb", "i_gain2", "i_shift2", "i_exp", "i_expb", "wshr",
    "i_shrb", "tabs", "enc",
)
OUTPUTS = ("bo", "tg", "gmix", "gexp", "gout", "gshr", "gsm", "fg", "gnet")
VECTORS = (
    "i_gain1", "i_shift1", "i_outb", "i_gain2", "i_shift2", "i_shrb", "i_mixb", None, None, None, "i_sb", "i_expb",
)


def scratch_list(n):
    v = pltpu.VMEM
    sem = pltpu.SemaphoreType.DMA
    rows = 4 * n.block
    half = 2 * n.block
    halo = 64
    slabs = (n.chips, n.slab, LANES)
    flat = (n.chips * n.slab, LANES)
    items = [
        ("xs", v((2, n.block, n.width), bf16)),
        ("gs", v((2, n.block, n.width), bf16)),
        ("ho", v((2, 16, n.width), bf16)),
        ("hs", v((2, 16, n.width), bf16)),
        ("pall", v((n.devices, 16, LANES), bf16)),
        ("pallf", v((n.devices * 16, LANES), f32)),
        ("wpre", v((n.pair, n.mw + n.hw), f32)),
        ("wrecv", v((n.own, n.mw + n.hw), f32)),
        ("pvf", v((16, LANES), f32)),
        ("pvec", v((16, LANES), bf16)),
        ("fvr", v((8, LANES), f32)),
        ("fvec", v((LANES, 8), f32)),
        ("fsel", v((n.own, LANES), f32)),
        ("pv", v((16, n.hw), f32)),
        ("r24", v((LANES, n.width), bf16)),
        ("r72", v((LANES, n.mw), bf16)),
        ("r96", v((LANES, n.hw), bf16)),
        ("d24", v((n.devices, n.width), f32)),
        ("d72", v((n.devices, n.mw), f32)),
        ("d96", v((n.devices, n.hw), f32)),
        ("perm", v((n.width, n.width), bf16)),
        ("n1p", v((rows + halo, n.width), bf16)),
        ("mixed", v((rows + halo, n.mw), bf16)),
        ("so", v((rows, n.mw), f32)),
        ("of", v(flat, f32)),
        ("gm", v(flat, f32)),
        ("uf", v(flat, f32)),
        ("gf", v(flat, f32)),
        ("toep", v((n.own, n.block, n.length), bf16)),
        ("u1", v((64, n.length), f32)),
        ("u2", v((64, n.length), f32)),
        ("l1", v((64, n.length), f32)),
        ("l2", v((LANES, n.length), f32)),
        ("c1", v((64, n.length), f32)),
        ("c2", v((64, n.length), f32)),
        ("imp", v((n.own, n.length), f32)),
        ("ig", v((n.own, n.length), f32)),
        ("w2o", v((n.cw, n.width), bf16)),
        ("low", v((rows, n.cw), bf16)),
        ("gated", v((rows, n.cw), bf16)),
        ("middle", v((rows, n.width), f32)),
        ("n2p", v((rows, n.width), bf16)),
        ("hid", v((rows, n.hw), bf16)),
        ("pre", v((rows, n.hw), bf16)),
        ("peo_s", v((rows, n.width), bf16)),
        ("peo_r", v((rows, n.width), bf16)),
        ("peb_s", v((half, n.width), bf16)),
        ("peb_r", v((half, n.width), bf16)),
        ("ped_r", v((rows, n.width), bf16)),
        ("pef_r", v((half, n.width), bf16)),
        ("acc", v((rows, n.width), f32)),
        ("branch", v((rows, n.width), bf16)),
        ("sg", v((rows, n.mw), f32)),
        ("nb_s", v((8, n.mw), f32)),
        ("nb_r", v((8, n.mw), f32)),
        ("mg", v((rows, n.mw), bf16)),
        ("msgs", v((n.devices * 16, LANES), f32)),
        ("rall", v((n.devices * 16, LANES), f32)),
        ("smf", v((8, LANES), f32)),
        ("msgf", v((n.devices * 8, LANES), f32)),
        ("rallf", v((n.devices * 8, LANES), f32)),
        ("fall", v((n.devices * 8, LANES), f32)),
        ("gv", v((16, n.hw), f32)),
    ]
    for k in range(4):
        items.append((f"sb{k}", v(slabs, bf16)))
        items.append((f"rb{k}", v(slabs, bf16)))
    for p in PIECES:
        r, c = n.blocks[p]
        items.append((f"w_{p}", v((n.chips, r, c), bf16)))
        if p != "exp":
            items.append((f"g_{p}", v((n.chips, r, c), bf16)))
        items.append((f"b_{p}", v((n.chips // 2, r, c), bf16)))
        items.append((f"a_{p}", v((n.chips // 4, r, c), bf16)))
        items.append((f"z_{p}", v((n.z_n - 1, r, c), bf16)))
    items += [
        ("ag_s", sem((2 * len(n.gathers),))),
        ("ag_r", sem((2 * len(n.gathers) * n.chips,))),
        ("rs_s", sem((6 * len(n.sums),))),
        ("rs_r", sem((6 * len(n.sums),))),
        ("ex_s", sem((28,))),
        ("ex_r", sem((28,))),
    ]
    return items


def fused_kernel(n, names, *refs):
    S = types.SimpleNamespace(**dict(zip(names, refs)))
    rows, half, blk = 4 * n.block, 2 * n.block, n.block
    S.tok_, S.cot_ = S.tok.at[:, 0], S.cot.at[:, 0]
    ch, seq = lax.axis_index("ch"), lax.axis_index("seq")
    y, core = lax.div(ch, 2), lax.rem(ch, 2)
    z, x = lax.div(seq, n.x_n), lax.rem(seq, n.x_n)
    me_dev = ch * n.seqs + seq
    other_ch = ch + 1 - 2 * core

    def chip(yy, zz, xx):
        return yy * n.seqs + zz * n.x_n + xx

    def slot(yy, zz, xx):
        return (zz * n.x_n + xx) * n.y_n + yy

    def at(yy, zz, xx):
        return (yy * 2 + core, zz * n.x_n + xx)

    me_chip, me_slot = chip(y, z, x), slot(y, z, x)
    sib = (other_ch, seq)

    def z_peer(j):
        peer = z
        bit = 1
        while bit <= j:
            if j & bit:
                peer = peer + bit * (1 - 2 * lax.rem(lax.div(z, bit), 2))
            bit *= 2
        return peer

    ends = []

    def send(src, dst, send_sem, recv_sem, target):
        pltpu.make_async_remote_copy(
            src_ref=src, dst_ref=dst, send_sem=send_sem, recv_sem=recv_sem,
            device_id=target, device_id_type=MESH,
        ).start()

    def wait(ref, sem):
        pltpu.make_async_copy(ref, ref, sem).wait()

    def later(ref, sem):
        ends.append((ref, sem))

    exchange_count = [0]

    def exchange(src, dst, target, free=False):
        k = exchange_count[0]
        exchange_count[0] += 1
        send(src, dst, S.ex_s.at[k], S.ex_r.at[k], target)
        if free:
            return lambda: wait(dst, S.ex_r.at[k]), lambda: wait(src, S.ex_s.at[k])
        later(src, S.ex_s.at[k])
        return lambda: wait(dst, S.ex_r.at[k])

    def to_others(src, dst, total):
        k = exchange_count[0]
        exchange_count[0] += 1
        for dc in range(n.chans):
            for ds in range(n.seqs):
                if dc or ds:
                    cc, ss = lax.rem(ch + dc, n.chans), lax.rem(seq + ds, n.seqs)
                    send(src(cc * n.seqs + ss), dst, S.ex_s.at[k], S.ex_r.at[k], (cc, ss))
        later(total, S.ex_s.at[k])
        return lambda: wait(total, S.ex_r.at[k])

    def to_chips(src, dst, total):
        k = exchange_count[0]
        exchange_count[0] += 1
        for dy in range(n.y_n):
            for dz in range(n.z_n):
                for dx in range(n.x_n):
                    if dy or dz or dx:
                        yy, zz, xx = lax.rem(y + dy, n.y_n), lax.rem(z + dz, n.z_n), lax.rem(x + dx, n.x_n)
                        send(src(yy, zz, xx), dst, S.ex_s.at[k], S.ex_r.at[k], at(yy, zz, xx))
        later(total, S.ex_s.at[k])
        return lambda: wait(total, S.ex_r.at[k])

    barrier = pltpu.get_barrier_semaphore()
    for dc in range(n.chans):
        for ds in range(n.seqs):
            if dc or ds:
                pl.semaphore_signal(
                    barrier, inc=1,
                    device_id=(lax.rem(ch + dc, n.chans), lax.rem(seq + ds, n.seqs)),
                    device_id_type=MESH,
                )
    theirs = pl.ds(pl.multiple_of((1 - core) * n.own, 8), n.own)
    ours = pl.ds(pl.multiple_of(core * n.own, 8), n.own)
    rows_mix, rows_exp = S.i_mix[...].astype(f32), S.i_exp[...].astype(f32)
    span, wide_span = n.cw // 2, n.hw // 2
    for k in range(2):
        to = slice(k * n.own, (k + 1) * n.own)
        for g in range(3):
            for yy in range(2):
                lo, src = g * n.cw + yy * span, g * n.width + (2 * yy + k) * span
                S.wpre[to, lo : lo + span] = rows_mix[:, src : src + span]
        for yy in range(2):
            lo, src = n.mw + yy * wide_span, (2 * yy + k) * wide_span
            S.wpre[to, lo : lo + wide_span] = rows_exp[:, src : src + wide_span]
    S.pvf[...] = jnp.zeros_like(S.pvf)
    for i, name in enumerate(VECTORS):
        if name:
            ref = getattr(S, name)
            size = ref.shape[0]
            S.pvf[i : i + 1, :size] = ref[...].astype(f32).reshape(1, size)
    S.pvf[7:10, : n.tap] = S.i_sw[...].astype(f32)
    S.pvec[...] = S.pvf[...].astype(bf16)
    S.w_shr[me_chip] = S.wshr[...]
    out_rows = S.i_out[...].astype(f32)
    S.w_out[me_chip] = jnp.concatenate([out_rows[:, : n.cw], out_rows[:, n.cw :]], axis=0).astype(bf16)

    def chosen(row, width):
        return S.tabs[row : row + 1, :width]

    def pick(row0, row1, width):
        return jnp.where(core == 0, chosen(row0, width), chosen(row1, width))

    def one_hot(height, index):
        return lax.broadcasted_iota(jnp.int32, (height, index.shape[1]), 0) == index

    S.r24[...] = one_hot(LANES, chosen(0, n.width)).astype(f32).astype(bf16)
    S.d24[...] = one_hot(n.devices, chosen(1, n.width)).astype(f32)
    S.r72[...] = one_hot(LANES, pick(2, 4, n.mw)).astype(f32).astype(bf16)
    S.d72[...] = one_hot(n.devices, pick(3, 5, n.mw)).astype(f32)

    pl.semaphore_wait(barrier, n.devices - 1)


    wait_pre, sent_pre = exchange(S.wpre.at[theirs], S.wrecv, sib, free=True)
    wait_xs = exchange(S.tok_, S.xs, sib)
    after = lax.rem(seq + 1, n.seqs)
    wait_ho = exchange(S.tok_.at[:, blk - 16 : blk, :], S.ho, (ch, after))
    wait_hs = exchange(S.tok_.at[:, blk - 16 : blk, :], S.hs, (other_ch, after))
    wait_params = to_others(
        lambda d: S.pvec, S.pall.at[me_dev], S.pall.at[pl.ds(0, n.devices - 1)]
    )
    wait_gs = exchange(S.cot_, S.gs, sib)
    S.pall[me_dev] = S.pvec[...]

    def flip(axis):
        return (1 - y, z, x) if axis == "y" else (y, z, 1 - x)

    far = (1 - y, z, 1 - x)

    class Line:
        def __init__(self, p, h):
            weight, start, *widths = n.gathers[p]
            self.buf = getattr(S, f"w_{weight}")
            self.cols = pl.ds(start + h * widths[0], widths[h])
            self.base = list(n.gathers).index(p) * 2 + h
            first, second = ("x", "y") if h == 0 else ("y", "x")
            self.first_dev, self.second_dev = at(*flip(first)), at(*flip(second))
            self.lead, self.side = flip(first), flip(second)

        def part(self, index):
            return self.buf.at[index, :, self.cols]

        def recv(self, k):
            return S.ag_r.at[self.base * n.chips + k]

        def push(self, index, k, target):
            send(self.part(index), self.part(index), S.ag_s.at[self.base], self.recv(k), target)

        def start_z(self):
            for j in range(1, n.z_n):
                self.push(me_chip, j, at(y, z_peer(j), x))

        def start_xy(self):
            self.push(me_chip, n.z_n, self.first_dev)
            self.push(me_chip, 2 * n.z_n, self.second_dev)

        def along(self, j):
            index = chip(y, z_peer(j), x)
            wait(self.part(index), self.recv(j))
            self.push(index, n.z_n + j, self.first_dev)
            self.push(index, 2 * n.z_n + j, self.second_dev)

        def across(self, j):
            index = chip(self.lead[0], z_peer(j), self.lead[2])
            wait(self.part(index), self.recv(n.z_n + j))
            self.push(index, 3 * n.z_n + j, self.second_dev)

        def finish(self):
            for j in range(n.z_n):
                wait(self.part(chip(self.side[0], z_peer(j), self.side[2])), self.recv(2 * n.z_n + j))
            for j in range(n.z_n):
                wait(self.part(chip(far[0], z_peer(j), far[2])), self.recv(3 * n.z_n + j))

        def sent(self):
            wait(self.buf.at[pl.ds(0, n.chips - 1), :, self.cols], S.ag_s.at[self.base])

    class Plane:
        def __init__(self, p):
            weight, start, width = n.gathers[p]
            self.buf = getattr(S, f"w_{weight}")
            self.cols = pl.ds(start, width)
            self.base = list(n.gathers).index(p) * 2
            self.x_dev, self.y_dev = at(*flip("x")), at(*flip("y"))
            self.x_chip, self.y_chip, self.far_chip = chip(*flip("x")), chip(*flip("y")), chip(*far)

        def part(self, index):
            return self.buf.at[index, :, self.cols]

        def recv(self, k):
            return S.ag_r.at[self.base * n.chips + k]

        def push(self, index, k, target):
            send(self.part(index), self.part(index), S.ag_s.at[self.base], self.recv(k), target)

        def start_xy(self):
            self.push(me_chip, 0, self.x_dev)
            self.push(me_chip, 1, self.y_dev)

        def corner(self):
            wait(self.part(self.x_chip), self.recv(0))
            self.push(self.x_chip, 2, self.y_dev)
            wait(self.part(self.y_chip), self.recv(1))

        def start_z(self):
            for j in range(1, n.z_n):
                self.push(me_chip, 3 + j, at(y, z_peer(j), x))
                self.push(self.x_chip, 2 + n.z_n + j, at(y, z_peer(j), x))
                self.push(self.y_chip, 1 + 2 * n.z_n + j, at(y, z_peer(j), x))

        def corner_z(self):
            wait(self.part(self.far_chip), self.recv(2))
            for j in range(1, n.z_n):
                self.push(self.far_chip, 3 * n.z_n + j, at(y, z_peer(j), x))

        def finish(self):
            for q, (yy, xx) in enumerate(((y, x), (y, 1 - x), (1 - y, x), (1 - y, 1 - x))):
                for j in range(1, n.z_n):
                    wait(self.part(chip(yy, z_peer(j), xx)), self.recv(3 - q + q * n.z_n + j))

        def sent(self):
            wait(self.part(pl.ds(0, n.chips - 1)), S.ag_s.at[self.base])

    gathers = {p: [Plane(p)] if p == "t" else [Line(p, 0), Line(p, 1)] for p in n.gathers}

    def gather(p, step, *args):
        for g in gathers[p]:
            getattr(g, step)(*args)

    gather("t", "start_xy")

    wait_pre()
    own_half, sib_half = S.wpre[ours, :], S.wrecv[...]
    slab = jnp.concatenate(
        [jnp.where(core == 0, own_half, sib_half), jnp.where(core == 0, sib_half, own_half)], axis=0
    ).astype(bf16)
    S.w_mix[me_chip] = slab[:, : n.mw]
    gather("m", "start_z")
    gather("m", "start_xy")
    S.w_exp[me_chip] = slab[:, n.mw :]

    todo = []

    def plan(p, step, *args):
        todo.extend(functools.partial(getattr(g, step), *args) for g in gathers[p])

    for p, then in (("m", "go"), ("go", "e"), ("e", "s"), ("s", "")):
        for j in range(1, n.z_n):
            for q in p:
                plan(q, "along", j)
        for q in then:
            plan(q, "start_z")
        if p == "m":
            plan("t", "corner")
        if p == "e":
            plan("t", "start_z")
            plan("t", "corner_z")
        for j in range(n.z_n):
            for q in p:
                plan(q, "across", j)
        for q in then:
            plan(q, "start_xy")
        if p == "m":
            mixer_steps = len(todo)
    plan_length = len(todo)

    def pump(count):
        for _ in range(min(count, len(todo))):
            todo.pop(0)()

    pump(2)
    S.perm[...] = one_hot(n.width, chosen(8, n.width)).astype(f32).astype(bf16)
    pump(2)
    wait_params()
    S.pallf[...] = S.pall[...].astype(f32).reshape(n.devices * 16, LANES)
    groups = [(range(0, 6), S.r24, S.d24), (range(6, 11), S.r72, S.d72), (range(11, 12), S.r96, S.d96)]

    def vectors_from_shards(members, right, mask):
        width = right.shape[1]
        for i in members:
            left = S.pallf[pl.ds(i, n.devices, stride=16), :].astype(bf16)
            S.pv[i : i + 1, :width] = jnp.sum(dot_nn(left, right[...]) * mask[...], axis=0, keepdims=True)

    vectors_from_shards(*groups[0])
    pump(2)

    def vector(i, lo=0, size=None):
        return S.pv[i : i + 1, lo : lo + (n.width if size is None else size)]

    hi = lax.Precision.HIGHEST

    def filter_setup():
        for i, ref in enumerate((S.i_be, S.i_fs, S.i_bi, S.i_ss)):
            S.fvr[i : i + 1, 0:64] = ref[...].reshape(1, 64)
        S.fvec[...] = jnp.transpose(S.fvr[...])
        last = [ref[...].reshape(1, n.width) for ref in (S.i_rate, S.i_skip)]
        last = jnp.concatenate(last + [jnp.zeros((6, n.width), f32)], axis=0)
        table = jnp.concatenate([S.i_filt[...], last], axis=0)
        first = lax.broadcasted_iota(jnp.int32, (n.own, n.width), 0) + me_dev * n.own
        mine = lax.broadcasted_iota(jnp.int32, (n.own, n.width), 1) == first
        S.fsel[:, : 72] = dot_nt(jnp.where(mine, 1.0, 0.0), table, hi)

    def filter_first():
        u = dot_tn(S.embw[...], S.enc[0 : S.embw.shape[0]], hi) + S.fvec[0:64, 0:1]
        S.u1[...] = u
        s, c = sin_cos(u * S.fvec[0:64, 1:2])
        S.l1[...] = s
        S.c1[...] = c

    def filter_second():
        u = dot_tn(S.inw[...], S.l1[...], hi) + S.fvec[0:64, 2:3]
        S.u2[...] = u
        s, c = sin_cos(u * S.fvec[0:64, 3:4])
        S.l2[0:64] = s
        row = lax.broadcasted_iota(jnp.int32, (LANES - 64, n.length), 0)
        col = lax.broadcasted_iota(jnp.int32, (LANES - 64, n.length), 1)
        S.l2[64:LANES] = jnp.where((row == 0) & (col == 0), 1.0, 0.0)
        S.c2[...] = c

    def decay():
        time = lax.broadcasted_iota(jnp.int32, (n.own, n.length), 1).astype(f32)
        return jnp.exp(-S.fsel[:, 64:65] * time)

    def filter_third():
        S.imp[...] = dot_nn(S.fsel[:, 0:64], S.l2[0:64], hi) * decay()

    def toeplitz(r):
        line = S.imp[pl.ds(r, 1), :]
        line = jnp.concatenate([jnp.zeros((1, LANES), f32), line], axis=1)
        wide = jnp.broadcast_to(line, (blk, LANES + n.length))
        S.toep[r] = pltpu.roll(wide, 0, 1, stride=1, stride_axis=0)[:, LANES:].astype(bf16)

    def norm_rows(values, gain, shift):
        unit, _ = normalise(values.astype(f32))
        low = (unit * vector(gain) + vector(shift)).astype(bf16)
        return dot_nn(low, S.perm[...]).astype(bf16)

    S.n1p[0:half] = norm_rows(S.tok_[...].reshape(half, n.width), 0, 1)
    pump(2)
    wait_xs()
    S.n1p[half:rows] = norm_rows(S.xs[...].reshape(half, n.width), 0, 1)
    pump(2)
    wait_ho()
    wait_hs()
    S.n1p[rows : rows + 32] = norm_rows(S.ho[...].reshape(32, n.width), 0, 1)
    S.n1p[rows + 32 : rows + 64] = norm_rows(S.hs[...].reshape(32, n.width), 0, 1)
    pump(4)

    pump(mixer_steps - (plan_length - len(todo)))
    vectors_from_shards(*groups[1])
    gather("m", "finish")
    pump(4)

    def project(g):
        lo = g * n.cw
        weight = S.w_mix[:, :, lo : lo + n.cw].reshape(n.width, n.cw)
        for r0, r1 in ((0, half), (half, rows + 64)):
            S.mixed[r0:r1, lo : lo + n.cw] = (
                dot_nn(S.n1p[r0:r1], weight) + vector(6, lo, n.cw)
            ).astype(bf16)
    first_block = seq == 0
    last_block = seq == n.seqs - 1

    def shifted(s, lo):
        own = S.mixed[s * blk : (s + 1) * blk, lo : lo + n.cw].astype(f32)
        before = S.mixed[rows + 16 * s : rows + 16 * (s + 1), lo : lo + n.cw].astype(f32)
        before = jnp.where(first_block, jnp.zeros_like(before), before)
        both = jnp.concatenate([before, own], axis=0)
        return own, pltpu.roll(both, 1, 0)[16:], pltpu.roll(both, 2, 0)[16:]

    def short_forward(g):
        lo = g * n.cw
        for s in range(4):
            now, one, two = shifted(s, lo)
            S.so[s * blk : (s + 1) * blk, lo : lo + n.cw] = (
                vector(7, lo, n.cw) * two + vector(8, lo, n.cw) * one
                + vector(9, lo, n.cw) * now + vector(10, lo, n.cw)
            )

    for g in (1, 2):
        project(g)
        short_forward(g)

    def token_rows(s):
        return slice(s * blk, (s + 1) * blk)

    def gate(s, g):
        return S.so[token_rows(s), g * n.cw : (g + 1) * n.cw]

    def to_channels(k, make):
        out, into = getattr(S, f"sb{k}"), getattr(S, f"rb{k}")
        for s in range(4):
            turned = jnp.transpose(make(s))
            for m in range(n.chips):
                row = m * n.slab + s * n.own
                S.of[row : row + n.own, :] = turned[m * n.own : (m + 1) * n.own]
        out[...] = S.of[...].astype(bf16).reshape(n.chips, n.slab, LANES)
        arrived = to_chips(
            lambda yy, zz, xx: out.at[chip(yy, zz, xx)], into.at[me_slot], into.at[pl.ds(0, n.chips - 1)]
        )
        into[me_slot] = out[me_chip]
        return arrived

    def to_tokens(k):
        out, into = getattr(S, f"sb{k}"), getattr(S, f"rb{k}")
        out[...] = S.of[...].astype(bf16).reshape(n.chips, n.slab, LANES)
        arrived = to_chips(
            lambda yy, zz, xx: out.at[slot(yy, zz, xx)], into.at[me_chip], into.at[pl.ds(0, n.chips - 1)]
        )
        into[me_chip] = out[me_slot]
        return arrived

    def token_view(k, s):
        got = getattr(S, f"rb{k}")[...].astype(f32)
        return jnp.transpose(got[:, s * n.own : (s + 1) * n.own, :].reshape(n.cw, LANES))

    wait_u = to_channels(0, lambda s: gate(s, 1) * gate(s, 2))
    third = n.own // 3
    pump(14 + 16 + 2)
    filter_setup()
    filter_first()
    filter_second()
    filter_third()
    S.r96[...] = one_hot(LANES, chosen(6, n.hw)).astype(f32).astype(bf16)
    S.d96[...] = one_hot(n.devices, chosen(7, n.hw) + core * n.seqs).astype(f32)
    vectors_from_shards(*groups[2])
    for q in range(3):
        lax.fori_loop(q * third, (q + 1) * third, lambda r, carry: (toeplitz(r), carry)[1], 0)
    pump(10)
    wait_u()

    group = n.y_n * 4
    lines = n.seqs * group
    S.uf[...] = S.rb0[...].astype(f32).reshape(n.chips * n.slab, LANES)

    def channel_rows(ref, r):
        return ref[pl.ds(r, lines, stride=n.own), :]

    def conv_forward(r, carry):
        own = channel_rows(S.uf, r)
        wide = dot_nn(own.astype(bf16), S.toep[r])
        blocks = []
        for i in range(n.seqs):
            total = wide[group * i : group * (i + 1), 0:LANES]
            for k in range(1, i + 1):
                total = total + wide[group * (i - k) : group * (i - k + 1), LANES * k : LANES * (k + 1)]
            blocks.append(total)
        result = jnp.concatenate(blocks, axis=0) + S.fsel[pl.ds(r, 1), 65:66] * own
        S.of[pl.ds(r, lines, stride=n.own), :] = result
        return carry

    for q in range(3):
        lax.fori_loop(q * third, (q + 1) * third, conv_forward, 0)
        pump(3)
    wait_low = to_tokens(1)
    pump(100)
    gather("g", "finish")
    project(0)
    short_forward(0)
    gather("o", "finish")
    slabs = S.w_out[...].astype(f32)
    S.w2o[:, : n.cw] = slabs[:, : n.own, :].reshape(n.cw, n.cw).astype(bf16)
    S.w2o[:, n.cw :] = slabs[:, n.own :, :].reshape(n.cw, n.cw).astype(bf16)
    wait_low()

    for s in range(4):
        low = token_view(1, s)
        S.low[token_rows(s)] = low.astype(bf16)
        S.gated[token_rows(s)] = (gate(s, 0) * low).astype(bf16)
    waits = []
    for part in (1, 0):
        r = slice(part * half, (part + 1) * half)
        o = slice((1 - part) * half, (2 - part) * half)
        S.acc[r] = dot_nn(S.gated[r], S.w2o[...])
        S.peo_s[r] = S.acc[r].astype(bf16)
        waits.append(exchange(S.peo_s.at[r], S.peo_r.at[o], sib, free=True))
    wait_gs()

    def tokens_of(part):
        return (S.tok_ if part == 0 else S.xs)[...].reshape(half, n.width).astype(f32)

    def cot_of(part):
        return (S.cot_ if part == 0 else S.gs)[...].reshape(half, n.width)

    for arrived, sent in waits:
        arrived()
        sent()
    for part in range(2):
        r = slice(part * half, (part + 1) * half)
        S.middle[r] = tokens_of(part) + (S.acc[r] + S.peo_r[r].astype(f32)) + vector(2)
        S.n2p[r] = norm_rows(S.middle[r], 3, 4)

    for p in "est":
        gather(p, "finish")
    chunk = n.hw // 4
    units = chunk // n.unit
    for q in range(4):
        lo = q * chunk
        weight = S.w_exp[:, :, lo : lo + chunk].reshape(n.width, chunk)
        shrink = S.w_shr[q * units : (q + 1) * units].reshape(chunk, n.width)
        total = jnp.zeros((1, chunk), f32)
        for part in range(2):
            r = slice(part * half, (part + 1) * half)
            v = dot_nn(S.n2p[r], weight) + vector(11, lo, chunk)
            back = dot_nt(cot_of(part), shrink)
            phi = 0.5 + 0.5 * lax.erf(v * np.float32(1.0 / np.sqrt(2.0)))
            slope = phi + v * (np.float32(1.0 / np.sqrt(2.0 * np.pi)) * jnp.exp(-0.5 * v * v))
            S.hid[r, lo : lo + chunk] = (v * phi).astype(bf16)
            pre = (back * slope).astype(bf16)
            S.pre[r, lo : lo + chunk] = pre
            total = total + jnp.sum(pre.astype(f32), axis=0, keepdims=True)
        S.gv[11:12, lo : lo + chunk] = total
    waits = []
    for part in (1, 0):
        r = slice(part * half, (part + 1) * half)
        o = slice((1 - part) * half, (2 - part) * half)
        S.acc[r] = dot_nt(S.pre[r], S.w_exp[...].reshape(n.width, n.hw))
        S.peo_s[r] = S.acc[r].astype(bf16)
        waits.append(exchange(S.peo_s.at[r], S.ped_r.at[o], sib))

    def gradient(weight):
        return S.w_exp if weight == "exp" else getattr(S, f"g_{weight}")

    def add_into(ref, index, cols, *terms):
        total = ref[index, :, cols].astype(f32)
        for term in terms:
            total = total + term.astype(f32)
        ref[index, :, cols] = total.astype(bf16)

    def scatter_line(p, h):
        weight, start, *widths = n.sums[p]
        grads, cols = gradient(weight), pl.ds(start + h * widths[0], widths[h])
        from_b, from_a, from_z = (getattr(S, f"{k}_{weight}") for k in "baz")
        base = list(n.sums).index(p) * 6 + h * 3
        second, first = ("y", "x") if h == 0 else ("x", "y")
        second_dev, first_dev = at(*flip(second)), at(*flip(first))

        def side(i):
            if second == "y":
                return y * n.seqs + i
            return chip(lax.div(i, n.z_n), lax.rem(i, n.z_n), x)

        def boxed(ref):
            return ref.reshape(n.y_n, n.z_n, n.x_n, *ref.shape[1:])

        def start_b():
            if second == "y":
                src, dst = grads.at[pl.ds((1 - y) * n.seqs, n.seqs), :, cols], from_b.at[:, :, cols]
            else:
                src = boxed(grads).at[:, :, 1 - x, :, cols]
                dst = from_b.reshape(n.y_n, n.z_n, *from_b.shape[1:]).at[:, :, :, cols]
            send(src, dst, S.rs_s.at[base], S.rs_r.at[base], second_dev)
            later(from_b.at[:, :, cols], S.rs_s.at[base])

        def end_b():
            wait(from_b.at[:, :, cols], S.rs_r.at[base])

            def add(i, carry):
                add_into(grads, side(i), cols, from_b[i, :, cols])
                return carry

            lax.fori_loop(0, n.chips // 2, add, 0)
            yy, xx = (y, 1 - x) if first == "x" else (1 - y, x)
            send(boxed(grads).at[yy, :, xx, :, cols], from_a.at[:, :, cols], S.rs_s.at[base + 1], S.rs_r.at[base + 1], first_dev)
            later(from_a.at[:, :, cols], S.rs_s.at[base + 1])

        def end_a():
            wait(from_a.at[:, :, cols], S.rs_r.at[base + 1])

            def add(zz, carry):
                add_into(grads, chip(y, zz, x), cols, from_a[zz, :, cols])
                return carry

            lax.fori_loop(0, n.z_n, add, 0)
            for j in range(1, n.z_n):
                send(
                    grads.at[chip(y, z_peer(j), x), :, cols], from_z.at[j - 1, :, cols],
                    S.rs_s.at[base + 2], S.rs_r.at[base + 2], at(y, z_peer(j), x),
                )
            later(from_z.at[:, :, cols], S.rs_s.at[base + 2])

        def end_z():
            wait(from_z.at[:, :, cols], S.rs_r.at[base + 2])
            total = grads[me_chip, :, cols].astype(f32)
            for j in range(n.z_n - 1):
                total = total + from_z[j, :, cols].astype(f32)
            return total

        return start_b, end_b, end_a, end_z

    def scatter_plane(p):
        weight, start, width = n.sums[p]
        grads, full = gradient(weight), pl.ds(start, width)
        eight, four, three = (getattr(S, f"{k}_{weight}") for k in "baz")
        base = list(n.sums).index(p) * 6
        plane = ((y, x), (y, 1 - x), (1 - y, x), (1 - y, 1 - x))
        x_dev, y_dev = at(*flip("x")), at(*flip("y"))
        x_chip, y_chip, far_chip = chip(*flip("x")), chip(*flip("y")), chip(*far)

        def landing(q, j):
            k = q * (n.z_n - 1) + j - 1
            many = n.chips // 2
            return (eight, k, 0) if k < many else (four, k - many, 1)

        def start_z():
            for q, (yy, xx) in enumerate(plane):
                for j in range(1, n.z_n):
                    ref, k, which = landing(q, j)
                    send(
                        grads.at[chip(yy, z_peer(j), xx), :, full], ref.at[k, :, full],
                        S.rs_s.at[base + which], S.rs_r.at[base + which], at(y, z_peer(j), x),
                    )
            later(eight.at[:, :, full], S.rs_s.at[base])
            later(four.at[:, :, full], S.rs_s.at[base + 1])

        def end_z():
            wait(eight.at[:, :, full], S.rs_r.at[base])
            wait(four.at[:, :, full], S.rs_r.at[base + 1])
            for q, (yy, xx) in enumerate(plane):
                terms = []
                for j in range(1, n.z_n):
                    ref, k, _ = landing(q, j)
                    terms.append(ref[k, :, full])
                add_into(grads, chip(yy, z, xx), full, *terms)
            send(grads.at[far_chip, :, full], three.at[0, :, full], S.rs_s.at[base + 2], S.rs_r.at[base + 2], x_dev)
            later(three.at[0, :, full], S.rs_s.at[base + 2])

        def end_corner():
            wait(three.at[0, :, full], S.rs_r.at[base + 2])
            add_into(grads, y_chip, full, three[0, :, full])
            for k, index, target in ((1, y_chip, y_dev), (2, x_chip, x_dev)):
                send(grads.at[index, :, full], three.at[k, :, full], S.rs_s.at[base + 3 + k], S.rs_r.at[base + 3 + k], target)
                later(three.at[k, :, full], S.rs_s.at[base + 3 + k])

        def end_xy():
            total = grads[me_chip, :, full].astype(f32)
            for k in (1, 2):
                wait(three.at[k, :, full], S.rs_r.at[base + 3 + k])
                total = total + three[k, :, full].astype(f32)
            return total

        return start_z, end_z, end_corner, end_xy

    scatters = {p: [scatter_plane(p)] if p == "t" else [scatter_line(p, h) for h in range(2)] for p in n.sums}

    def scatter(p, stage):
        return [s[stage]() for s in scatters[p]]

    def steps(*place):
        for p, stage in STEPS.get(place, ()):
            scatter(p, stage)

    all_cot = jnp.concatenate([cot_of(0), cot_of(1)], axis=0)
    for q in range(4):
        lo = q * chunk
        S.g_shr[q * units : (q + 1) * units] = (
            dot_tn(S.hid[:, lo : lo + chunk], all_cot).astype(bf16).reshape(units, n.unit, n.width)
        )
    steps("shrink")
    S.gv[5:6, : n.width] = jnp.sum(cot_of(0).astype(f32), axis=0, keepdims=True)
    for w in waits:
        w()

    for part in range(2):
        r = slice(part * half, (part + 1) * half)
        grad = dot_nt((S.acc[r] + S.ped_r[r].astype(f32)).astype(bf16), S.perm[...])
        unit, scale = normalise(S.middle[r])
        if part == 0:
            S.gv[3:4, : n.width] = jnp.sum(grad * unit, axis=0, keepdims=True)
            S.gv[4:5, : n.width] = jnp.sum(grad, axis=0, keepdims=True)
        total = cot_of(part).astype(f32) + norm_back(unit, scale, grad * vector(3))
        S.acc[r] = total
        S.branch[r] = total.astype(bf16)

    for s in range(4):
        S.sg[token_rows(s), : n.cw] = dot_nt(S.branch[token_rows(s)], S.w2o[...])
    wait_g = to_channels(2, lambda s: S.sg[token_rows(s), : n.cw] * gate(s, 0))
    for s in range(4):
        S.sg[token_rows(s), : n.cw] = S.sg[token_rows(s), : n.cw] * S.low[token_rows(s)].astype(f32)

    def send_heads(lo, width):
        head_row = lax.broadcasted_iota(jnp.int32, (8, width), 0)
        heads = jnp.zeros((8, width), f32)
        for s in range(4):
            top = S.sg[s * blk : s * blk + 8, lo : lo + width]
            heads = heads + jnp.where(lax.div(head_row, 2) == s, pltpu.roll(top, 2 * s, 0) if s else top, 0.0)
        cols = pl.ds(lo, width)
        S.nb_s[:, cols] = heads
        return exchange(S.nb_s.at[:, cols], S.nb_r.at[:, cols], (ch, lax.rem(seq + n.seqs - 1, n.seqs)))

    def tap_sums(g):
        lo = g * n.cw
        sums = [jnp.zeros((1, n.cw), f32) for _ in range(4)]
        for s in range(4):
            grad = S.sg[token_rows(s), lo : lo + n.cw]
            now, one, two = shifted(s, lo)
            for i, term in enumerate((grad * two, grad * one, grad * now, grad)):
                sums[i] = sums[i] + jnp.sum(term, axis=0, keepdims=True)
        for i in range(4):
            S.gv[7 + i : 8 + i, lo : lo + n.cw] = sums[i]

    def mixed_back(g):
        lo = g * n.cw
        total = jnp.zeros((1, n.cw), f32)
        nexts = S.nb_r[:, lo : lo + n.cw]
        nexts = jnp.where(last_block, jnp.zeros_like(nexts), nexts)
        for s in range(4):
            grad = S.sg[token_rows(s), lo : lo + n.cw]
            tail = pltpu.roll(nexts, 8 - 2 * s, 0) if s else nexts
            both = jnp.concatenate([grad, tail], axis=0)
            low = (
                vector(9, lo, n.cw) * grad
                + vector(8, lo, n.cw) * pltpu.roll(both, blk + 7, 0)[:blk]
                + vector(7, lo, n.cw) * pltpu.roll(both, blk + 6, 0)[:blk]
            ).astype(bf16)
            S.mg[token_rows(s), lo : lo + n.cw] = low
            total = total + jnp.sum(low.astype(f32), axis=0, keepdims=True)
        S.gv[6:7, lo : lo + n.cw] = total
        S.g_mix[:, :, lo : lo + n.cw] = (
            dot_tn(S.n1p[0:rows], S.mg[:, lo : lo + n.cw]).astype(bf16).reshape(n.chips, n.pair, n.cw)
        )

    S.msgs[...] = jnp.zeros_like(S.msgs)

    def pack(members, right, mask):
        width = right.shape[1]
        value = jnp.concatenate([S.gv[i : i + 1, :width] * mask[...] for i in members], axis=0)
        shards = dot_two(dot_nt, value, right[...])
        for k, i in enumerate(members):
            S.msgs[pl.ds(i, n.devices, stride=16), :] = shards[k * n.devices : (k + 1) * n.devices]

    wait_nb = send_heads(0, n.cw)
    steps("heads")
    S.gv[2:3, : n.width] = jnp.sum(S.branch[0:half].astype(f32), axis=0, keepdims=True)
    gather("e", "sent")
    for q in range(4):
        lo = q * chunk
        S.w_exp[:, :, lo : lo + chunk] = (
            dot_tn(S.n2p[...], S.pre[:, lo : lo + chunk]).astype(bf16).reshape(n.chips, n.pair, chunk)
        )

    steps("expand")

    for part in (1, 0):
        r = slice(part * half, (part + 1) * half)
        value = dot_nn(S.hid[r], S.w_shr[...].reshape(n.hw, n.width))
        if part:
            S.peb_s[...] = value.astype(bf16)
            wait_bo, sent_bo = exchange(S.peb_s, S.peb_r, sib, free=True)
        else:
            S.middle[r] = S.middle[r] + value + vector(5)
    outs = dot_tn(S.gated[...], S.branch[...]).reshape(n.chips, n.own, n.width)
    S.g_out[...] = jnp.concatenate([outs[:, :, : n.cw], outs[:, :, n.cw :]], axis=1).astype(bf16)
    steps("output")
    tap_sums(0)
    wait_nb()
    mixed_back(0)
    steps("mixer", 0)
    pack((2, 3, 4, 5), S.r24, S.d24)
    pack((11,), S.r96, S.d96)
    wait_bo()
    sent_bo()
    S.bo[...] = (S.middle[0:half] + S.peb_r[...].astype(f32)).astype(bf16).reshape(2, blk, n.width)
    steps("before", "grad")
    wait_g()
    steps("after", "grad")

    flat = lax.broadcasted_iota(jnp.int32, (blk, blk), 0) + lax.broadcasted_iota(jnp.int32, (blk, blk), 1)
    mirror = jnp.where(flat == blk - 1, 1.0, 0.0).astype(bf16)
    S.gf[...] = S.rb2[...].astype(f32).reshape(n.chips * n.slab, LANES)
    S.gm[...] = dot_nn(S.rb2[...].reshape(n.chips * n.slab, LANES), mirror)
    S.uf[...] = dot_nn(S.rb0[...].reshape(n.chips * n.slab, LANES), mirror)

    def conv_back(r, carry):
        turned = channel_rows(S.gm, r)
        wide = dot_nn(turned.astype(bf16), S.toep[r])
        blocks = []
        for i in range(n.seqs):
            total = wide[group * i : group * (i + 1), 0:LANES]
            for k in range(1, n.seqs - i):
                total = total + wide[group * (i + k) : group * (i + k + 1), LANES * k : LANES * (k + 1)]
            blocks.append(total)
        back = jnp.concatenate(blocks, axis=0) + S.fsel[pl.ds(r, 1), 65:66] * turned
        S.of[pl.ds(r, lines, stride=n.own), :] = dot_nn(back.astype(bf16), mirror)
        grad = channel_rows(S.gf, r)
        steps = [grad]
        for k in range(1, n.seqs):
            steps.append(
                jnp.concatenate([grad[group * k :], jnp.zeros((group * k, LANES), f32)], axis=0)
            )
        ahead = jnp.concatenate(steps, axis=1).astype(bf16)
        outer = dot_tn(channel_rows(S.uf, r).astype(bf16), ahead)
        outer = jnp.concatenate([jnp.zeros((blk, LANES), f32), outer], axis=1)
        outer = pltpu.roll(outer, n.length + 1, 1, stride=1, stride_axis=0)
        S.ig[pl.ds(r, 1), :] = jnp.sum(outer, axis=0, keepdims=True)[:, LANES:]
        return carry

    for q in range(3):
        lax.fori_loop(q * third, (q + 1) * third, conv_back, 0)
        if q == 2:
            wait_in = to_tokens(3)
        steps("conv_back", q)

    d_line = S.ig[...] * decay()
    fg_rows = pl.ds(pl.multiple_of(me_dev * n.own, 8), n.own)
    S.fg[fg_rows, :] = dot_two(dot_nt, d_line, S.l2[...])
    wait_fg = to_chips(lambda yy, zz, xx: S.fg.at[fg_rows], S.fg.at[fg_rows], S.fg.at[pl.ds(0, (n.chips - 1) * n.own)])
    steps("filter")
    top, low = split_two(d_line)
    wide_filter = S.fsel[:, 0:64].astype(bf16)
    d_l2 = (dot_tn(wide_filter, top) + dot_tn(wide_filter, low)) * S.c2[...]
    d_u2 = d_l2 * S.fvec[0:64, 3:4]
    top, low = split_two(d_u2)
    inner = S.inw[...].astype(bf16)
    d_l1 = (dot_nn(inner, top) + dot_nn(inner, low)) * S.c1[...]
    d_u1 = d_l1 * S.fvec[0:64, 1:2]
    l1, enc = S.l1[...].astype(bf16), S.enc[...].astype(bf16)
    net = jnp.concatenate([dot_nt(top, l1) + dot_nt(low, l1), dot_two(dot_nt, d_u1, enc)], axis=1)
    net_lane = lax.broadcasted_iota(jnp.int32, (64, LANES), 1)
    for i, term in enumerate((d_u1, d_l1 * S.u1[...], d_u2, d_l2 * S.u2[...])):
        net = jnp.where(net_lane == LANES - 8 + i, jnp.sum(term, axis=1, keepdims=True), net)
    S.msgf[...] = jnp.zeros_like(S.msgf)
    S.msgf[pl.ds(0, n.devices, stride=8), :] = net[0 : n.devices]
    S.msgf[pl.ds(1, n.devices, stride=8), :] = net[n.devices :]

    def eight(d):
        return pl.ds(pl.multiple_of(d * 8, 8), 8)

    wait_msgf = to_others(
        lambda d: S.msgf.at[eight(d)], S.rallf.at[eight(me_dev)], S.rallf.at[pl.ds(0, (n.devices - 1) * 8)]
    )
    S.rallf[eight(me_dev), :] = S.msgf[eight(me_dev), :]
    steps("before", "input")
    wait_in()

    for s in range(4):
        grad = token_view(3, s)
        S.sg[token_rows(s), n.cw : 2 * n.cw] = grad * gate(s, 2)
        S.sg[token_rows(s), 2 * n.cw :] = grad * gate(s, 1)
    wait_nb = send_heads(n.cw, 2 * n.cw)
    wait_msgf()
    S.smf[...] = jnp.sum(S.rallf[...].reshape(n.devices, 8, LANES), axis=0)
    wait_net = to_others(lambda d: S.smf, S.fall.at[eight(me_dev)], S.fall.at[pl.ds(0, (n.devices - 1) * 8)])
    S.fall[eight(me_dev), :] = S.smf[...]
    wait_fg()
    sib_waits = []
    for yy in range(n.y_n):
        span = pl.ds(pl.multiple_of((yy * 2 + core) * n.seqs * n.own, 8), n.seqs * n.own)
        sib_span = pl.ds(pl.multiple_of((yy * 2 + 1 - core) * n.seqs * n.own, 8), n.seqs * n.own)
        k = exchange_count[0]
        exchange_count[0] += 1
        send(S.fg.at[span], S.fg.at[span], S.ex_s.at[k], S.ex_r.at[k], sib)
        later(S.fg.at[span], S.ex_s.at[k])
        sib_waits.append((sib_span, k))
    steps("next", "heads")
    tap_sums(1)
    tap_sums(2)
    wait_nb()
    mixed_back(1)
    steps("mixer", 1)
    mixed_back(2)
    steps("mixer", 2)
    weight = S.w_mix[...].reshape(n.width, n.mw)
    S.peb_s[...] = dot_nt(S.mg[half:rows], weight).astype(bf16)
    wait_f = exchange(S.peb_s, S.pef_r, sib)
    pack(range(6, 11), S.r72, S.d72)
    mine = dot_nt(S.mg[0:half], weight)
    steps("first", "norm")
    wait_f()
    grad = dot_nt((mine + S.pef_r[...].astype(f32)).astype(bf16), S.perm[...])
    unit, scale = normalise(tokens_of(0))
    S.gv[0:1, : n.width] = jnp.sum(grad * unit, axis=0, keepdims=True)
    S.gv[1:2, : n.width] = jnp.sum(grad, axis=0, keepdims=True)
    S.tg[...] = (S.acc[0:half] + norm_back(unit, scale, grad * vector(0))).astype(bf16).reshape(2, blk, n.width)

    steps("tokens")

    pack((0, 1), S.r24, S.d24)

    def message(d):
        return pl.ds(pl.multiple_of(d * 16, 16), 16)

    wait_msgs = to_others(
        lambda d: S.msgs.at[message(d)], S.rall.at[message(me_dev)], S.rall.at[pl.ds(0, (n.devices - 1) * 16)]
    )
    S.rall[message(me_dev), :] = S.msgs[message(me_dev), :]
    steps("vectors")

    wait_msgs()
    S.gsm[...] = jnp.sum(S.rall[...].reshape(n.devices, 16, LANES), axis=0)
    sent_pre()

    def finish(p, ref, at_col):
        lo = at_col
        for value in scatter(p, 3):
            ref[:, lo : lo + value.shape[1]] = value
            lo += value.shape[1]

    finish("s", S.gshr, 0)
    finish("t", S.gshr, n.sums["t"][1])
    both = jnp.concatenate(scatter("o", 3), axis=1)
    S.gout[:, : n.cw], S.gout[:, n.cw :] = both[: n.own], both[n.own :]
    finish("e", S.wpre, n.mw)
    finish("m0", S.wpre, 0)
    for span, k in sib_waits:
        wait(S.fg.at[span], S.ex_r.at[k])
    finish("m1", S.wpre, n.cw)
    finish("m2", S.wpre, 2 * n.cw)
    wait_fin = exchange(S.wpre.at[theirs], S.wrecv, sib)
    S.gmix[core] = S.wpre[ours, : n.mw]
    S.gexp[core] = S.wpre[ours, n.mw :]
    wait_net()
    S.gnet[0 : n.devices] = S.fall[pl.ds(0, n.devices, stride=8), :]
    S.gnet[n.devices :] = S.fall[pl.ds(1, n.devices, stride=8), :]
    wait_fin()
    S.gmix[1 - core] = S.wrecv[:, : n.mw]
    S.gexp[1 - core] = S.wrecv[:, n.mw :]
    for p in "mgost":
        gather(p, "sent")
    for ref, sem in ends:
        wait(ref, sem)


def emit_kernel(n, emb, bo, tg, gmix, gexp, gout, gshr, gsm, fg, gnet, *outs):
    (o_bo, o_tg, o_g1, o_s1, o_mix, o_mixb, o_sw, o_sb, o_embw, o_be, o_fs, o_inw, o_bi, o_ss, o_fw, o_lb, o_out,
     o_outb, o_g2, o_s2, o_exp, o_expb, o_shr, o_shrb) = outs
    o_bo[:, 0], o_tg[:, 0] = bo[...], tg[...]
    span, wide_span = n.cw // 2, n.hw // 2
    for k in range(2):
        for yy in range(2):
            for g in range(3):
                lo, dst = g * n.cw + yy * span, g * n.width + (2 * yy + k) * span
                o_mix[:, dst : dst + span] = gmix[k, :, lo : lo + span]
            lo, dst = yy * wide_span, (2 * yy + k) * wide_span
            o_exp[:, dst : dst + wide_span] = gexp[k, :, lo : lo + wide_span]
    o_out[...], o_shr[...] = gout[...], gshr[...]
    for i, ref in ((0, o_g1), (1, o_s1), (2, o_outb), (3, o_g2), (4, o_s2), (5, o_shrb), (6, o_mixb), (10, o_sb), (11, o_expb)):
        size = ref.shape[0]
        ref[...] = gsm[i : i + 1, :size].reshape(size)
    o_sw[...] = gsm[7:10, : n.tap]
    net = jnp.transpose(gnet[...])
    o_inw[...] = net[0:64]
    o_embw[...] = net[64 : 64 + emb]
    for i, ref in enumerate((o_be, o_fs, o_bi, o_ss)):
        ref[...] = net[LANES - 8 + i : LANES - 7 + i].reshape(64)
    filt = jnp.transpose(fg[...])
    o_fw[...] = filt[0:64]
    o_lb[...] = filt[64:65].reshape(n.width)


def fused(n, *args):
    emb = args[8].shape[0]
    tables_in = (jnp.asarray(tables(n)), jnp.asarray(encoding_table(n.length, (emb - 1) // 2, 64)))
    shape = jax.ShapeDtypeStruct
    outs = (
        shape((2, n.block, n.width), bf16), shape((2, n.block, n.width), bf16),
        shape((2, n.own, n.mw), f32), shape((2, n.own, n.hw), f32), shape((n.own, n.width), f32),
        shape((n.unit, n.width), f32), shape((16, LANES), f32), shape((n.width, LANES), f32),
        shape((64, LANES), f32),
    )
    scratch = scratch_list(n)
    names = INPUTS + OUTPUTS + tuple(name for name, _ in scratch)
    vmem = pl.BlockSpec(memory_space=pltpu.VMEM)
    results = pl.pallas_call(
        functools.partial(fused_kernel, n, names),
        out_shape=outs,
        in_specs=[vmem] * len(INPUTS),
        out_specs=[vmem] * len(outs),
        scratch_shapes=[s for _, s in scratch],
        compiler_params=pltpu.CompilerParams(
            collective_id=0, has_side_effects=True, vmem_limit_bytes=63 << 20
        ),
    )(*args, *tables_in)
    like = args[:1] * 2 + args[2:15] + args[16:]
    final = tuple(shape(a.shape, f32 if i > 1 else bf16) for i, a in enumerate(like))
    return pl.pallas_call(
        functools.partial(emit_kernel, n, emb),
        out_shape=final,
        in_specs=[vmem] * len(outs),
        out_specs=[vmem] * len(final),
        compiler_params=pltpu.CompilerParams(vmem_limit_bytes=63 << 20),
    )(*results)


highest = lax.Precision.HIGHEST


def from_behind(block, axis, distance):
    devices = range(lax.axis_size(axis))
    route = [(i - distance, i) for i in devices if i - distance in devices]
    return lax.ppermute(block, axis, route)


def matmul(left, right):
    return jnp.dot(left, right, precision=highest, preferred_element_type=jnp.float32)


def layer_norm(values, gain, shift):
    centre = values - jnp.mean(values, axis=-1, keepdims=True)
    spread = jnp.mean(centre * centre, axis=-1, keepdims=True)
    return centre * lax.rsqrt(spread + 1e-05) * gain + shift


def exact_gelu(values):
    return jax.nn.gelu(values, approximate=False)


def filter_values(
    seq_length,
    embed_matrix,
    embed_offset,
    sine_first,
    inner_matrix,
    inner_offset,
    sine_second,
    head_matrix,
    rates,
):
    positions = jnp.arange(seq_length).astype(jnp.float32)
    band_count = (embed_matrix.shape[0] - 1) // 2
    frequency = jnp.linspace(0.0001, band_count - 1, band_count).astype(jnp.float32)
    angles = 2.0 * jnp.pi / seq_length * positions[:, None] * frequency[None, :]
    encoded = jnp.concatenate(
        [positions[:, None] / (seq_length - 1), jnp.cos(angles), -jnp.sin(angles)], axis=1
    )
    layer_first = jnp.sin(sine_first * (matmul(encoded, embed_matrix) + embed_offset))
    layer_second = jnp.sin(sine_second * (matmul(layer_first, inner_matrix) + inner_offset))
    return matmul(layer_second, head_matrix) * jnp.exp(-rates[None, :] * positions[:, None])


def spectral_tables(block_rows):
    period = 2 * block_rows
    freq_rows = jnp.arange(block_rows + 1)
    sample_cols = jnp.arange(period)
    phase = (freq_rows[:, None] * sample_cols[None, :] % period).astype(jnp.float32) * (
        2.0 * jnp.pi / period
    )
    forward_full = jnp.concatenate([jnp.cos(phase), -jnp.sin(phase)], axis=0)
    out_times = jnp.arange(block_rows) + block_rows
    out_phase = (out_times[:, None] * freq_rows[None, :] % period).astype(jnp.float32) * (
        2.0 * jnp.pi / period
    )
    edge = (freq_rows == 0) | (freq_rows == block_rows)
    factor = jnp.where(edge, 1.0, 2.0).astype(jnp.float32) / period
    inverse_table = jnp.concatenate(
        [factor[None, :] * jnp.cos(out_phase), -factor[None, :] * jnp.sin(out_phase)], axis=1
    )
    return (forward_full, inverse_table)


def spec_product(filt, spectrum):
    return jnp.stack(
        [
            filt[0] * spectrum[0] - filt[1] * spectrum[1],
            filt[0] * spectrum[1] + filt[1] * spectrum[0],
        ]
    )


def spec_adjoint(filt, grad_spec):
    return jnp.stack(
        [
            filt[0] * grad_spec[0] + filt[1] * grad_spec[1],
            filt[0] * grad_spec[1] - filt[1] * grad_spec[0],
        ]
    )


def contract_rows(left, right):
    return lax.dot_general(
        left, right, (((0,), (0,)), ((), ())), preferred_element_type=jnp.float32
    )


def contract_cols(left, right):
    return lax.dot_general(
        left, right, (((1,), (1,)), ((), ())), preferred_element_type=jnp.float32
    )


def on_device(
    tokens,
    cotangent,
    first_gain,
    first_shift,
    mixer_weight,
    mixer_bias,
    short_weight,
    short_bias,
    embed_weight,
    embed_bias,
    first_sine,
    inner_weight,
    inner_bias,
    second_sine,
    filter_weight,
    decay_rate,
    long_bias,
    output_weight,
    output_bias,
    second_gain,
    second_shift,
    expand_weight,
    expand_bias,
    shrink_weight,
    shrink_bias,
):
    chan_count = lax.axis_size("ch")
    seq_count = lax.axis_size("seq")
    chan_index = lax.axis_index("ch")
    seq_index = lax.axis_index("seq")
    block_rows = tokens.shape[2]
    width = tokens.shape[3]
    span_width = width // chan_count
    seq_length = block_rows * seq_count
    freq_count = block_rows + 1
    gathered = (
        lax.all_gather(first_gain, ("ch", "seq"), axis=0, tiled=True),
        lax.all_gather(first_shift, ("ch", "seq"), axis=0, tiled=True),
        lax.all_gather(mixer_weight, ("ch", "seq"), axis=0, tiled=True),
        lax.all_gather(mixer_bias, ("ch", "seq"), axis=0, tiled=True),
        lax.all_gather(short_weight, ("ch", "seq"), axis=1, tiled=True),
        lax.all_gather(short_bias, ("ch", "seq"), axis=0, tiled=True),
        lax.all_gather(output_weight, ("ch", "seq"), axis=0, tiled=True),
        lax.all_gather(output_bias, ("ch", "seq"), axis=0, tiled=True),
        lax.all_gather(second_gain, ("ch", "seq"), axis=0, tiled=True),
        lax.all_gather(second_shift, ("ch", "seq"), axis=0, tiled=True),
        lax.all_gather(expand_weight, ("ch", "seq"), axis=0, tiled=True),
        lax.all_gather(expand_bias, ("ch", "seq"), axis=0, tiled=True),
        lax.all_gather(shrink_weight, ("ch", "seq"), axis=0, tiled=True),
        lax.all_gather(shrink_bias, ("ch", "seq"), axis=0, tiled=True),
    )
    (
        gain_one,
        shift_one,
        mix_matrix,
        mix_offset,
        short_taps,
        short_offset,
        out_matrix,
        out_offset,
        gain_two,
        shift_two,
        expand_matrix,
        expand_offset,
        shrink_matrix,
        shrink_offset,
    ) = gathered
    gain_one_f = gain_one.astype(jnp.float32)
    shift_one_f = shift_one.astype(jnp.float32)
    mix_offset_f = mix_offset.astype(jnp.float32)
    taps_f = short_taps.astype(jnp.float32)
    short_offset_f = short_offset.astype(jnp.float32)
    out_offset_f = out_offset.astype(jnp.float32)
    gain_two_f = gain_two.astype(jnp.float32)
    shift_two_f = shift_two.astype(jnp.float32)
    expand_offset_f = expand_offset.astype(jnp.float32)
    shrink_offset_f = shrink_offset.astype(jnp.float32)

    def local_filter(params):
        (
            embed_matrix,
            embed_offset,
            sine_a,
            inner_matrix,
            inner_offset,
            sine_b,
            head_matrix,
            skip_gain,
        ) = params
        head_slice = lax.dynamic_slice_in_dim(head_matrix, chan_index * span_width, span_width, 1)
        rate_slice = lax.dynamic_slice_in_dim(decay_rate, chan_index * span_width, span_width, 0)
        skip_slice = lax.dynamic_slice_in_dim(skip_gain, chan_index * span_width, span_width, 0)
        impulse_part = filter_values(
            seq_length,
            embed_matrix,
            embed_offset,
            sine_a,
            inner_matrix,
            inner_offset,
            sine_b,
            head_slice,
            rate_slice,
        )
        return (impulse_part, skip_slice)

    filter_params = (
        embed_weight,
        embed_bias,
        first_sine,
        inner_weight,
        inner_bias,
        second_sine,
        filter_weight,
        long_bias,
    )
    (impulse, skip_part), filter_back = jax.vjp(local_filter, filter_params)
    skip_tiled = jnp.tile(skip_part, chan_count)
    forward_full, inverse_table = spectral_tables(block_rows)
    forward_half = forward_full[:, :block_rows]
    inverse_adjoint = inverse_table.T
    impulse_blocks = impulse.reshape(seq_count, block_rows, span_width)
    earlier = jnp.concatenate([jnp.zeros_like(impulse_blocks[:1]), impulse_blocks[:-1]], axis=0)
    segments = jnp.concatenate([earlier, impulse_blocks], axis=1)
    filt_spec = jnp.einsum("fm,nmc->nfc", forward_full, segments, precision=highest)
    filt_spec = filt_spec.reshape(seq_count, 2, freq_count, 1, span_width)
    zero_spec = jnp.zeros((2 * freq_count, width), jnp.float32)

    def contribution(spectrum, source):
        distance = seq_index - source
        causal = (distance >= 0).astype(jnp.float32)
        slot_index = jnp.clip(distance, 0, seq_count - 1)
        filt = lax.dynamic_index_in_dim(filt_spec, slot_index, 0, keepdims=False)
        shaped = spectrum.reshape(2, freq_count, chan_count, span_width)
        return causal * spec_product(filt, shaped).reshape(2 * freq_count, width)

    def micro_step(carry, inputs):
        grads, filt_grad, skip_grad = carry
        block_in, block_cot = inputs
        resid = block_in.astype(jnp.float32)
        normed_one, norm_back_one = jax.vjp(layer_norm, resid, gain_one_f, shift_one_f)
        normed_low = normed_one.astype(jnp.bfloat16)
        mixed = (
            jnp.dot(normed_low, mix_matrix, preferred_element_type=jnp.float32) + mix_offset_f
        ).astype(jnp.bfloat16)
        before = from_behind(mixed[block_rows - 2 :], "seq", 1)
        padded = jnp.concatenate([before, mixed], axis=0).astype(jnp.float32)
        short_out = (
            taps_f[0] * padded[:-2]
            + taps_f[1] * padded[1:-1]
            + taps_f[2] * padded[2:]
            + short_offset_f
        )
        gate_out = short_out[:, :width]
        gate_in = short_out[:, width : 2 * width]
        values = short_out[:, 2 * width :]
        product = (gate_in * values).astype(jnp.bfloat16)
        channel_view = lax.all_to_all(
            product.reshape(block_rows, chan_count, span_width),
            "ch",
            split_axis=1,
            concat_axis=1,
            tiled=True,
        ).reshape(block_rows, width)
        own_float = channel_view.astype(jnp.float32)
        own_spec = matmul(forward_half, own_float)
        shard_piece = lax.all_gather(channel_view[None], "seq", axis=0, tiled=True)

        def add_single(offset, partial_value):
            spectrum = matmul(forward_half, shard_piece[offset].astype(jnp.float32))
            return partial_value + contribution(spectrum, offset)

        summed = lax.fori_loop(0, shard_piece.shape[0], add_single, zero_spec)
        long_out = matmul(inverse_table, summed) + skip_tiled * own_float
        long_low = long_out.astype(jnp.bfloat16)
        token_view = lax.all_to_all(
            long_low.reshape(block_rows, chan_count, span_width),
            "ch",
            split_axis=1,
            concat_axis=1,
            tiled=True,
        ).reshape(block_rows, width)
        token_float = token_view.astype(jnp.float32)
        gated_out = (gate_out * token_float).astype(jnp.bfloat16)
        middle = (
            resid
            + jnp.dot(gated_out, out_matrix, preferred_element_type=jnp.float32)
            + out_offset_f
        )
        normed_two, norm_back_two = jax.vjp(layer_norm, middle, gain_two_f, shift_two_f)
        normed_two_low = normed_two.astype(jnp.bfloat16)
        hidden_pre = (
            jnp.dot(normed_two_low, expand_matrix, preferred_element_type=jnp.float32)
            + expand_offset_f
        )
        hidden_act, gelu_back = jax.vjp(exact_gelu, hidden_pre)
        hidden_low = hidden_act.astype(jnp.bfloat16)
        result = (
            middle
            + jnp.dot(hidden_low, shrink_matrix, preferred_element_type=jnp.float32)
            + shrink_offset_f
        )
        block_result = result.astype(jnp.bfloat16)
        grad_out = block_cot.astype(jnp.float32)
        shrink_grad = contract_rows(hidden_low, block_cot)
        shrink_off_grad = jnp.sum(grad_out, axis=0)
        hidden_grad = contract_cols(block_cot, shrink_matrix)
        pre_grad = gelu_back(hidden_grad)[0].astype(jnp.bfloat16)
        expand_grad = contract_rows(normed_two_low, pre_grad)
        expand_off_grad = jnp.sum(pre_grad.astype(jnp.float32), axis=0)
        normed_two_grad = contract_cols(pre_grad, expand_matrix)
        middle_ln_grad, gain_two_grad, shift_two_grad = norm_back_two(normed_two_grad)
        middle_grad = grad_out + middle_ln_grad
        branch_low = middle_grad.astype(jnp.bfloat16)
        out_grad = contract_rows(gated_out, branch_low)
        out_off_grad = jnp.sum(branch_low.astype(jnp.float32), axis=0)
        gated_grad = contract_cols(branch_low, out_matrix)
        gate_out_grad = gated_grad * token_float
        token_grad = (gated_grad * gate_out).astype(jnp.bfloat16)
        channel_grad = lax.all_to_all(
            token_grad.reshape(block_rows, chan_count, span_width),
            "ch",
            split_axis=1,
            concat_axis=1,
            tiled=True,
        ).reshape(block_rows, width)
        channel_grad_f = channel_grad.astype(jnp.float32)
        own_shaped = own_spec.reshape(2, freq_count, chan_count, span_width)

        def back_term(running, grad_spec, target):
            spec_acc, filt_acc = running
            distance = target - seq_index
            causal = (distance >= 0).astype(jnp.float32)
            slot_index = jnp.clip(distance, 0, seq_count - 1)
            filt = lax.dynamic_index_in_dim(filt_spec, slot_index, 0, keepdims=False)
            shaped = grad_spec.reshape(2, freq_count, chan_count, span_width)
            spec_acc = spec_acc + causal * spec_adjoint(filt, shaped).reshape(2 * freq_count, width)
            filt_term = causal * jnp.sum(spec_adjoint(own_shaped, shaped), axis=2, keepdims=True)
            current = lax.dynamic_index_in_dim(filt_acc, slot_index, 0, keepdims=True)
            filt_acc = lax.dynamic_update_index_in_dim(
                filt_acc, current + filt_term[None], slot_index, 0
            )
            return (spec_acc, filt_acc)

        back_shard_piece = lax.all_gather(channel_grad[None], "seq", axis=0, tiled=True)

        def back_single(offset, partial_value):
            grad_spec = matmul(inverse_adjoint, back_shard_piece[offset].astype(jnp.float32))
            return back_term(partial_value, grad_spec, offset)

        spec_grad, filt_grad = lax.fori_loop(
            0, back_shard_piece.shape[0], back_single, (zero_spec, filt_grad)
        )
        input_grad = (
            lax.dot_general(
                forward_half,
                spec_grad,
                (((0,), (0,)), ((), ())),
                precision=highest,
                preferred_element_type=jnp.float32,
            )
            + skip_tiled * channel_grad_f
        )
        skip_grad = skip_grad + jnp.sum(
            (channel_grad_f * own_float).reshape(block_rows, chan_count, span_width), axis=(0, 1)
        )
        input_low = input_grad.astype(jnp.bfloat16)
        token_input = (
            lax.all_to_all(
                input_low.reshape(block_rows, chan_count, span_width),
                "ch",
                split_axis=1,
                concat_axis=1,
                tiled=True,
            )
            .reshape(block_rows, width)
            .astype(jnp.float32)
        )
        short_grad = jnp.concatenate(
            [gate_out_grad, token_input * values, token_input * gate_in], axis=1
        )
        short_off_grad = jnp.sum(short_grad, axis=0)
        taps_grad = jnp.stack(
            [
                jnp.sum(short_grad * padded[:-2], axis=0),
                jnp.sum(short_grad * padded[1:-1], axis=0),
                jnp.sum(short_grad * padded[2:], axis=0),
            ]
        )
        padded_grad = (
            jnp.pad(taps_f[0] * short_grad, ((0, 2), (0, 0)))
            + jnp.pad(taps_f[1] * short_grad, ((1, 1), (0, 0)))
            + jnp.pad(taps_f[2] * short_grad, ((2, 0), (0, 0)))
        )
        after = from_behind(padded_grad[:2], "seq", -1)
        mixed_grad = padded_grad[2:] + jnp.concatenate(
            [jnp.zeros((block_rows - 2, 3 * width), jnp.float32), after], axis=0
        )
        mixed_low = mixed_grad.astype(jnp.bfloat16)
        mix_grad = contract_rows(normed_low, mixed_low)
        mix_off_grad = jnp.sum(mixed_low.astype(jnp.float32), axis=0)
        normed_one_grad = contract_cols(mixed_low, mix_matrix)
        resid_ln_grad, gain_one_grad, shift_one_grad = norm_back_one(normed_one_grad)
        tokens_grad = (middle_grad + resid_ln_grad).astype(jnp.bfloat16)
        step_grads = (
            gain_one_grad,
            shift_one_grad,
            mix_grad,
            mix_off_grad,
            taps_grad,
            short_off_grad,
            out_grad,
            out_off_grad,
            gain_two_grad,
            shift_two_grad,
            expand_grad,
            expand_off_grad,
            shrink_grad,
            shrink_off_grad,
        )
        grads = jax.tree.map(lambda left, right: left + right, grads, step_grads)
        return ((grads, filt_grad, skip_grad), (block_result, tokens_grad))

    zero_grads = tuple((jnp.zeros(item.shape, jnp.float32) for item in gathered))
    init = (zero_grads, jnp.zeros_like(filt_spec), jnp.zeros((span_width,), jnp.float32))
    (grads, filt_grad, skip_grad), (results, token_grads) = lax.scan(
        micro_step, init, (tokens[:, 0], cotangent[:, 0])
    )
    shards = (
        lax.psum_scatter(grads[0], ("ch", "seq"), scatter_dimension=0, tiled=True),
        lax.psum_scatter(grads[1], ("ch", "seq"), scatter_dimension=0, tiled=True),
        lax.psum_scatter(grads[2], ("ch", "seq"), scatter_dimension=0, tiled=True),
        lax.psum_scatter(grads[3], ("ch", "seq"), scatter_dimension=0, tiled=True),
        lax.psum_scatter(grads[4], ("ch", "seq"), scatter_dimension=1, tiled=True),
        lax.psum_scatter(grads[5], ("ch", "seq"), scatter_dimension=0, tiled=True),
        lax.psum_scatter(grads[6], ("ch", "seq"), scatter_dimension=0, tiled=True),
        lax.psum_scatter(grads[7], ("ch", "seq"), scatter_dimension=0, tiled=True),
        lax.psum_scatter(grads[8], ("ch", "seq"), scatter_dimension=0, tiled=True),
        lax.psum_scatter(grads[9], ("ch", "seq"), scatter_dimension=0, tiled=True),
        lax.psum_scatter(grads[10], ("ch", "seq"), scatter_dimension=0, tiled=True),
        lax.psum_scatter(grads[11], ("ch", "seq"), scatter_dimension=0, tiled=True),
        lax.psum_scatter(grads[12], ("ch", "seq"), scatter_dimension=0, tiled=True),
        lax.psum_scatter(grads[13], ("ch", "seq"), scatter_dimension=0, tiled=True),
    )
    segment_grad = jnp.einsum(
        "fm,nfc->nmc",
        forward_full,
        filt_grad.reshape(seq_count, 2 * freq_count, span_width),
        precision=highest,
    )
    impulse_grad = segment_grad[:, block_rows:] + jnp.concatenate(
        [segment_grad[1:, :block_rows], jnp.zeros((1, block_rows, span_width), jnp.float32)], axis=0
    )
    local_grads = filter_back((impulse_grad.reshape(seq_length, span_width), skip_grad))[0]
    summed_filter = lax.psum(local_grads, ("ch", "seq"))
    return (
        results[:, None],
        token_grads[:, None],
        shards[0],
        shards[1],
        shards[2],
        shards[3],
        shards[4],
        shards[5],
        summed_filter[0],
        summed_filter[1],
        summed_filter[2],
        summed_filter[3],
        summed_filter[4],
        summed_filter[5],
        summed_filter[6],
        summed_filter[7],
        shards[6],
        shards[7],
        shards[8],
        shards[9],
        shards[10],
        shards[11],
        shards[12],
        shards[13],
    )


def block(*args):
    tokens, expand_weight = args[0], args[21]
    n = Sizes(
        lax.axis_size("ch"), lax.axis_size("seq"), tokens.shape[2], tokens.shape[3], expand_weight.shape[1]
    )
    if n.own % 8 == 0 and n.pair % 16 == 0 and n.unit % 16 == 0 and n.block == LANES:
        return fused(n, *args)
    return on_device(*args)


def solution(mesh):
    return jax.shard_map(
        block,
        mesh=mesh,
        in_specs=(
            P(None, "ch", "seq", None),
            P(None, "ch", "seq", None),
            P(("ch", "seq")),
            P(("ch", "seq")),
            P(("ch", "seq"), None),
            P(("ch", "seq")),
            P(None, ("ch", "seq")),
            P(("ch", "seq")),
            P(),
            P(),
            P(),
            P(),
            P(),
            P(),
            P(),
            P(),
            P(),
            P(("ch", "seq"), None),
            P(("ch", "seq")),
            P(("ch", "seq")),
            P(("ch", "seq")),
            P(("ch", "seq"), None),
            P(("ch", "seq")),
            P(("ch", "seq"), None),
            P(("ch", "seq")),
        ),
        out_specs=(
            P(None, "ch", "seq", None),
            P(None, "ch", "seq", None),
            P(("ch", "seq")),
            P(("ch", "seq")),
            P(("ch", "seq"), None),
            P(("ch", "seq")),
            P(None, ("ch", "seq")),
            P(("ch", "seq")),
            P(),
            P(),
            P(),
            P(),
            P(),
            P(),
            P(),
            P(),
            P(("ch", "seq"), None),
            P(("ch", "seq")),
            P(("ch", "seq")),
            P(("ch", "seq")),
            P(("ch", "seq"), None),
            P(("ch", "seq")),
            P(("ch", "seq"), None),
            P(("ch", "seq")),
        ),
        check_vma=False,
    )
```
